32 devices in a mesh: group: 4 (over z), within: 8 (over y, x, core).
Axes of the slice: x: 2, y: 2, z: 4, core: 2. Of those that a mesh axis runs over, the one named last changes fastest.
Arguments:
- vectors: bfloat16 [16384, 768], P(('group', 'within')), may hold values from -6 to 6
- centroids: float32 [2048, 768], P(('group', 'within')), may hold values from -6 to 6
- list_ids: int32 [16384], P(('group', 'within')), may hold values from 0 to 2047, as said below
- codes: int32 [16384, 96], P(('group', 'within')), may hold values from 0 to 255, as said below
- rotation: float32 [768, 768], replicated, may hold values from -0.21875 to 0.21875
Outputs:
- rotated_out: bfloat16 [16384, 768], P(('group', 'within'))
- codebooks: float32 [96, 2048], P('within')
The draws below stay inside these ranges and needn't reach their ends.
Inputs may be any that keep to these rules, and one draw needn't show every extreme that they name: `list_ids`: the rows of the d-th block of 512 rows name only lists d * 64 to (d + 1) * 64 - 1, each of them at least once. `codes`: in subspace m, the rows of the d-th block of 512 rows name codeword 256/2 + (d + m) mod (128) in 2 to 5 consecutive rows (counted round the block) and codewords below 128 elsewhere.
All inputs are finite; a program needn't handle non-finite values.
Results may differ from the reference program's by a relative error of at most 0.012.
Values may be sent and summed in bfloat16 or wider, within the bound.
No kernel may reach another device: no remote copies, remote signals or barrier semaphores. Data moves between devices by JAX's collectives and lax.ppermute only.
A program may use at most 64 MiB of HBM per device.

```python
import jax
import jax.numpy as jnp
from jax import lax

D = 768
M = 96
K = 256
DSUB = 8
ROWS_DEV = 512
LISTS_DEV = 64
ALTS = 2
NS_STEPS = 2
ROWS = 16384
LISTS = 2048


def draw_list_ids(key, part):
    blocks = ROWS // ROWS_DEV
    key_perm, key_rand = jax.random.split(key)
    perm_keys = jax.random.split(key_perm, blocks)
    heads = jax.vmap(lambda single: jax.random.permutation(single, LISTS_DEV))(perm_keys).astype(jnp.int32)
    chosen = jax.random.randint(key_rand, (blocks, ROWS_DEV), 0, LISTS_DEV, dtype=jnp.int32)
    chosen = chosen.at[:, :LISTS_DEV].set(heads)
    global_ids = chosen + jnp.arange(blocks, dtype=jnp.int32)[:, None] * LISTS_DEV
    return global_ids.reshape(ROWS).astype(jnp.int32)


def draw_codes(key, part):
    blocks = ROWS // ROWS_DEV
    half = K // 2
    keys = jax.random.split(key, 5)
    first = jax.random.randint(keys[0], (ROWS, M), 0, half, dtype=jnp.int32)
    second = jax.random.randint(keys[1], (ROWS, M), 0, half, dtype=jnp.int32)
    order = jax.random.permutation(keys[2], half).astype(jnp.int32)
    common = jnp.take(order, jnp.minimum(first, second)).reshape(blocks, ROWS_DEV, M)
    block_index = jnp.arange(blocks, dtype=jnp.int32)[:, None]
    subspace = jnp.arange(M, dtype=jnp.int32)[None, :]
    owned = half + (block_index + subspace) % half
    many = jax.random.randint(keys[3], (blocks, M), 2, 6, dtype=jnp.int32)
    start = jax.random.randint(keys[4], (blocks, M), 0, ROWS_DEV, dtype=jnp.int32)
    row_index = jnp.arange(ROWS_DEV, dtype=jnp.int32)[None, :, None]
    position = (row_index - start[:, None, :]) % ROWS_DEV
    chosen = jnp.where(position < many[:, None, :], owned[:, None, :], common)
    return chosen.reshape(ROWS, M).astype(jnp.int32)


def level_of(rng, dims, shards, smallest, top_value):
    def one(axis_at, shards_of):
        steps = jax.random.uniform(jax.random.fold_in(jax.random.fold_in(rng, 6), axis_at), (shards_of,), jnp.float32, smallest / len(shards), top_value / len(shards))
        return jnp.repeat(jnp.exp(steps), dims[axis_at] // shards_of).reshape((-1,) + (1,) * (len(dims) - axis_at - 1))

    factor_of = one(*shards[0])
    for cut in shards[1:]:
        factor_of = factor_of * one(*cut)
    return factor_of


def scatter_about(rng, shape, spread, most, cuts=(), kind=jnp.bfloat16):
    array = jax.random.normal(rng, shape, jnp.float32) * spread
    if len(cuts) > 0:
        array = level_of(rng, shape, cuts, -0.22, 0.18) * array
    return jnp.clip(array, min=-most, max=most).astype(kind)


def setup_inputs(seed: int = 0) -> dict:
    splits = jax.random.split(jax.random.key(seed), 6)
    return {
        "vectors": scatter_about(splits[0], (ROWS, D), 1.0, 6.0, ((0, 32),)),
        "centroids": scatter_about(splits[1], (LISTS, D), 1.0, 6.0, ((0, 32),), jnp.float32),
        "list_ids": draw_list_ids(jax.random.fold_in(splits[5], 71), 0),
        "codes": draw_codes(jax.random.fold_in(splits[5], 71), 0),
        "rotation": scatter_about(splits[4], (D, D), D ** -0.5, 0.21875, (), jnp.float32),
    }


exact_mode = lax.Precision.HIGHEST
epsilon = 1e-06

def polar_factor(cross):
    gram_matrix = jnp.einsum('ik,jk->ij', cross, cross, precision=exact_mode)
    norm_square = jnp.sqrt(jnp.sum(gram_matrix * gram_matrix) + epsilon)
    norm_scale = jnp.sqrt(norm_square)
    current = cross / norm_scale
    gram_matrix = gram_matrix / norm_square
    for iteration in range(NS_STEPS):
        if iteration > 0:
            gram_matrix = jnp.einsum('ik,jk->ij', current, current, precision=exact_mode)
        current = 1.5 * current - 0.5 * jnp.dot(gram_matrix, current, precision=exact_mode)
    return current

def reference(vectors, centroids, list_ids, codes, rotation):
    residual = (vectors.astype(jnp.float32) - jnp.take(centroids, list_ids, axis=0)).astype(jnp.bfloat16)
    segment_ids = (codes + jnp.arange(M, dtype=jnp.int32)[None, :] * K).reshape(-1)
    counts = jax.ops.segment_sum(jnp.ones((ROWS * M,), jnp.float32), segment_ids, num_segments=M * K).reshape(M, K)
    current = rotation
    codebook = jnp.zeros((M, K, DSUB), jnp.float32)
    for alternation in range(ALTS):
        rotated = jnp.dot(residual, current.astype(jnp.bfloat16), preferred_element_type=jnp.float32).astype(jnp.bfloat16)
        values = rotated.astype(jnp.float32).reshape(ROWS * M, DSUB)
        sums = jax.ops.segment_sum(values, segment_ids, num_segments=M * K).reshape(M, K, DSUB)
        codebook = sums / (counts[:, :, None] + 1.0)
        book_table = codebook.astype(jnp.bfloat16).reshape(M * K, DSUB)
        recon = jnp.take(book_table, segment_ids, axis=0).reshape(ROWS, D)
        cross = jnp.dot(residual.T, recon, preferred_element_type=jnp.float32) / ROWS
        current = polar_factor(cross)
    rotated_out = jnp.dot(residual, current.astype(jnp.bfloat16), preferred_element_type=jnp.float32).astype(jnp.bfloat16)
    return (rotated_out, codebook.reshape(M, K * DSUB))
```

```python
import functools

import jax
import jax.numpy as jnp
from jax import lax
from jax.experimental import pallas as pl
from jax.experimental.pallas import tpu as pltpu
from jax.sharding import PartitionSpec as P

K = 256
ALTS = 2
LO = 8
HI = K // LO
SUB = 8
PACK = 128 // HI
EPSILON = 1e-06
VMEM_BYTES = 56 * 1024 * 1024

F32 = jnp.float32
BF16 = jnp.bfloat16
NT = (((1,), (1,)), ((), ()))
NN = (((1,), (0,)), ((), ()))
TN = (((0,), (0,)), ((), ()))


def mm(a, b, dims=NN):
    return lax.dot_general(a, b, dims, preferred_element_type=F32)


def vmem_spec():
    return pl.BlockSpec(memory_space=pltpu.VMEM)


def any_spec():
    return pl.BlockSpec(memory_space=pl.ANY)


def params():
    return pltpu.CompilerParams(vmem_limit_bytes=VMEM_BYTES)


def swap(x, axis, size, bits):
    return lax.ppermute(x, axis, [(i, i ^ bits) for i in range(size)])


def residual_kernel(vectors_ref, centroids_ref, ids_ref, codes_ref, out_ref, codes_out_ref):
    lists = centroids_ref.shape[0]
    rows = vectors_ref.shape[0]
    local = lax.rem(ids_ref[...], lists)
    level = lax.broadcasted_iota(jnp.int32, (lists, rows), 0)
    table = jnp.where(level == local, 1.0, 0.0).astype(BF16)
    center = centroids_ref[...]
    first = center.astype(BF16)
    rest = center - first.astype(F32)
    second = rest.astype(BF16)
    third = (rest - second.astype(F32)).astype(BF16)
    picked = mm(table, first, TN) + mm(table, second, TN) + mm(table, third, TN)
    out_ref[...] = (vectors_ref[...].astype(F32) - picked).astype(BF16)
    codes_out_ref[...] = codes_ref[...].astype(F32).T.astype(BF16)


def residual_call(vectors, centroids, ids, codes):
    rows, width = vectors.shape
    return pl.pallas_call(
        residual_kernel,
        out_shape=(
            jax.ShapeDtypeStruct((rows, width), BF16),
            jax.ShapeDtypeStruct((codes.shape[1], rows), BF16),
        ),
        in_specs=[vmem_spec()] * 4,
        out_specs=(vmem_spec(), vmem_spec()),
        compiler_params=params(),
        name="residual",
    )(vectors, centroids, ids.reshape(1, rows), codes)


def split_codes(codes):
    whole = codes.astype(F32).astype(jnp.int32)
    return whole >> 3, whole & 7


def packs_of(owned):
    return [range(first, min(first + PACK, owned)) for first in range(0, owned, PACK)]


def hi_table(hi, pack):
    rows = hi.shape[1]
    level = lax.broadcasted_iota(jnp.int32, (HI, rows), 0)
    parts = [jnp.where(level == hi[m : m + 1, :], 1.0, 0.0) for m in pack]
    parts += [jnp.zeros((HI, rows), F32)] * (PACK - len(pack))
    return jnp.concatenate(parts, axis=0).astype(BF16)


def lane_owner(rows):
    return lax.broadcasted_iota(jnp.int32, (rows, 128), 1) // HI


def diagonal(wide, block):
    owner = lane_owner(block)
    total = jnp.zeros((block, 128), F32)
    for i in range(wide.shape[0] // block):
        total = jnp.where(owner == i, wide[i * block : (i + 1) * block, :], total)
    return total


def add_chunk(residual, rotation_rows, codes, totals, first, with_counts):
    owned = codes.shape[0]
    rotated = mm(rotation_rows, residual, NT).astype(BF16).astype(F32)
    hi, lo = split_codes(codes)
    rows = residual.shape[0]
    low_level = lax.broadcasted_iota(jnp.int32, (LO, rows), 0)
    for g, pack in enumerate(packs_of(owned)):
        table = hi_table(hi, pack)
        parts = []
        for m in pack:
            value = rotated[m * SUB : (m + 1) * SUB, :]
            low = jnp.broadcast_to(lo[m : m + 1, :], (SUB, rows))
            parts += [jnp.where(low == level, value, 0.0) for level in range(LO)]
        if with_counts:
            parts += [jnp.where(low_level == lo[m : m + 1, :], 1.0, 0.0) for m in pack]
        part = mm(jnp.concatenate(parts, axis=0).astype(BF16), table, NT)
        height = part.shape[0]
        if first:
            totals[g, :height, :] = part
        else:
            totals[g, :height, :] += part


def pack_sums(totals, owned, out_ref, with_counts):
    packs = packs_of(owned)
    block = LO * SUB
    counts = []
    for g, pack in enumerate(packs):
        size = len(pack)
        out_ref[g * block : (g + 1) * block, :] = diagonal(totals[g, : size * block, :], block).astype(BF16)
        if with_counts:
            counts.append(diagonal(totals[g, size * block : size * (block + LO), :], LO))
    if with_counts:
        every = jnp.concatenate(counts, axis=0)
        above = jnp.floor(every * (1.0 / 256.0))
        below = every - above * 256.0
        base = len(packs) * block
        height = len(packs) * LO
        pad = out_ref.shape[0] - base - 2 * height
        pieces = [above, below] + ([jnp.zeros((pad, 128), F32)] if pad else [])
        out_ref[base:, :] = jnp.concatenate(pieces, axis=0).astype(BF16)


def sums_rows(owned, with_counts):
    packs = len(packs_of(owned))
    rows = packs * LO * SUB
    if with_counts:
        rows += -(-2 * packs * LO // 16) * 16
    return rows


def totals_shape(owned):
    return pltpu.VMEM((len(packs_of(owned)), PACK * LO * (SUB + 1), 128), F32)


def start_copies(sources, held, sems):
    copies = [pltpu.make_async_copy(src, held.at[i], sems.at[i]) for i, src in enumerate(sources)]
    for copy in copies:
        copy.start()
    return copies


def sums_kernel(count, rotation_ref, codes_ref, *refs):
    chunks, out_ref, held, totals, sems = refs[:count], refs[count], *refs[count + 1 :]
    owned = codes_ref.shape[1]
    copies = start_copies(chunks, held, sems)
    rotation_rows = rotation_ref[...]
    for i, copy in enumerate(copies):
        copy.wait()
        add_chunk(held[i], rotation_rows, codes_ref[i], totals, i == 0, True)
    pack_sums(totals, owned, out_ref, True)


def sums_call(rotation_rows, codes, chunks):
    count, owned = codes.shape[:2]
    return pl.pallas_call(
        functools.partial(sums_kernel, count),
        out_shape=jax.ShapeDtypeStruct((sums_rows(owned, True), 128), BF16),
        in_specs=[vmem_spec()] * 2 + [any_spec()] * count,
        out_specs=vmem_spec(),
        scratch_shapes=[
            pltpu.VMEM((count,) + chunks[0].shape, BF16),
            totals_shape(owned),
            pltpu.SemaphoreType.DMA((count,)),
        ],
        compiler_params=params(),
        name="sums",
    )(rotation_rows, codes, *chunks)


def tree(values):
    while len(values) > 1:
        values = [values[i] + values[i + 1] for i in range(0, len(values), 2)]
    return values[0]


def cross_kernel(count, groups, with_counts, total_rows, codes_ref, *refs):
    sums = refs[:groups]
    refs = refs[groups:]
    owned = codes_ref.shape[1]
    packs = packs_of(owned)
    block = LO * SUB
    base = len(packs) * block
    height = len(packs) * LO
    if with_counts:
        chunks, refs = refs[:count], refs[count:]
        cross_ref, counts_ref, held, sems = refs
    else:
        counts_in, chunks, refs = refs[0], refs[1 : count + 1], refs[count + 1 :]
        cross_ref, book_ref, held, sems = refs
    copies = start_copies(chunks, held, sems)
    everything = tree([ref[...].astype(F32) for ref in sums])
    if with_counts:
        counts = everything[base : base + height] * 256.0 + everything[base + height : base + 2 * height]
        counts_ref[...] = counts
    else:
        counts = counts_in[...]
    books = []
    for g in range(len(packs)):
        rows = []
        for level in range(LO):
            at = g * block + level * SUB
            rows.append(everything[at : at + SUB] / (counts[g * LO + level : g * LO + level + 1] + 1.0))
        book = jnp.concatenate(rows, axis=0)
        if not with_counts:
            book_ref[g * block : (g + 1) * block, :] = book
        books.append(book)
    owner = lane_owner(block)
    wide = [
        jnp.concatenate([jnp.where(owner == i, book, 0.0) for i in range(len(pack))], axis=0).astype(BF16)
        for book, pack in zip(books, packs)
    ]
    total = jnp.zeros(cross_ref.shape, F32)
    for i, copy in enumerate(copies):
        hi, lo = split_codes(codes_ref[i])
        rows = hi.shape[1]
        rebuilt = []
        for g, pack in enumerate(packs):
            spread = mm(wide[g], hi_table(hi, pack))
            for j, m in enumerate(pack):
                low = jnp.broadcast_to(lo[m : m + 1, :], (SUB, rows))
                at = j * block
                value = spread[at : at + SUB]
                for level in range(1, LO):
                    value = jnp.where(low == level, spread[at + level * SUB : at + (level + 1) * SUB], value)
                rebuilt.append(value)
        copy.wait()
        total += mm(jnp.concatenate(rebuilt, axis=0).astype(BF16), held[i])
    cross_ref[...] = (total * (1.0 / total_rows)).astype(BF16)


def cross_call(codes, sums, counts, chunks, total_rows):
    count, owned = codes.shape[:2]
    packs = len(packs_of(owned))
    width = chunks[0].shape[1]
    with_counts = counts is None
    extra = (
        jax.ShapeDtypeStruct((packs * LO, 128), F32)
        if with_counts
        else jax.ShapeDtypeStruct((packs * LO * SUB, 128), F32)
    )
    small = list(sums) + ([] if with_counts else [counts])
    return pl.pallas_call(
        functools.partial(cross_kernel, count, len(sums), with_counts, total_rows),
        out_shape=(jax.ShapeDtypeStruct((owned * SUB, width), BF16), extra),
        in_specs=[vmem_spec()] * (1 + len(small)) + [any_spec()] * count,
        out_specs=(vmem_spec(), vmem_spec()),
        scratch_shapes=[
            pltpu.VMEM((count,) + chunks[0].shape, BF16),
            pltpu.SemaphoreType.DMA((count,)),
        ],
        compiler_params=params(),
        name="cross",
    )(codes, *small, *chunks)


def gather_blocks(place_ref, blocks, whole):
    height = blocks[0].shape[0]
    for k, ref in enumerate(blocks):
        at = pl.multiple_of((place_ref[0] ^ k) * height, 8)
        whole[pl.ds(at, height), :] = ref[...].astype(F32)


def first_step(whole):
    x = whole[...]
    xb = x.astype(BF16)
    gram = mm(xb, xb, NT)
    norm_square = jnp.sqrt(jnp.sum(gram * gram, keepdims=True) + EPSILON)
    scale = lax.rsqrt(norm_square)
    step = mm((gram * (1.0 / norm_square)).astype(BF16), xb)
    return (1.5 * x - 0.5 * step) * scale


def next_sums_kernel(count, blocks, place_ref, codes_ref, *refs):
    parts, refs = refs[:blocks], refs[blocks:]
    chunks, out_ref, held, totals, whole, sems = refs[:count], refs[count], *refs[count + 1 :]
    owned = codes_ref.shape[1]
    copies = start_copies(chunks, held, sems)
    gather_blocks(place_ref, parts, whole)
    x = first_step(whole)
    whole[...] = x
    height = parts[0].shape[0]
    mine = whole[pl.ds(pl.multiple_of(place_ref[0] * height, 8), height), :]
    xb = x.astype(BF16)
    gram = mm(mine.astype(BF16), xb, NT)
    rotation_rows = (1.5 * mine - 0.5 * mm(gram.astype(BF16), xb)).astype(BF16)
    for i, copy in enumerate(copies):
        copy.wait()
        add_chunk(held[i], rotation_rows, codes_ref[i], totals, i == 0, False)
    pack_sums(totals, owned, out_ref, False)


def next_sums_call(place, codes, blocks, chunks):
    count, owned = codes.shape[:2]
    width = chunks[0].shape[1]
    return pl.pallas_call(
        functools.partial(next_sums_kernel, count, len(blocks)),
        out_shape=jax.ShapeDtypeStruct((sums_rows(owned, False), 128), BF16),
        in_specs=[pl.BlockSpec(memory_space=pltpu.SMEM)] + [vmem_spec()] * (1 + len(blocks)) + [any_spec()] * count,
        out_specs=vmem_spec(),
        scratch_shapes=[
            pltpu.VMEM((count,) + chunks[0].shape, BF16),
            totals_shape(owned),
            pltpu.VMEM((width, width), F32),
            pltpu.SemaphoreType.DMA((count,)),
        ],
        compiler_params=params(),
        name="next_sums",
    )(place, codes, *blocks, *chunks)


def final_kernel(blocks, place_ref, residual_ref, *refs):
    parts, out_ref, whole = refs[:blocks], refs[blocks], refs[blocks + 1]
    gather_blocks(place_ref, parts, whole)
    x = first_step(whole)
    xb = x.astype(BF16)
    gram = mm(xb, xb, NT)
    rotation = (1.5 * x - 0.5 * mm(gram.astype(BF16), xb)).astype(BF16)
    out_ref[...] = mm(residual_ref[...], rotation, NT).astype(BF16)


def final_call(place, residual, blocks):
    width = residual.shape[1]
    return pl.pallas_call(
        functools.partial(final_kernel, len(blocks)),
        out_shape=jax.ShapeDtypeStruct(residual.shape, BF16),
        in_specs=[pl.BlockSpec(memory_space=pltpu.SMEM)] + [vmem_spec()] * (1 + len(blocks)),
        out_specs=vmem_spec(),
        scratch_shapes=[pltpu.VMEM((width, width), F32)],
        compiler_params=params(),
        name="final",
    )(place, residual, *blocks)


def gather_rows(residual, size):
    half = residual.shape[0] // 2
    bits = [1 << b for b in range(1, size.bit_length() - 1)]
    held = [{0: residual[:half]}, {0: residual[half:]}]
    for step in range(len(bits)):
        for h in range(2):
            bit = bits[step] if h == 0 else bits[len(bits) - 1 - step]
            for k in list(held[h]):
                held[h][k ^ bit] = swap(held[h][k], "within", size, bit)
    for h in range(2):
        for k in list(held[h]):
            held[h][k ^ 1] = swap(held[h][k], "within", size, 1)
    return [held[h][k] for k in range(size) for h in range(2)]


def gather_group(x, size):
    blocks = {k: swap(x, "within", size, k) if k else x for k in range(0, size, 2)}
    for k in list(blocks):
        blocks[k ^ 1] = swap(blocks[k], "within", size, 1)
    return [blocks[k] for k in range(size)]


def everywhere(x, size):
    return [x] + [swap(x, "group", size, k) for k in range(1, size)]


def per_device(vectors, centroids, list_ids, codes, rotation):
    groups = lax.axis_size("group")
    size = lax.axis_size("within")
    rows, width = vectors.shape
    subspaces = codes.shape[1]
    owned = subspaces // size
    total_rows = rows * size * groups
    place = lax.axis_index("within").astype(jnp.int32)
    places = place.reshape(1)
    residual, codes_t = residual_call(vectors, centroids, list_ids, codes)
    chunks = gather_rows(residual, size)
    moved = lax.all_to_all(codes_t.reshape(size, owned, rows), "within", 0, 0)
    order = jnp.arange(size, dtype=jnp.int32) ^ place
    moved = jnp.take(moved, order, axis=0)
    half = rows // 2
    own_codes = moved.reshape(size, owned, 2, half).transpose(0, 2, 1, 3).reshape(2 * size, owned, half)
    rotation_rows = lax.dynamic_slice_in_dim(rotation, place * owned * SUB, owned * SUB, 1).T.astype(BF16)
    sums = sums_call(rotation_rows, own_codes, chunks)
    counts = None
    for alternation in range(ALTS):
        parts = everywhere(sums, groups)
        cross, extra = cross_call(own_codes, parts, counts, chunks, total_rows)
        block = tree([p.astype(F32) for p in everywhere(cross, groups)]).astype(BF16)
        blocks = gather_group(block, size)
        if alternation + 1 < ALTS:
            counts = extra
            sums = next_sums_call(places, own_codes, blocks, chunks)
    rotated_out = final_call(places, residual, blocks)
    packs = len(packs_of(owned))
    book = extra.reshape(packs, LO * SUB, PACK, HI).transpose(0, 2, 3, 1).reshape(packs * PACK, K * SUB)
    return (rotated_out, book[:owned])


def solution(mesh):
    in_specs = (
        P(("group", "within"), None),
        P(("group", "within"), None),
        P(("group", "within")),
        P(("group", "within"), None),
        P(),
    )
    out_specs = (P(("group", "within"), None), P("within", None))
    return jax.shard_map(per_device, mesh=mesh, in_specs=in_specs, out_specs=out_specs, check_vma=False)
```

```python
import functools
import math

import jax
import jax.numpy as jnp
from jax import lax
from jax.experimental import pallas as pl
from jax.experimental.pallas import tpu as pltpu
from jax.sharding import PartitionSpec as P

K = 256
ALTS = 2
LO = 8
HI = K // LO
SUB = 8
PACK = 128 // HI
EPSILON = 1e-06
MIB = 1024 * 1024
BAND = 256

F32 = jnp.float32
BF16 = jnp.bfloat16
NT = (((1,), (1,)), ((), ()))
NN = (((1,), (0,)), ((), ()))
TN = (((0,), (0,)), ((), ()))


def mm(a, b, dims=NN):
    return lax.dot_general(a, b, dims, preferred_element_type=F32)


def vmem_spec():
    return pl.BlockSpec(memory_space=pltpu.VMEM)


def smem_spec():
    return pl.BlockSpec(memory_space=pltpu.SMEM)


def cost(us):
    return pl.CostEstimate(flops=int(us * 1e9), bytes_accessed=0, transcendentals=0)


def params(*arrays):
    held = sum(math.prod(a.shape) * a.dtype.itemsize for a in arrays)
    return pltpu.CompilerParams(vmem_limit_bytes=held + 12 * MIB)


def swap(x, axis, size, bits):
    return lax.ppermute(x, axis, [(i, i ^ bits) for i in range(size)])


def residual_kernel(vectors_ref, centroids_ref, ids_ref, *outs):
    lists = centroids_ref.shape[0]
    rows = vectors_ref.shape[0]
    half = rows // 2
    local = lax.rem(ids_ref[...], lists)
    level = lax.broadcasted_iota(jnp.int32, (lists, rows), 0)
    table = jnp.where(level == local, 1.0, 0.0).astype(BF16)
    center = centroids_ref[...]
    first = center.astype(BF16)
    rest = center - first.astype(F32)
    second = rest.astype(BF16)
    third = (rest - second.astype(F32)).astype(BF16)
    for h, out_ref in enumerate(outs):
        part = table[:, h * half : (h + 1) * half]
        picked = mm(part, first, TN) + mm(part, second, TN) + mm(part, third, TN)
        out_ref[...] = (vectors_ref[h * half : (h + 1) * half, :].astype(F32) - picked).astype(BF16)


def residual_call(vectors, centroids, ids):
    rows, width = vectors.shape
    return pl.pallas_call(
        residual_kernel,
        out_shape=(jax.ShapeDtypeStruct((rows // 2, width), BF16),) * 2,
        in_specs=[vmem_spec()] * 3,
        out_specs=(vmem_spec(),) * 2,
        compiler_params=params(),
        name="residual",
    )(vectors, centroids, ids.reshape(1, rows))


def packs_of(owned):
    return [range(first, min(first + PACK, owned)) for first in range(0, owned, PACK)]


def hi_table(hi, pack):
    rows = hi.shape[1]
    level = lax.broadcasted_iota(jnp.int32, (HI, rows), 0)
    parts = [jnp.where(level == hi[m : m + 1, :], 1.0, 0.0) for m in pack]
    parts += [jnp.zeros((HI, rows), F32)] * (PACK - len(pack))
    return jnp.concatenate(parts, axis=0).astype(BF16)


def lane_owner(rows):
    return lax.broadcasted_iota(jnp.int32, (rows, 128), 1) // HI


def diagonal(wide, block):
    owner = lane_owner(block)
    total = jnp.zeros((block, 128), F32)
    for i in range(wide.shape[0] // block):
        total = jnp.where(owner == i, wide[i * block : (i + 1) * block, :], total)
    return total


def pack_sums(rotated, codes, pack, with_counts):
    rows = codes.shape[1]
    hi, lo = codes >> 3, codes & 7
    table = hi_table(hi, pack)
    parts = []
    for m in pack:
        value = rotated[m * SUB : (m + 1) * SUB, :]
        low = jnp.broadcast_to(lo[m : m + 1, :], (SUB, rows))
        parts += [jnp.where(low == level, value, 0.0) for level in range(LO)]
    if with_counts:
        low_level = lax.broadcasted_iota(jnp.int32, (LO, rows), 0)
        parts += [jnp.where(low_level == lo[m : m + 1, :], 1.0, 0.0) for m in pack]
    return mm(jnp.concatenate(parts, axis=0).astype(BF16), table, NT)


def pack_layout(owned, with_counts):
    packs = len(packs_of(owned))
    base, height = packs * LO * SUB, packs * LO
    return base, height, base + (-(-2 * height // 16) * 16 if with_counts else 0)


def write_sums(sums, counts, owned, out_ref):
    base, height, total = pack_layout(owned, counts is not None)
    out_ref[:base, :] = sums.astype(BF16)
    if counts is not None:
        above = jnp.floor(counts * (1.0 / 256.0))
        pieces = [above, counts - above * 256.0]
        pad = total - base - 2 * height
        pieces += [jnp.zeros((pad, 128), F32)] if pad else []
        out_ref[base:, :] = jnp.concatenate(pieces, axis=0).astype(BF16)


def pack_diagonals(totals, owned, with_counts):
    block = LO * SUB
    sums, counts = [], []
    for total, pack in zip(totals, packs_of(owned)):
        size = len(pack)
        sums.append(diagonal(total[: size * block], block))
        if with_counts:
            counts.append(diagonal(total[size * block :], LO))
    return jnp.concatenate(sums, axis=0), jnp.concatenate(counts, axis=0) if with_counts else None


def tree(values):
    while len(values) > 1:
        values = [values[i] + values[i + 1] for i in range(0, len(values), 2)]
    return values[0]


def merge_parts(parts, owned, with_counts):
    base, height, unused = pack_layout(owned, with_counts)
    whole = tree([ref[...].astype(F32) for ref in parts])
    if not with_counts:
        return whole, None
    return whole[:base], whole[base : base + height] * 256.0 + whole[base + height : base + 2 * height]


def code_rows(rows):
    return rows // 128 * 16


def write_codes(codes, out_ref, at):
    owned, rows = codes.shape
    filled = jnp.concatenate([codes, jnp.zeros((16 - owned, rows), F32)], axis=0).astype(BF16)
    for c in range(rows // 128):
        out_ref[at + 16 * c : at + 16 * c + 16, :] = filled[:, 128 * c : 128 * c + 128]


def local_sums_kernel(size, place_ref, rotation_ref, codes_ref, upper_ref, lower_ref, *refs):
    outs, turned, staged = refs[:2], refs[2], refs[3]
    subspaces = codes_ref.shape[0]
    owned = subspaces // size
    base = pack_layout(owned, True)[2]
    residual = jnp.concatenate([upper_ref[...], lower_ref[...]], axis=0)
    rotated = mm(residual, rotation_ref[...].astype(BF16)).astype(BF16).astype(F32)
    turned[...] = rotated.T
    for j in range(size):
        staged[j, :owned, :] = codes_ref[j * owned : (j + 1) * owned, :]
    for k in range(size):
        other = place_ref[0] ^ k
        codes = staged[other][:owned]
        value = turned[pl.ds(pl.multiple_of(other * (owned * SUB), 8), owned * SUB), :]
        totals = [pack_sums(value, codes, pack, True) for pack in packs_of(owned)]
        sums, counts = pack_diagonals(totals, owned, True)
        slot = outs[k % 2].at[k // 2]
        write_sums(sums, counts, owned, slot.at[:base])
        write_codes(codes.astype(F32), slot, base)


def local_sums_call(place, rotation, codes, upper, lower, size):
    subspaces, rows = codes.shape
    owned = subspaces // size
    height = -(-owned // 8) * 8
    shape = jax.ShapeDtypeStruct((size // 2, pack_layout(owned, True)[2] + code_rows(rows), 128), BF16)
    return pl.pallas_call(
        functools.partial(local_sums_kernel, size),
        out_shape=(shape,) * 2,
        in_specs=[smem_spec()] + [vmem_spec()] * 4,
        out_specs=(vmem_spec(),) * 2,
        scratch_shapes=[pltpu.VMEM((rotation.shape[1], rows), F32), pltpu.VMEM((size, height, rows), jnp.int32)],
        compiler_params=params(rotation),
        cost_estimate=cost(4),
        name="local_sums",
    )(place, rotation, codes, upper, lower)


def merge_cores_kernel(owned, even_ref, came_ref, *outs):
    base = pack_layout(owned, True)[2]
    length = even_ref.shape[1] - base
    for i, out_ref in enumerate(outs):
        sums, counts = merge_parts([even_ref.at[i], came_ref.at[i]], owned, True)
        write_sums(sums, counts, owned, out_ref.at[:base])
        out_ref[base : base + length, :] = even_ref[i, base:, :]
        out_ref[base + length :, :] = came_ref[i, base:, :]


def merge_cores_call(even, came, owned):
    slots, height, lanes = even.shape
    shape = jax.ShapeDtypeStruct((2 * height - pack_layout(owned, True)[2], lanes), BF16)
    return pl.pallas_call(
        functools.partial(merge_cores_kernel, owned),
        out_shape=(shape,) * slots,
        in_specs=[vmem_spec()] * 2,
        out_specs=(vmem_spec(),) * slots,
        compiler_params=params(),
        cost_estimate=cost(1),
        name="merge_cores",
    )(even, came)


def merge_chips_kernel(owned, *refs):
    parts, (out_ref, codes_ref) = refs[:-2], refs[-2:]
    base = pack_layout(owned, True)[2]
    sums, counts = merge_parts(parts, owned, True)
    write_sums(sums, counts, owned, out_ref)
    length = (parts[0].shape[0] - base) // 2
    for i, part in enumerate(parts):
        for core in range(2):
            for c in range(length // 16):
                at = base + core * length + 16 * c
                piece = part[at : at + 16, :].astype(F32)
                codes_ref[2 * i + core, :, 128 * c : 128 * c + 128] = piece[:owned].astype(jnp.int32)


def merge_chips_call(parts, owned, rows):
    size = 2 * len(parts)
    return pl.pallas_call(
        functools.partial(merge_chips_kernel, owned),
        out_shape=(
            jax.ShapeDtypeStruct((pack_layout(owned, True)[2], 128), BF16),
            jax.ShapeDtypeStruct((size, owned, rows), jnp.int32),
        ),
        in_specs=[vmem_spec()] * len(parts),
        out_specs=(vmem_spec(),) * 2,
        compiler_params=params(),
        cost_estimate=cost(1),
        name="merge_chips",
    )(*parts)


def spans_of(size):
    step = min(2, size)
    return [range(first, first + step) for first in range(0, size, step)]


def span_codes(codes_ref, span):
    return jnp.concatenate([codes_ref[k] for k in span], axis=1)


def span_rows(chunks, span):
    return jnp.concatenate([chunks[2 * k + h][...] for k in span for h in range(2)], axis=0)


def cross_kernel(size, groups, with_counts, total_rows, codes_ref, *refs):
    sums, refs = refs[:groups], refs[groups:]
    owned = codes_ref.shape[1]
    packs = packs_of(owned)
    block = LO * SUB
    if with_counts:
        chunks, (cross_ref, counts_ref) = refs[: 2 * size], refs[2 * size :]
    else:
        counts_in, chunks, (cross_ref, book_ref) = refs[0], refs[1 : 2 * size + 1], refs[2 * size + 1 :]
    everything, counts = merge_parts(sums, owned, with_counts)
    if with_counts:
        counts_ref[...] = counts
    else:
        counts = counts_in[...]
    books = []
    for g in range(len(packs)):
        rows = []
        for level in range(LO):
            at = g * block + level * SUB
            rows.append(everything[at : at + SUB] / (counts[g * LO + level : g * LO + level + 1] + 1.0))
        book = jnp.concatenate(rows, axis=0)
        if not with_counts:
            book_ref[g * block : (g + 1) * block, :] = book
        books.append(book)
    owner = lane_owner(block)
    wide = [
        jnp.concatenate([jnp.where(owner == i, book, 0.0) for i in range(len(pack))], axis=0).astype(BF16)
        for book, pack in zip(books, packs)
    ]
    total = None
    for span in spans_of(size):
        codes = span_codes(codes_ref, span)
        hi, lo = codes >> 3, codes & 7
        rows = codes.shape[1]
        rebuilt = []
        for g, pack in enumerate(packs):
            spread = mm(wide[g], hi_table(hi, pack))
            for j, m in enumerate(pack):
                low = jnp.broadcast_to(lo[m : m + 1, :], (SUB, rows))
                at = j * block
                value = spread[at : at + SUB]
                for level in range(1, LO):
                    value = jnp.where(low == level, spread[at + level * SUB : at + (level + 1) * SUB], value)
                rebuilt.append(value)
        part = mm(jnp.concatenate(rebuilt, axis=0).astype(BF16), span_rows(chunks, span))
        total = part if total is None else total + part
    cross_ref[...] = (total * (1.0 / total_rows)).astype(BF16)


def cross_call(codes, sums, counts, chunks, total_rows):
    size, owned, unused = codes.shape
    packs = len(packs_of(owned))
    width = chunks[0].shape[1]
    with_counts = counts is None
    extra = jax.ShapeDtypeStruct((packs * LO * (1 if with_counts else SUB), 128), F32)
    small = list(sums) + ([] if with_counts else [counts])
    return pl.pallas_call(
        functools.partial(cross_kernel, size, len(sums), with_counts, total_rows),
        out_shape=(jax.ShapeDtypeStruct((owned * SUB, width), BF16), extra),
        in_specs=[vmem_spec()] * (1 + len(small) + len(chunks)),
        out_specs=(vmem_spec(), vmem_spec()),
        compiler_params=params(*chunks),
        name="cross",
    )(codes, *small, *chunks)


def bands(x):
    return [x[i : i + BAND] for i in range(0, x.shape[0], BAND)]


def first_step(xb):
    steps = []
    square = None
    for band in bands(xb):
        gram = mm(band, xb, NT)
        part = jnp.sum(gram * gram, keepdims=True)
        square = part if square is None else square + part
        steps.append(mm(gram.astype(BF16), xb))
    norm_square = jnp.sqrt(square + EPSILON)
    scale = lax.rsqrt(norm_square)
    less = 0.5 * scale / norm_square
    return [(1.5 * scale) * band.astype(F32) - less * step for band, step in zip(bands(xb), steps)]


def join(parts):
    if parts[0].shape[0] % 16 == 0:
        return jnp.concatenate(parts, axis=0)
    return jnp.concatenate([p.astype(F32) for p in parts], axis=0).astype(BF16)


def next_sums_kernel(size, codes_ref, *refs):
    parts, chunks, out_ref = refs[:size], refs[size : 3 * size], refs[3 * size]
    owned = codes_ref.shape[1]
    height = parts[0].shape[0]
    x = first_step(join([ref[...] for ref in parts]))
    xb = jnp.concatenate([band.astype(BF16) for band in x], axis=0)
    mine = x[0][:height]
    gram = mm(mine.astype(BF16), xb, NT)
    rotation_rows = (1.5 * mine - 0.5 * mm(gram.astype(BF16), xb)).astype(BF16)
    totals = None
    for span in spans_of(size):
        rotated = mm(rotation_rows, span_rows(chunks, span), NT).astype(BF16).astype(F32)
        codes = span_codes(codes_ref, span)
        more = [pack_sums(rotated, codes, pack, False) for pack in packs_of(owned)]
        totals = more if totals is None else [a + b for a, b in zip(totals, more)]
    write_sums(pack_diagonals(totals, owned, False)[0], None, owned, out_ref)


def next_sums_call(codes, blocks, chunks):
    size, owned, unused = codes.shape
    return pl.pallas_call(
        functools.partial(next_sums_kernel, size),
        out_shape=jax.ShapeDtypeStruct((pack_layout(owned, False)[2], 128), BF16),
        in_specs=[vmem_spec()] * (1 + len(blocks) + len(chunks)),
        out_specs=vmem_spec(),
        compiler_params=params(*chunks),
        name="next_sums",
    )(codes, *blocks, *chunks)


def final_kernel(size, place_ref, upper_ref, lower_ref, *refs):
    parts, out_ref, whole = refs[:size], refs[size], refs[size + 1]
    height = parts[0].shape[0]
    for k, ref in enumerate(parts):
        at = pl.multiple_of((place_ref[0] ^ k) * height, 16 if whole.dtype == BF16 else 8)
        whole[pl.ds(at, height), :] = ref[...].astype(whole.dtype)
    x = first_step(whole[...].astype(BF16))
    xb = jnp.concatenate([band.astype(BF16) for band in x], axis=0)
    residual = jnp.concatenate([upper_ref[...], lower_ref[...]], axis=0)
    for i, band in enumerate(x):
        gram = mm(xb[i * BAND : (i + 1) * BAND], xb, NT).astype(BF16)
        rotation = (1.5 * band - 0.5 * mm(gram, xb)).astype(BF16)
        out_ref[:, i * BAND : (i + 1) * BAND] = mm(residual, rotation, NT).astype(BF16)


def final_call(place, upper, lower, blocks):
    rows, width = upper.shape
    kind = BF16 if blocks[0].shape[0] % 16 == 0 else F32
    return pl.pallas_call(
        functools.partial(final_kernel, len(blocks)),
        out_shape=jax.ShapeDtypeStruct((2 * rows, width), BF16),
        in_specs=[smem_spec()] + [vmem_spec()] * (2 + len(blocks)),
        out_specs=vmem_spec(),
        scratch_shapes=[pltpu.VMEM((width, width), kind)],
        compiler_params=params(),
        name="final",
    )(place, upper, lower, *blocks)


def gather_rows(halves, size):
    bits = [1 << b for b in range(1, size.bit_length() - 1)]
    held = [{0: half} for half in halves]
    for h in range(2):
        held[h][1] = swap(held[h][0], "within", size, 1)
    for step in range(len(bits)):
        for h in range(2):
            bit = bits[step] if h == 0 else bits[len(bits) - 1 - step]
            for k in [k for k in held[h] if k % 2 == 0]:
                held[h][k ^ bit] = swap(held[h][k], "within", size, bit)
    for h in range(2):
        for k in [k for k in held[h] if k % 2 == 0 and k]:
            held[h][k ^ 1] = swap(held[h][k], "within", size, 1)
    return [held[h][k] for k in range(size) for h in range(2)]


def gather_group(x, size):
    blocks = {k: swap(x, "within", size, k) if k else x for k in range(0, size, 2)}
    for k in list(blocks):
        blocks[k ^ 1] = swap(blocks[k], "within", size, 1)
    return [blocks[k] for k in range(size)]


def scatter_sums(even, odd, owned, rows, size):
    merged = merge_cores_call(even, swap(odd, "within", size, 1), owned)
    parts = [merged[0]] + [swap(merged[k // 2], "within", size, k) for k in range(2, size, 2)]
    return merge_chips_call(parts, owned, rows)


def everywhere(x, size):
    return [x] + [swap(x, "group", size, k) for k in range(1, size)]


def per_device(vectors, centroids, list_ids, codes, rotation):
    groups = lax.axis_size("group")
    size = lax.axis_size("within")
    rows, width = vectors.shape
    owned = codes.shape[1] // size
    total_rows = rows * size * groups
    place = lax.axis_index("within").astype(jnp.int32).reshape(1)
    upper, lower = residual_call(vectors, centroids, list_ids)
    chunks = gather_rows((upper, lower), size)
    even, odd = local_sums_call(place, rotation, codes.T, upper, lower, size)
    sums, own_codes = scatter_sums(even, odd, owned, rows, size)
    counts = None
    for alternation in range(ALTS):
        parts = everywhere(sums, groups)
        cross, extra = cross_call(own_codes, parts, counts, chunks, total_rows)
        block = tree([p.astype(F32) for p in everywhere(cross, groups)]).astype(BF16)
        blocks = gather_group(block, size)
        if alternation + 1 < ALTS:
            counts = extra
            sums = next_sums_call(own_codes, blocks, chunks)
    rotated_out = final_call(place, upper, lower, blocks)
    packs = len(packs_of(owned))
    book = extra.reshape(packs, LO * SUB, PACK, HI).transpose(0, 2, 3, 1).reshape(packs * PACK, K * SUB)
    return (rotated_out, book[:owned])


def solution(mesh):
    in_specs = (
        P(("group", "within"), None),
        P(("group", "within"), None),
        P(("group", "within")),
        P(("group", "within"), None),
        P(),
    )
    out_specs = (P(("group", "within"), None), P("within", None))
    return jax.shard_map(per_device, mesh=mesh, in_specs=in_specs, out_specs=out_specs, check_vma=False)
```

```python
import functools
import math

import jax
import jax.numpy as jnp
from jax import lax
from jax.experimental import pallas as pl
from jax.experimental.pallas import tpu as pltpu
from jax.sharding import PartitionSpec as P

K = 256
ALTS = 2
LO = 8
HI = K // LO
SUB = 8
PACK = 128 // HI
EPSILON = 1e-06
MIB = 1024 * 1024
BAND = 256

F32 = jnp.float32
BF16 = jnp.bfloat16
NT = (((1,), (1,)), ((), ()))
NN = (((1,), (0,)), ((), ()))
TN = (((0,), (0,)), ((), ()))


def mm(a, b, dims=NN):
    return lax.dot_general(a, b, dims, preferred_element_type=F32)


def vmem_spec():
    return pl.BlockSpec(memory_space=pltpu.VMEM)


def smem_spec():
    return pl.BlockSpec(memory_space=pltpu.SMEM)


def cost(us):
    return pl.CostEstimate(flops=int(us * 1e9), bytes_accessed=0, transcendentals=0)


def params(*arrays):
    held = sum(math.prod(a.shape) * a.dtype.itemsize for a in arrays)
    return pltpu.CompilerParams(vmem_limit_bytes=held + 12 * MIB)


def swap(x, axis, size, bits):
    return lax.ppermute(x, axis, [(i, i ^ bits) for i in range(size)])


def residual_kernel(vectors_ref, centroids_ref, ids_ref, out_ref):
    lists = centroids_ref.shape[0]
    rows = vectors_ref.shape[0]
    local = lax.rem(ids_ref[...], lists)
    level = lax.broadcasted_iota(jnp.int32, (lists, rows), 0)
    table = jnp.where(level == local, 1.0, 0.0).astype(BF16)
    center = centroids_ref[...]
    first = center.astype(BF16)
    rest = center - first.astype(F32)
    second = rest.astype(BF16)
    third = (rest - second.astype(F32)).astype(BF16)
    picked = mm(table, first, TN) + mm(table, second, TN) + mm(table, third, TN)
    out_ref[...] = (vectors_ref[...].astype(F32) - picked).astype(BF16)


def residual_call(vectors, centroids, ids):
    rows, width = vectors.shape
    return pl.pallas_call(
        residual_kernel,
        out_shape=jax.ShapeDtypeStruct((rows, width), BF16),
        in_specs=[vmem_spec()] * 3,
        out_specs=vmem_spec(),
        compiler_params=params(),
        name="residual",
    )(vectors, centroids, ids.reshape(1, rows))


def packs_of(owned):
    return [range(first, min(first + PACK, owned)) for first in range(0, owned, PACK)]


def hi_table(hi, pack):
    rows = hi.shape[1]
    level = lax.broadcasted_iota(jnp.int32, (HI, rows), 0)
    parts = [jnp.where(level == hi[m : m + 1, :], 1.0, 0.0) for m in pack]
    parts += [jnp.zeros((HI, rows), F32)] * (PACK - len(pack))
    return jnp.concatenate(parts, axis=0).astype(BF16)


def lane_owner(rows):
    return lax.broadcasted_iota(jnp.int32, (rows, 128), 1) // HI


def diagonal(wide, block):
    owner = lane_owner(block)
    total = jnp.zeros((block, 128), F32)
    for i in range(wide.shape[0] // block):
        total = jnp.where(owner == i, wide[i * block : (i + 1) * block, :], total)
    return total


def pack_sums(rotated, codes, pack, with_counts):
    rows = codes.shape[1]
    hi, lo = codes >> 3, codes & 7
    table = hi_table(hi, pack)
    parts = []
    for m in pack:
        value = rotated[m * SUB : (m + 1) * SUB, :]
        low = jnp.broadcast_to(lo[m : m + 1, :], (SUB, rows))
        parts += [jnp.where(low == level, value, 0.0) for level in range(LO)]
    if with_counts:
        low_level = lax.broadcasted_iota(jnp.int32, (LO, rows), 0)
        parts += [jnp.where(low_level == lo[m : m + 1, :], 1.0, 0.0) for m in pack]
    return mm(jnp.concatenate(parts, axis=0).astype(BF16), table, NT)


def pack_layout(owned, with_counts):
    packs = len(packs_of(owned))
    base, height = packs * LO * SUB, packs * LO
    return base, height, base + (-(-2 * height // 16) * 16 if with_counts else 0)


def write_sums(sums, counts, owned, out_ref):
    base, height, total = pack_layout(owned, counts is not None)
    out_ref[:base, :] = sums.astype(BF16)
    if counts is not None:
        above = jnp.floor(counts * (1.0 / 256.0))
        pieces = [above, counts - above * 256.0]
        pad = total - base - 2 * height
        pieces += [jnp.zeros((pad, 128), F32)] if pad else []
        out_ref[base:, :] = jnp.concatenate(pieces, axis=0).astype(BF16)


def pack_diagonals(totals, owned, with_counts):
    block = LO * SUB
    sums, counts = [], []
    for total, pack in zip(totals, packs_of(owned)):
        size = len(pack)
        sums.append(diagonal(total[: size * block], block))
        if with_counts:
            counts.append(diagonal(total[size * block :], LO))
    return jnp.concatenate(sums, axis=0), jnp.concatenate(counts, axis=0) if with_counts else None


def tree(values):
    while len(values) > 1:
        values = [values[i] + values[i + 1] for i in range(0, len(values), 2)]
    return values[0]


def merge_parts(parts, owned, with_counts):
    base, height, unused = pack_layout(owned, with_counts)
    whole = tree([ref[...].astype(F32) for ref in parts])
    if not with_counts:
        return whole, None
    return whole[:base], whole[base : base + height] * 256.0 + whole[base + height : base + 2 * height]


def code_rows(rows):
    return rows // 128 * 16


def write_codes(codes, out_ref, at):
    owned, rows = codes.shape
    filled = jnp.concatenate([codes, jnp.zeros((16 - owned, rows), F32)], axis=0).astype(BF16)
    for c in range(rows // 128):
        out_ref[at + 16 * c : at + 16 * c + 16, :] = filled[:, 128 * c : 128 * c + 128]


def local_sums_kernel(size, place_ref, rotation_ref, codes_ref, residual_ref, *refs):
    outs, turned, staged = refs[:2], refs[2], refs[3]
    subspaces = codes_ref.shape[0]
    owned = subspaces // size
    base = pack_layout(owned, True)[2]
    rotated = mm(residual_ref[...], rotation_ref[...].astype(BF16)).astype(BF16).astype(F32)
    turned[...] = rotated.T
    for j in range(size):
        staged[j, :owned, :] = codes_ref[j * owned : (j + 1) * owned, :]
    for k in range(size):
        other = place_ref[0] ^ k
        codes = staged[other][:owned]
        value = turned[pl.ds(pl.multiple_of(other * (owned * SUB), 8), owned * SUB), :]
        totals = [pack_sums(value, codes, pack, True) for pack in packs_of(owned)]
        sums, counts = pack_diagonals(totals, owned, True)
        slot = outs[k % 2].at[k // 2]
        write_sums(sums, counts, owned, slot.at[:base])
        write_codes(codes.astype(F32), slot, base)


def local_sums_call(place, rotation, codes, residual, size):
    subspaces, rows = codes.shape
    owned = subspaces // size
    height = -(-owned // 8) * 8
    shape = jax.ShapeDtypeStruct((size // 2, pack_layout(owned, True)[2] + code_rows(rows), 128), BF16)
    return pl.pallas_call(
        functools.partial(local_sums_kernel, size),
        out_shape=(shape,) * 2,
        in_specs=[smem_spec()] + [vmem_spec()] * 3,
        out_specs=(vmem_spec(),) * 2,
        scratch_shapes=[pltpu.VMEM((rotation.shape[1], rows), F32), pltpu.VMEM((size, height, rows), jnp.int32)],
        compiler_params=params(rotation),
        cost_estimate=cost(0),
        name="local_sums",
    )(place, rotation, codes, residual)


def merge_cores_kernel(owned, even_ref, came_ref, *outs):
    base = pack_layout(owned, True)[2]
    length = even_ref.shape[1] - base
    for i, out_ref in enumerate(outs):
        sums, counts = merge_parts([even_ref.at[i], came_ref.at[i]], owned, True)
        write_sums(sums, counts, owned, out_ref.at[:base])
        out_ref[base : base + length, :] = even_ref[i, base:, :]
        out_ref[base + length :, :] = came_ref[i, base:, :]


def merge_cores_call(even, came, owned):
    slots, height, lanes = even.shape
    shape = jax.ShapeDtypeStruct((2 * height - pack_layout(owned, True)[2], lanes), BF16)
    return pl.pallas_call(
        functools.partial(merge_cores_kernel, owned),
        out_shape=(shape,) * slots,
        in_specs=[vmem_spec()] * 2,
        out_specs=(vmem_spec(),) * slots,
        compiler_params=params(),
        cost_estimate=cost(0),
        name="merge_cores",
    )(even, came)


def merge_chips_kernel(owned, *refs):
    parts, (out_ref, codes_ref) = refs[:-2], refs[-2:]
    base = pack_layout(owned, True)[2]
    sums, counts = merge_parts(parts, owned, True)
    write_sums(sums, counts, owned, out_ref)
    length = (parts[0].shape[0] - base) // 2
    for i, part in enumerate(parts):
        for core in range(2):
            for c in range(length // 16):
                at = base + core * length + 16 * c
                piece = part[at : at + 16, :].astype(F32)
                codes_ref[2 * i + core, :, 128 * c : 128 * c + 128] = piece[:owned].astype(jnp.int32)


def merge_chips_call(parts, owned, rows):
    size = 2 * len(parts)
    return pl.pallas_call(
        functools.partial(merge_chips_kernel, owned),
        out_shape=(
            jax.ShapeDtypeStruct((pack_layout(owned, True)[2], 128), BF16),
            jax.ShapeDtypeStruct((size, owned, rows), jnp.int32),
        ),
        in_specs=[vmem_spec()] * len(parts),
        out_specs=(vmem_spec(),) * 2,
        compiler_params=params(),
        cost_estimate=cost(0),
        name="merge_chips",
    )(*parts)


def merge_kernel(owned, first_ref, second_ref, out_ref):
    sums, counts = merge_parts([first_ref, second_ref], owned, True)
    write_sums(sums, counts, owned, out_ref)


def merge_call(first, second, owned):
    return pl.pallas_call(
        functools.partial(merge_kernel, owned),
        out_shape=jax.ShapeDtypeStruct(first.shape, BF16),
        in_specs=[vmem_spec()] * 2,
        out_specs=vmem_spec(),
        compiler_params=params(),
        cost_estimate=cost(0),
        name="merge_groups",
    )(first, second)


def spans_of(held):
    return [(k, k ^ 1) for k in held if k % 2 == 0]


def span_codes(codes_ref, span):
    return jnp.concatenate([codes_ref[k] for k in span], axis=1)


def span_rows(pieces, span):
    return jnp.concatenate([ref[...] for k in span for ref in pieces[k]], axis=0)


def pieces_of(held, refs):
    at = 0
    pieces = {}
    for k, count in held.items():
        pieces[k] = refs[at : at + count]
        at += count
    return pieces


def read_books(sums, counts_in, owned):
    everything, counts = merge_parts(sums, owned, counts_in is None)
    if counts is None:
        counts = counts_in[...]
    block = LO * SUB
    books = []
    for g in range(len(packs_of(owned))):
        rows = []
        for level in range(LO):
            at = g * block + level * SUB
            rows.append(everything[at : at + SUB] / (counts[g * LO + level : g * LO + level + 1] + 1.0))
        books.append(jnp.concatenate(rows, axis=0))
    return books, counts


def widen(books, owned):
    owner = lane_owner(LO * SUB)
    return [
        jnp.concatenate([jnp.where(owner == i, book, 0.0) for i in range(len(pack))], axis=0).astype(BF16)
        for book, pack in zip(books, packs_of(owned))
    ]


def add_spans(total, wide, codes_ref, pieces, spans):
    owned = codes_ref.shape[1]
    for span in spans:
        codes = span_codes(codes_ref, span)
        hi, lo = codes >> 3, codes & 7
        rows = codes.shape[1]
        rebuilt = []
        for g, pack in enumerate(packs_of(owned)):
            spread = mm(wide[g], hi_table(hi, pack))
            for j, m in enumerate(pack):
                low = jnp.broadcast_to(lo[m : m + 1, :], (SUB, rows))
                at = j * LO * SUB
                value = spread[at : at + SUB]
                for level in range(1, LO):
                    value = jnp.where(low == level, spread[at + level * SUB : at + (level + 1) * SUB], value)
                rebuilt.append(value)
        part = mm(jnp.concatenate(rebuilt, axis=0).astype(BF16), span_rows(pieces, span))
        total = part if total is None else total + part
    return total


def flat(chunks):
    return {k: len(c) for k, c in chunks.items()}, [piece for c in chunks.values() for piece in c]


def cross_near_kernel(held, groups, codes_ref, *refs):
    sums, pieces, outs = refs[:groups], pieces_of(held, refs[groups:]), refs[groups + sum(held.values()) :]
    total_ref, wide_ref, counts_ref = outs
    owned = codes_ref.shape[1]
    books, counts = read_books(sums, None, owned)
    counts_ref[...] = counts
    wide = widen(books, owned)
    for g, one in enumerate(wide):
        wide_ref[g, : one.shape[0], :] = one
    total_ref[...] = add_spans(None, wide, codes_ref, pieces, spans_of(held))


def cross_near_call(codes, sums, chunks):
    owned = codes.shape[1]
    packs = len(packs_of(owned))
    held, rows = flat(chunks)
    return pl.pallas_call(
        functools.partial(cross_near_kernel, held, len(sums)),
        out_shape=(
            jax.ShapeDtypeStruct((owned * SUB, rows[0].shape[1]), F32),
            jax.ShapeDtypeStruct((packs, PACK * LO * SUB, 128), BF16),
            jax.ShapeDtypeStruct((packs * LO, 128), F32),
        ),
        in_specs=[vmem_spec()] * (1 + len(sums) + len(rows)),
        out_specs=(vmem_spec(),) * 3,
        compiler_params=params(*rows),
        cost_estimate=cost(0),
        name="cross_near",
    )(codes, *sums, *rows)


def cross_far_kernel(held, total_rows, codes_ref, total_ref, wide_ref, *refs):
    pieces, cross_ref = pieces_of(held, refs), refs[-1]
    packs = packs_of(codes_ref.shape[1])
    wide = [wide_ref[g, : len(pack) * LO * SUB, :] for g, pack in enumerate(packs)]
    total = add_spans(total_ref[...], wide, codes_ref, pieces, spans_of(held))
    cross_ref[...] = (total * (1.0 / total_rows)).astype(BF16)


def cross_far_call(codes, total, wide, chunks, total_rows):
    held, rows = flat(chunks)
    return pl.pallas_call(
        functools.partial(cross_far_kernel, held, total_rows),
        out_shape=jax.ShapeDtypeStruct(total.shape, BF16),
        in_specs=[vmem_spec()] * (3 + len(rows)),
        out_specs=vmem_spec(),
        compiler_params=params(*rows),
        cost_estimate=cost(0),
        name="cross_far",
    )(codes, total, wide, *rows)


def cross_kernel(held, groups, total_rows, codes_ref, *refs):
    sums, counts_in, pieces = refs[:groups], refs[groups], pieces_of(held, refs[groups + 1 :])
    cross_ref, book_ref = refs[-2:]
    owned = codes_ref.shape[1]
    block = LO * SUB
    books, unused = read_books(sums, counts_in, owned)
    for g, book in enumerate(books):
        book_ref[g * block : (g + 1) * block, :] = book
    total = add_spans(None, widen(books, owned), codes_ref, pieces, spans_of(held))
    cross_ref[...] = (total * (1.0 / total_rows)).astype(BF16)


def cross_call(codes, sums, counts, chunks, total_rows):
    owned = codes.shape[1]
    held, rows = flat(chunks)
    return pl.pallas_call(
        functools.partial(cross_kernel, held, len(sums), total_rows),
        out_shape=(
            jax.ShapeDtypeStruct((owned * SUB, rows[0].shape[1]), BF16),
            jax.ShapeDtypeStruct((len(packs_of(owned)) * LO * SUB, 128), F32),
        ),
        in_specs=[vmem_spec()] * (2 + len(sums) + len(rows)),
        out_specs=(vmem_spec(), vmem_spec()),
        compiler_params=params(*rows),
        cost_estimate=cost(0),
        name="cross",
    )(codes, *sums, counts, *rows)


def bands(x):
    return [x[i : i + BAND] for i in range(0, x.shape[0], BAND)]


def first_step(xb):
    steps = []
    square = None
    for band in bands(xb):
        gram = mm(band, xb, NT)
        part = jnp.sum(gram * gram, keepdims=True)
        square = part if square is None else square + part
        steps.append(mm(gram.astype(BF16), xb))
    norm_square = jnp.sqrt(square + EPSILON)
    scale = lax.rsqrt(norm_square)
    less = 0.5 * scale / norm_square
    return [(1.5 * scale) * band.astype(F32) - less * step for band, step in zip(bands(xb), steps)]


def join(parts):
    if parts[0].shape[0] % 16 == 0:
        return jnp.concatenate(parts, axis=0)
    return jnp.concatenate([p.astype(F32) for p in parts], axis=0).astype(BF16)


def next_sums_kernel(held, codes_ref, *refs):
    size = len(held)
    parts, pieces, out_ref = refs[:size], pieces_of(held, refs[size:]), refs[-1]
    owned = codes_ref.shape[1]
    height = parts[0].shape[0]
    x = first_step(join([ref[...] for ref in parts]))
    xb = jnp.concatenate([band.astype(BF16) for band in x], axis=0)
    mine = x[0][:height]
    gram = mm(mine.astype(BF16), xb, NT)
    rotation_rows = (1.5 * mine - 0.5 * mm(gram.astype(BF16), xb)).astype(BF16)
    totals = None
    for span in spans_of(held):
        rotated = mm(rotation_rows, span_rows(pieces, span), NT).astype(BF16).astype(F32)
        codes = span_codes(codes_ref, span)
        more = [pack_sums(rotated, codes, pack, False) for pack in packs_of(owned)]
        totals = more if totals is None else [a + b for a, b in zip(totals, more)]
    write_sums(pack_diagonals(totals, owned, False)[0], None, owned, out_ref)


def next_sums_call(codes, blocks, chunks):
    owned = codes.shape[1]
    held, rows = flat(chunks)
    return pl.pallas_call(
        functools.partial(next_sums_kernel, held),
        out_shape=jax.ShapeDtypeStruct((pack_layout(owned, False)[2], 128), BF16),
        in_specs=[vmem_spec()] * (1 + len(blocks) + len(rows)),
        out_specs=vmem_spec(),
        compiler_params=params(*rows),
        cost_estimate=cost(0),
        name="next_sums",
    )(codes, *blocks, *rows)


def final_kernel(size, place_ref, residual_ref, *refs):
    parts, out_ref, whole = refs[:size], refs[size], refs[size + 1]
    height = parts[0].shape[0]
    for k, ref in enumerate(parts):
        at = pl.multiple_of((place_ref[0] ^ k) * height, 16 if whole.dtype == BF16 else 8)
        whole[pl.ds(at, height), :] = ref[...].astype(whole.dtype)
    x = first_step(whole[...].astype(BF16))
    xb = jnp.concatenate([band.astype(BF16) for band in x], axis=0)
    residual = residual_ref[...]
    for i, band in enumerate(x):
        gram = mm(xb[i * BAND : (i + 1) * BAND], xb, NT).astype(BF16)
        rotation = (1.5 * band - 0.5 * mm(gram, xb)).astype(BF16)
        out_ref[:, i * BAND : (i + 1) * BAND] = mm(residual, rotation, NT).astype(BF16)


def final_call(place, residual, blocks):
    rows, width = residual.shape
    kind = BF16 if blocks[0].shape[0] % 16 == 0 else F32
    return pl.pallas_call(
        functools.partial(final_kernel, len(blocks)),
        out_shape=jax.ShapeDtypeStruct((rows, width), BF16),
        in_specs=[smem_spec()] + [vmem_spec()] * (1 + len(blocks)),
        out_specs=vmem_spec(),
        scratch_shapes=[pltpu.VMEM((width, width), kind)],
        compiler_params=params(),
        cost_estimate=cost(0),
        name="final",
    )(place, residual, *blocks)


def after(x, *first):
    return lax.optimization_barrier((x,) + first)[0]


def near_rows(rows, size):
    return {1 << b: swap(rows, "within", size, 1 << b) for b in range(1, size.bit_length() - 1)}


def far_rows(rows, near, size):
    bits = list(near)
    half = rows.shape[0] // 2
    halves = []
    for order, cut in ((bits, slice(0, half)), (bits[::-1], slice(half, None))):
        here = {0: rows, order[0]: near[order[0]][cut]}
        for bit in order[1:]:
            for k in list(here):
                here[k ^ bit] = swap(here[k], "within", size, bit) if k else near[bit][cut]
        halves.append(here)
    return {k: (halves[0][k], halves[1][k]) for k in halves[0] if k and k not in near}


def both_cores(whole, size):
    return {k ^ 1: tuple(swap(piece, "within", size, 1) for piece in pieces) for k, pieces in whole.items()}


def gather_group(x, size):
    blocks = {k: swap(x, "within", size, k) if k else x for k in range(0, size, 2)}
    for k in list(blocks):
        blocks[k ^ 1] = swap(blocks[k], "within", size, 1)
    return [blocks[k] for k in range(size)]


def scatter_sums(merged, owned, rows, size):
    parts = [merged[0]] + [swap(merged[k // 2], "within", size, k) for k in range(2, size, 2)]
    return merge_chips_call(parts, owned, rows)


def everywhere(x, size):
    return [x] + [swap(x, "group", size, k) for k in range(1, size)]


def reduce_cross(cross, size):
    return tree([p.astype(F32) for p in everywhere(cross, size)]).astype(BF16)


def per_device(vectors, centroids, list_ids, codes, rotation):
    groups = lax.axis_size("group")
    size = lax.axis_size("within")
    rows, width = vectors.shape
    owned = codes.shape[1] // size
    total_rows = rows * size * groups
    place = lax.axis_index("within").astype(jnp.int32).reshape(1)
    residual = residual_call(vectors, centroids, list_ids)
    near = near_rows(residual, size)
    twin = swap(residual, "within", size, 1)
    even, odd = local_sums_call(place, rotation, codes.T, after(residual, twin), size)
    merged = merge_cores_call(even, swap(odd, "within", size, 1), owned)
    sums, own_codes = scatter_sums(merged, owned, rows, size)
    far = far_rows(residual, near, size)
    near = {k: after(rows_near, sums) for k, rows_near in near.items()}
    for bit in [1 << b for b in range(groups.bit_length() - 2)]:
        sums = merge_call(sums, swap(sums, "group", groups, bit), owned)
    parts = [sums, swap(sums, "group", groups, groups // 2)]
    chunks = {0: (residual,), 1: (twin,)}
    for k, rows_near in near.items():
        chunks[k] = (rows_near,)
        chunks[k ^ 1] = (swap(rows_near, "within", size, 1),)
    total, wide, counts = cross_near_call(own_codes, parts, chunks)
    far = {k: tuple(after(piece, parts[1]) for piece in pieces) for k, pieces in far.items()}
    far = {**far, **both_cores(far, size)}
    cross = cross_far_call(own_codes, total, wide, far, total_rows)
    chunks.update(far)
    for alternation in range(1, ALTS):
        blocks = gather_group(reduce_cross(cross, groups), size)
        parts = everywhere(next_sums_call(own_codes, blocks, chunks), groups)
        cross, book = cross_call(own_codes, parts, counts, chunks, total_rows)
    blocks = gather_group(reduce_cross(cross, groups), size)
    rotated_out = final_call(place, residual, blocks)
    packs = len(packs_of(owned))
    book = book.reshape(packs, LO * SUB, PACK, HI).transpose(0, 2, 3, 1).reshape(packs * PACK, K * SUB)
    return (rotated_out, book[:owned])


def solution(mesh):
    in_specs = (
        P(("group", "within"), None),
        P(("group", "within"), None),
        P(("group", "within")),
        P(("group", "within"), None),
        P(),
    )
    out_specs = (P(("group", "within"), None), P("within", None))
    return jax.shard_map(per_device, mesh=mesh, in_specs=in_specs, out_specs=out_specs, check_vma=False)
```

```python
import functools
import math

import jax
import jax.numpy as jnp
from jax import lax
from jax.experimental import pallas as pl
from jax.experimental.pallas import tpu as pltpu
from jax.sharding import PartitionSpec as P

K = 256
ALTS = 2
LO = 8
HI = K // LO
SUB = 8
PACK = 128 // HI
EPSILON = 1e-06
MIB = 1024 * 1024
BAND = 256

F32 = jnp.float32
BF16 = jnp.bfloat16
NT = (((1,), (1,)), ((), ()))
NN = (((1,), (0,)), ((), ()))
TN = (((0,), (0,)), ((), ()))


def mm(a, b, dims=NN):
    return lax.dot_general(a, b, dims, preferred_element_type=F32)


def vmem_spec():
    return pl.BlockSpec(memory_space=pltpu.VMEM)


def smem_spec():
    return pl.BlockSpec(memory_space=pltpu.SMEM)


def cost(us):
    return pl.CostEstimate(flops=int(us * 1e9), bytes_accessed=0, transcendentals=0)


def params(*arrays):
    held = sum(math.prod(a.shape) * a.dtype.itemsize for a in arrays)
    return pltpu.CompilerParams(vmem_limit_bytes=held + 12 * MIB)


def swap(x, axis, size, bits):
    return lax.ppermute(x, axis, [(i, i ^ bits) for i in range(size)])


def pick_kernel(lists, ids_ref, table_ref):
    local = lax.rem(ids_ref[...], lists)
    level = lax.broadcasted_iota(jnp.int32, table_ref.shape, 0)
    table_ref[...] = jnp.where(level == local, 1.0, 0.0).astype(BF16)


def pick_call(ids, lists):
    rows = ids.shape[0]
    return pl.pallas_call(
        functools.partial(pick_kernel, lists),
        out_shape=jax.ShapeDtypeStruct((lists, rows), BF16),
        in_specs=[vmem_spec()],
        out_specs=vmem_spec(),
        compiler_params=params(),
        cost_estimate=cost(10),
        name="pick",
    )(ids.reshape(1, rows))


def residual_kernel(vectors_ref, centroids_ref, table_ref, out_ref):
    table = table_ref[...]
    center = centroids_ref[...]
    first = center.astype(BF16)
    rest = center - first.astype(F32)
    second = rest.astype(BF16)
    third = (rest - second.astype(F32)).astype(BF16)
    picked = mm(table, first, TN) + mm(table, second, TN) + mm(table, third, TN)
    out_ref[...] = (vectors_ref[...].astype(F32) - picked).astype(BF16)


def residual_call(vectors, centroids, ids):
    return pl.pallas_call(
        residual_kernel,
        out_shape=jax.ShapeDtypeStruct(vectors.shape, BF16),
        in_specs=[vmem_spec()] * 3,
        out_specs=vmem_spec(),
        compiler_params=params(),
        cost_estimate=cost(10),
        name="residual",
    )(vectors, centroids, pick_call(ids, centroids.shape[0]))


def packs_of(owned):
    return [range(first, min(first + PACK, owned)) for first in range(0, owned, PACK)]


def hi_table(hi, pack):
    rows = hi.shape[1]
    level = lax.broadcasted_iota(jnp.int32, (HI, rows), 0)
    parts = [jnp.where(level == hi[m : m + 1, :], 1.0, 0.0) for m in pack]
    parts += [jnp.zeros((HI, rows), F32)] * (PACK - len(pack))
    return jnp.concatenate(parts, axis=0).astype(BF16)


def lane_owner(rows):
    return lax.broadcasted_iota(jnp.int32, (rows, 128), 1) // HI


def diagonal(wide, block):
    owner = lane_owner(block)
    total = jnp.zeros((block, 128), F32)
    for i in range(wide.shape[0] // block):
        total = jnp.where(owner == i, wide[i * block : (i + 1) * block, :], total)
    return total


def pack_sums(rotated, codes, pack, with_counts, table=None):
    rows = codes.shape[1]
    hi, lo = codes >> 3, codes & 7
    parts = []
    for m in pack:
        value = rotated[m * SUB : (m + 1) * SUB, :]
        low = jnp.broadcast_to(lo[m : m + 1, :], (SUB, rows))
        parts += [jnp.where(low == level, value, 0.0) for level in range(LO)]
    if with_counts:
        low_level = lax.broadcasted_iota(jnp.int32, (LO, rows), 0)
        parts += [jnp.where(low_level == lo[m : m + 1, :], 1.0, 0.0) for m in pack]
    marked = jnp.concatenate(parts, axis=0).astype(BF16)
    return mm(marked, hi_table(hi, pack), NT) if table is None else mm(marked, table)


def pack_layout(owned, with_counts):
    packs = len(packs_of(owned))
    base, height = packs * LO * SUB, packs * LO
    return base, height, base + (-(-2 * height // 16) * 16 if with_counts else 0)


def write_sums(sums, counts, owned, out_ref):
    base, height, total = pack_layout(owned, counts is not None)
    out_ref[:base, :] = sums.astype(BF16)
    if counts is not None:
        above = jnp.floor(counts * (1.0 / 256.0))
        pieces = [above, counts - above * 256.0]
        pad = total - base - 2 * height
        pieces += [jnp.zeros((pad, 128), F32)] if pad else []
        out_ref[base:, :] = jnp.concatenate(pieces, axis=0).astype(BF16)


def pack_diagonals(totals, owned, with_counts):
    block = LO * SUB
    sums, counts = [], []
    for total, pack in zip(totals, packs_of(owned)):
        size = len(pack)
        sums.append(diagonal(total[: size * block], block))
        if with_counts:
            counts.append(diagonal(total[size * block :], LO))
    return jnp.concatenate(sums, axis=0), jnp.concatenate(counts, axis=0) if with_counts else None


def tree(values):
    while len(values) > 1:
        values = [values[i] + values[i + 1] for i in range(0, len(values), 2)]
    return values[0]


def merge_parts(parts, owned, with_counts):
    base, height, unused = pack_layout(owned, with_counts)
    whole = tree([ref[...].astype(F32) for ref in parts])
    if not with_counts:
        return whole, None
    return whole[:base], whole[base : base + height] * 256.0 + whole[base + height : base + 2 * height]


def code_rows(rows):
    return rows // 128 * 16


def write_codes(codes, out_ref, at):
    owned, rows = codes.shape
    filled = jnp.concatenate([codes, jnp.zeros((16 - owned, rows), F32)], axis=0).astype(BF16)
    for c in range(rows // 128):
        out_ref[at + 16 * c : at + 16 * c + 16, :] = filled[:, 128 * c : 128 * c + 128]


def local_sums_kernel(size, place_ref, rotation_ref, codes_ref, residual_ref, *refs):
    outs, turned, staged = refs[:2], refs[2], refs[3]
    subspaces = codes_ref.shape[0]
    owned = subspaces // size
    base = pack_layout(owned, True)[2]
    rotated = mm(residual_ref[...], rotation_ref[...].astype(BF16)).astype(BF16).astype(F32)
    turned[...] = rotated.T
    for j in range(size):
        staged[j, :owned, :] = codes_ref[j * owned : (j + 1) * owned, :]
    for k in range(size):
        other = place_ref[0] ^ k
        codes = staged[other][:owned]
        value = turned[pl.ds(pl.multiple_of(other * (owned * SUB), 8), owned * SUB), :]
        totals = [pack_sums(value, codes, pack, True) for pack in packs_of(owned)]
        sums, counts = pack_diagonals(totals, owned, True)
        slot = outs[k % 2].at[k // 2]
        write_sums(sums, counts, owned, slot.at[:base])
        write_codes(codes.astype(F32), slot, base)


def local_sums_call(place, rotation, codes, residual, size):
    subspaces, rows = codes.shape
    owned = subspaces // size
    height = -(-owned // 8) * 8
    shape = jax.ShapeDtypeStruct((size // 2, pack_layout(owned, True)[2] + code_rows(rows), 128), BF16)
    return pl.pallas_call(
        functools.partial(local_sums_kernel, size),
        out_shape=(shape,) * 2,
        in_specs=[smem_spec()] + [vmem_spec()] * 3,
        out_specs=(vmem_spec(),) * 2,
        scratch_shapes=[pltpu.VMEM((rotation.shape[1], rows), F32), pltpu.VMEM((size, height, rows), jnp.int32)],
        compiler_params=params(rotation),
        cost_estimate=cost(0),
        name="local_sums",
    )(place, rotation, codes, residual)


def merge_cores_kernel(owned, even_ref, came_ref, *outs):
    base = pack_layout(owned, True)[2]
    length = even_ref.shape[1] - base
    for i, out_ref in enumerate(outs):
        sums, counts = merge_parts([even_ref.at[i], came_ref.at[i]], owned, True)
        write_sums(sums, counts, owned, out_ref.at[:base])
        out_ref[base : base + length, :] = even_ref[i, base:, :]
        out_ref[base + length :, :] = came_ref[i, base:, :]


def merge_cores_call(even, came, owned):
    slots, height, lanes = even.shape
    shape = jax.ShapeDtypeStruct((2 * height - pack_layout(owned, True)[2], lanes), BF16)
    return pl.pallas_call(
        functools.partial(merge_cores_kernel, owned),
        out_shape=(shape,) * slots,
        in_specs=[vmem_spec()] * 2,
        out_specs=(vmem_spec(),) * slots,
        compiler_params=params(),
        cost_estimate=cost(0),
        name="merge_cores",
    )(even, came)


def merge_chips_kernel(owned, *refs):
    parts, (out_ref, codes_ref) = refs[:-2], refs[-2:]
    base = pack_layout(owned, True)[2]
    sums, counts = merge_parts(parts, owned, True)
    write_sums(sums, counts, owned, out_ref)
    length = (parts[0].shape[0] - base) // 2
    for i, part in enumerate(parts):
        for core in range(2):
            for c in range(length // 16):
                at = base + core * length + 16 * c
                piece = part[at : at + 16, :].astype(F32)
                codes_ref[2 * i + core, :, 128 * c : 128 * c + 128] = piece[:owned].astype(jnp.int32)


def merge_chips_call(parts, owned, rows):
    size = 2 * len(parts)
    return pl.pallas_call(
        functools.partial(merge_chips_kernel, owned),
        out_shape=(
            jax.ShapeDtypeStruct((pack_layout(owned, True)[2], 128), BF16),
            jax.ShapeDtypeStruct((size, owned, rows), jnp.int32),
        ),
        in_specs=[vmem_spec()] * len(parts),
        out_specs=(vmem_spec(),) * 2,
        compiler_params=params(),
        cost_estimate=cost(0),
        name="merge_chips",
    )(*parts)


def merge_kernel(owned, first_ref, second_ref, out_ref):
    sums, counts = merge_parts([first_ref, second_ref], owned, True)
    write_sums(sums, counts, owned, out_ref)


def merge_call(first, second, owned):
    return pl.pallas_call(
        functools.partial(merge_kernel, owned),
        out_shape=jax.ShapeDtypeStruct(first.shape, BF16),
        in_specs=[vmem_spec()] * 2,
        out_specs=vmem_spec(),
        compiler_params=params(),
        cost_estimate=cost(0),
        name="merge_groups",
    )(first, second)


def spans_of(held):
    return [(k, k ^ 1) for k in held if k % 2 == 0]


def span_codes(codes_ref, span):
    return jnp.concatenate([codes_ref[k] for k in span], axis=1)


def span_rows(pieces, span):
    return jnp.concatenate([ref[...] for k in span for ref in pieces[k]], axis=0)


def pieces_of(held, refs):
    at = 0
    pieces = {}
    for k, count in held.items():
        pieces[k] = refs[at : at + count]
        at += count
    return pieces


def read_books(sums, counts_in, owned):
    everything, counts = merge_parts(sums, owned, counts_in is None)
    if counts is None:
        counts = counts_in[...]
    block = LO * SUB
    books = []
    for g in range(len(packs_of(owned))):
        rows = []
        for level in range(LO):
            at = g * block + level * SUB
            rows.append(everything[at : at + SUB] / (counts[g * LO + level : g * LO + level + 1] + 1.0))
        books.append(jnp.concatenate(rows, axis=0))
    return books, counts


def widen(books, owned):
    owner = lane_owner(LO * SUB)
    return [
        jnp.concatenate([jnp.where(owner == i, book, 0.0) for i in range(len(pack))], axis=0).astype(BF16)
        for book, pack in zip(books, packs_of(owned))
    ]


def add_spans(total, wide, codes_ref, pieces, spans, tables=None):
    owned = codes_ref.shape[1]
    for i, span in enumerate(spans):
        codes = span_codes(codes_ref, span)
        hi, lo = codes >> 3, codes & 7
        rows = codes.shape[1]
        rebuilt = []
        for g, pack in enumerate(packs_of(owned)):
            table = hi_table(hi, pack) if tables is None else tables[i, g * 128 : (g + 1) * 128, :]
            spread = mm(wide[g], table)
            for j, m in enumerate(pack):
                low = jnp.broadcast_to(lo[m : m + 1, :], (SUB, rows))
                at = j * LO * SUB
                value = spread[at : at + SUB]
                for level in range(1, LO):
                    value = jnp.where(low == level, spread[at + level * SUB : at + (level + 1) * SUB], value)
                rebuilt.append(value)
        part = mm(jnp.concatenate(rebuilt, axis=0).astype(BF16), span_rows(pieces, span))
        total = part if total is None else total + part
    return total


def flat(chunks):
    return {k: len(c) for k, c in chunks.items()}, [piece for c in chunks.values() for piece in c]


def cross_near_kernel(held, groups, codes_ref, *refs):
    sums, pieces, outs = refs[:groups], pieces_of(held, refs[groups:]), refs[groups + sum(held.values()) :]
    total_ref, wide_ref, counts_ref = outs
    owned = codes_ref.shape[1]
    books, counts = read_books(sums, None, owned)
    counts_ref[...] = counts
    wide = widen(books, owned)
    for g, one in enumerate(wide):
        wide_ref[g, : one.shape[0], :] = one
    total_ref[...] = add_spans(None, wide, codes_ref, pieces, spans_of(held))


def cross_near_call(codes, sums, chunks):
    owned = codes.shape[1]
    packs = len(packs_of(owned))
    held, rows = flat(chunks)
    return pl.pallas_call(
        functools.partial(cross_near_kernel, held, len(sums)),
        out_shape=(
            jax.ShapeDtypeStruct((owned * SUB, rows[0].shape[1]), F32),
            jax.ShapeDtypeStruct((packs, PACK * LO * SUB, 128), BF16),
            jax.ShapeDtypeStruct((packs * LO, 128), F32),
        ),
        in_specs=[vmem_spec()] * (1 + len(sums) + len(rows)),
        out_specs=(vmem_spec(),) * 3,
        compiler_params=params(*rows),
        cost_estimate=cost(0),
        name="cross_near",
    )(codes, *sums, *rows)


def cross_far_kernel(held, total_rows, codes_ref, total_ref, wide_ref, *refs):
    pieces, cross_ref = pieces_of(held, refs), refs[-1]
    packs = packs_of(codes_ref.shape[1])
    wide = [wide_ref[g, : len(pack) * LO * SUB, :] for g, pack in enumerate(packs)]
    total = add_spans(total_ref[...], wide, codes_ref, pieces, spans_of(held))
    cross_ref[...] = (total * (1.0 / total_rows)).astype(BF16)


def cross_far_call(codes, total, wide, chunks, total_rows):
    held, rows = flat(chunks)
    return pl.pallas_call(
        functools.partial(cross_far_kernel, held, total_rows),
        out_shape=jax.ShapeDtypeStruct(total.shape, BF16),
        in_specs=[vmem_spec()] * (3 + len(rows)),
        out_specs=vmem_spec(),
        compiler_params=params(*rows),
        cost_estimate=cost(0),
        name="cross_far",
    )(codes, total, wide, *rows)


def cross_kernel(held, groups, total_rows, ready, codes_ref, *refs):
    tables, refs = (refs[0], refs[1:]) if ready else (None, refs)
    sums, counts_in, pieces = refs[:groups], refs[groups], pieces_of(held, refs[groups + 1 :])
    cross_ref, book_ref = refs[-2:]
    owned = codes_ref.shape[1]
    block = LO * SUB
    books, unused = read_books(sums, counts_in, owned)
    for g, book in enumerate(books):
        book_ref[g * block : (g + 1) * block, :] = book
    total = add_spans(None, widen(books, owned), codes_ref, pieces, spans_of(held), tables)
    cross_ref[...] = (total * (1.0 / total_rows)).astype(BF16)


def cross_call(codes, ready, sums, counts, chunks, total_rows):
    owned = codes.shape[1]
    held, rows = flat(chunks)
    tables = [ready[2]] if ready else []
    return pl.pallas_call(
        functools.partial(cross_kernel, held, len(sums), total_rows, bool(ready)),
        out_shape=(
            jax.ShapeDtypeStruct((owned * SUB, rows[0].shape[1]), BF16),
            jax.ShapeDtypeStruct((len(packs_of(owned)) * LO * SUB, 128), F32),
        ),
        in_specs=[vmem_spec()] * (2 + len(tables) + len(sums) + len(rows)),
        out_specs=(vmem_spec(), vmem_spec()),
        compiler_params=params(*rows, *tables),
        cost_estimate=cost(0),
        name="cross",
    )(codes, *tables, *sums, counts, *rows)


def prepare_kernel(held, codes_ref, *refs):
    pieces, (turned_ref, table_ref, across_ref) = pieces_of(held, refs), refs[-3:]
    packs = packs_of(codes_ref.shape[1])
    for i, span in enumerate(spans_of(held)):
        turned_ref[i, :, :] = span_rows(pieces, span).T
        hi = span_codes(codes_ref, span) >> 3
        for g, pack in enumerate(packs):
            table = hi_table(hi, pack)
            across_ref[i, g * 128 : (g + 1) * 128, :] = table
            table_ref[i, :, g * 128 : (g + 1) * 128] = table.T


def prepare_call(codes, chunks):
    size, owned, rows = codes.shape
    held, pieces = flat(chunks)
    lanes = 128 * len(packs_of(owned))
    width = pieces[0].shape[1]
    spans = len(spans_of(held))
    each = size // spans * rows
    shapes = (
        jax.ShapeDtypeStruct((spans, width, each), BF16),
        jax.ShapeDtypeStruct((spans, each, lanes), BF16),
        jax.ShapeDtypeStruct((spans, lanes, each), BF16),
    )
    if sum(math.prod(a.shape) * 2 for a in shapes) > 16 * MIB:
        return None
    return pl.pallas_call(
        functools.partial(prepare_kernel, held),
        out_shape=shapes,
        in_specs=[vmem_spec()] * (1 + len(pieces)),
        out_specs=(vmem_spec(),) * 3,
        compiler_params=params(*pieces, *shapes),
        cost_estimate=cost(0),
        name="prepare",
    )(codes, *pieces)


def bands(x):
    return [x[i : i + BAND] for i in range(0, x.shape[0], BAND)]


def first_step(xb):
    steps = []
    square = None
    for band in bands(xb):
        gram = mm(band, xb, NT)
        part = jnp.sum(gram * gram, keepdims=True)
        square = part if square is None else square + part
        steps.append(mm(gram.astype(BF16), xb))
    norm_square = jnp.sqrt(square + EPSILON)
    scale = lax.rsqrt(norm_square)
    less = 0.5 * scale / norm_square
    return [(1.5 * scale) * band.astype(F32) - less * step for band, step in zip(bands(xb), steps)]


def join(parts):
    if parts[0].shape[0] % 16 == 0:
        return jnp.concatenate(parts, axis=0)
    return jnp.concatenate([p.astype(F32) for p in parts], axis=0).astype(BF16)


def next_sums_kernel(held, ready, codes_ref, *refs):
    size = len(held)
    parts, out_ref = refs[:size], refs[-1]
    if ready:
        turned_ref, table_ref = refs[size : size + 2]
    else:
        pieces = pieces_of(held, refs[size:])
    owned = codes_ref.shape[1]
    height = parts[0].shape[0]
    x = first_step(join([ref[...] for ref in parts]))
    xb = jnp.concatenate([band.astype(BF16) for band in x], axis=0)
    mine = x[0][:height]
    gram = mm(mine.astype(BF16), xb, NT)
    rotation_rows = (1.5 * mine - 0.5 * mm(gram.astype(BF16), xb)).astype(BF16)
    totals = None
    for i, span in enumerate(spans_of(held)):
        if ready:
            rotated = mm(rotation_rows, turned_ref[i])
        else:
            rotated = mm(rotation_rows, span_rows(pieces, span), NT)
        rotated = rotated.astype(BF16).astype(F32)
        codes = span_codes(codes_ref, span)
        more = []
        for g, pack in enumerate(packs_of(owned)):
            table = table_ref[i, :, g * 128 : (g + 1) * 128] if ready else None
            more.append(pack_sums(rotated, codes, pack, False, table))
        totals = more if totals is None else [a + b for a, b in zip(totals, more)]
    write_sums(pack_diagonals(totals, owned, False)[0], None, owned, out_ref)


def next_sums_call(codes, ready, blocks, chunks):
    owned = codes.shape[1]
    held, rows = flat(chunks)
    given = list(ready[:2]) if ready else rows
    return pl.pallas_call(
        functools.partial(next_sums_kernel, held, bool(ready)),
        out_shape=jax.ShapeDtypeStruct((pack_layout(owned, False)[2], 128), BF16),
        in_specs=[vmem_spec()] * (1 + len(blocks) + len(given)),
        out_specs=vmem_spec(),
        compiler_params=params(*given),
        cost_estimate=cost(0),
        name="next_sums",
    )(codes, *blocks, *given)


def final_kernel(size, place_ref, residual_ref, *refs):
    parts, out_ref, whole = refs[:size], refs[size], refs[size + 1]
    height = parts[0].shape[0]
    for k, ref in enumerate(parts):
        at = pl.multiple_of((place_ref[0] ^ k) * height, 16 if whole.dtype == BF16 else 8)
        whole[pl.ds(at, height), :] = ref[...].astype(whole.dtype)
    x = first_step(whole[...].astype(BF16))
    xb = jnp.concatenate([band.astype(BF16) for band in x], axis=0)
    for i in range(0, residual_ref.shape[0], BAND):
        once = mm(residual_ref[i : i + BAND, :], xb, NT)
        less = mm(mm(once.astype(BF16), xb).astype(BF16), xb, NT)
        out_ref[i : i + BAND, :] = (1.5 * once - 0.5 * less).astype(BF16)


def final_call(place, residual, blocks):
    rows, width = residual.shape
    kind = BF16 if blocks[0].shape[0] % 16 == 0 else F32
    return pl.pallas_call(
        functools.partial(final_kernel, len(blocks)),
        out_shape=jax.ShapeDtypeStruct((rows, width), BF16),
        in_specs=[smem_spec()] + [vmem_spec()] * (1 + len(blocks)),
        out_specs=vmem_spec(),
        scratch_shapes=[pltpu.VMEM((width, width), kind)],
        compiler_params=params(),
        cost_estimate=cost(0),
        name="final",
    )(place, residual, *blocks)


def after(x, *first):
    return lax.optimization_barrier((x,) + first)[0]


def near_rows(rows, size):
    return {1 << b: swap(rows, "within", size, 1 << b) for b in range(1, size.bit_length() - 1)}


def far_rows(rows, near, size):
    bits = list(near)
    half = rows.shape[0] // 2
    halves = []
    for order, cut in ((bits, slice(0, half)), (bits[::-1], slice(half, None))):
        here = {0: rows, order[0]: near[order[0]][cut]}
        for bit in order[1:]:
            for k in list(here):
                here[k ^ bit] = swap(here[k], "within", size, bit) if k else near[bit][cut]
        halves.append(here)
    return {k: (halves[0][k], halves[1][k]) for k in halves[0] if k and k not in near}


def both_cores(whole, size):
    return {k ^ 1: tuple(swap(piece, "within", size, 1) for piece in pieces) for k, pieces in whole.items()}


def gather_group(x, size):
    blocks = {k: swap(x, "within", size, k) if k else x for k in range(0, size, 2)}
    for k in list(blocks):
        blocks[k ^ 1] = swap(blocks[k], "within", size, 1)
    return [blocks[k] for k in range(size)]


def scatter_sums(merged, owned, rows, size):
    parts = [merged[0]] + [swap(merged[k // 2], "within", size, k) for k in range(2, size, 2)]
    return merge_chips_call(parts, owned, rows)


def add_over_groups(x, size, last):
    for bit in [1 << b for b in range(size.bit_length() - 2)]:
        x = (x.astype(F32) + swap(x, "group", size, bit).astype(F32)).astype(BF16)
    x = after(x, *last)
    return [x, swap(x, "group", size, size // 2)]


def reduce_cross(cross, size, *last):
    return tree([part.astype(F32) for part in add_over_groups(cross, size, last)]).astype(BF16)


def per_device(vectors, centroids, list_ids, codes, rotation):
    groups = lax.axis_size("group")
    size = lax.axis_size("within")
    rows, width = vectors.shape
    owned = codes.shape[1] // size
    total_rows = rows * size * groups
    place = lax.axis_index("within").astype(jnp.int32).reshape(1)
    residual = residual_call(vectors, centroids, list_ids)
    near = near_rows(residual, size)
    twin = swap(residual, "within", size, 1)
    even, odd = local_sums_call(place, rotation, codes.T, after(residual, twin), size)
    merged = merge_cores_call(even, swap(odd, "within", size, 1), owned)
    sums, own_codes = scatter_sums(merged, owned, rows, size)
    far = far_rows(residual, near, size)
    near = {k: after(rows_near, sums) for k, rows_near in near.items()}
    for bit in [1 << b for b in range(groups.bit_length() - 2)]:
        sums = merge_call(sums, swap(sums, "group", groups, bit), owned)
    parts = [sums, swap(sums, "group", groups, groups // 2)]
    chunks = {0: (residual,), 1: (twin,)}
    for k, rows_near in near.items():
        chunks[k] = (rows_near,)
        chunks[k ^ 1] = (swap(rows_near, "within", size, 1),)
    total, wide, counts = cross_near_call(own_codes, parts, chunks)
    far = {k: tuple(after(piece, parts[1]) for piece in pieces) for k, pieces in far.items()}
    far = {**far, **both_cores(far, size)}
    cross = cross_far_call(own_codes, total, wide, far, total_rows)
    chunks.update(far)
    ready = prepare_call(after(own_codes, cross), chunks)
    for alternation in range(1, ALTS):
        block = reduce_cross(cross, groups)
        if ready:
            block = after(block, *ready)
        parts = add_over_groups(next_sums_call(own_codes, ready, gather_group(block, size), chunks), groups, ())
        cross, book = cross_call(own_codes, ready, parts, counts, chunks, total_rows)
    packs = len(packs_of(owned))
    book = book.reshape(packs, LO * SUB, PACK, HI).transpose(0, 2, 3, 1).reshape(packs * PACK, K * SUB)[:owned]
    blocks = gather_group(reduce_cross(cross, groups, book), size)
    rotated_out = final_call(place, residual, blocks)
    return (rotated_out, book)


def solution(mesh):
    in_specs = (
        P(("group", "within"), None),
        P(("group", "within"), None),
        P(("group", "within")),
        P(("group", "within"), None),
        P(),
    )
    out_specs = (P(("group", "within"), None), P("within", None))
    return jax.shard_map(per_device, mesh=mesh, in_specs=in_specs, out_specs=out_specs, check_vma=False)
```

```python
import functools
import math

import jax
import jax.numpy as jnp
from jax import lax
from jax.experimental import pallas as pl
from jax.experimental.pallas import tpu as pltpu
from jax.sharding import PartitionSpec as P

K = 256
ALTS = 2
LO = 4
HI = K // LO
SUB = 8
LANES = 256
PACK = LANES // HI
MARKS = 8
EPSILON = 1e-06
MIB = 1024 * 1024
BAND = 256

F32 = jnp.float32
BF16 = jnp.bfloat16
NT = (((1,), (1,)), ((), ()))
NN = (((1,), (0,)), ((), ()))
TN = (((0,), (0,)), ((), ()))


def mm(a, b, dims=NN):
    return lax.dot_general(a, b, dims, preferred_element_type=F32)


def vmem_spec():
    return pl.BlockSpec(memory_space=pltpu.VMEM)


def smem_spec():
    return pl.BlockSpec(memory_space=pltpu.SMEM)


def cost(us):
    return pl.CostEstimate(flops=int(us * 1e9), bytes_accessed=0, transcendentals=0)


def params(*arrays):
    held = sum(math.prod(a.shape) * a.dtype.itemsize for a in arrays)
    return pltpu.CompilerParams(vmem_limit_bytes=held + 12 * MIB)


def swap(x, axis, size, bits):
    return lax.ppermute(x, axis, [(i, i ^ bits) for i in range(size)])


def pick_kernel(lists, ids_ref, table_ref):
    local = lax.rem(ids_ref[...], lists)
    level = lax.broadcasted_iota(jnp.int32, table_ref.shape, 0)
    table_ref[...] = jnp.where(level == local, 1.0, 0.0).astype(BF16)


def pick_call(ids, lists):
    rows = ids.shape[0]
    return pl.pallas_call(
        functools.partial(pick_kernel, lists),
        out_shape=jax.ShapeDtypeStruct((lists, rows), BF16),
        in_specs=[vmem_spec()],
        out_specs=vmem_spec(),
        compiler_params=params(),
        cost_estimate=cost(10),
        name="pick",
    )(ids.reshape(1, rows))


def residual_kernel(vectors_ref, centroids_ref, table_ref, out_ref):
    table = table_ref[...]
    center = centroids_ref[...]
    first = center.astype(BF16)
    rest = center - first.astype(F32)
    second = rest.astype(BF16)
    third = (rest - second.astype(F32)).astype(BF16)
    picked = mm(table, first, TN) + mm(table, second, TN) + mm(table, third, TN)
    out_ref[...] = (vectors_ref[...].astype(F32) - picked).astype(BF16)


def residual_call(vectors, centroids, ids):
    return pl.pallas_call(
        residual_kernel,
        out_shape=jax.ShapeDtypeStruct(vectors.shape, BF16),
        in_specs=[vmem_spec()] * 3,
        out_specs=vmem_spec(),
        compiler_params=params(),
        cost_estimate=cost(10),
        name="residual",
    )(vectors, centroids, pick_call(ids, centroids.shape[0]))


def split(codes):
    return codes >> 2, codes & 3


def packs_of(owned):
    return [range(first, min(first + PACK, owned)) for first in range(0, owned, PACK)]


def hi_table(hi, pack):
    rows = hi.shape[1]
    level = lax.broadcasted_iota(jnp.int32, (HI, rows), 0)
    parts = [jnp.where(level == hi[m : m + 1, :], 1.0, 0.0) for m in pack]
    parts += [jnp.zeros((HI, rows), F32)] * (PACK - len(pack))
    return jnp.concatenate(parts, axis=0).astype(BF16)


def lane_owner(rows):
    return lax.broadcasted_iota(jnp.int32, (rows, LANES), 1) // HI


def diagonal(wide, block):
    owner = lane_owner(block)
    total = jnp.zeros((block, LANES), F32)
    for i in range(wide.shape[0] // block):
        total = jnp.where(owner == i, wide[i * block : (i + 1) * block, :], total)
    return total


def pack_sums(rotated, codes, pack, with_counts, table=None):
    rows = codes.shape[1]
    hi, lo = split(codes)
    parts = []
    for m in pack:
        value = rotated[m * SUB : (m + 1) * SUB, :]
        low = jnp.broadcast_to(lo[m : m + 1, :], (SUB, rows))
        parts += [jnp.where(low == level, value, 0.0) for level in range(LO)]
    if with_counts:
        low_level = lax.broadcasted_iota(jnp.int32, (MARKS, rows), 0)
        parts += [jnp.where(low_level == lo[m : m + 1, :], 1.0, 0.0) for m in pack]
    marked = jnp.concatenate(parts, axis=0).astype(BF16)
    return mm(marked, hi_table(hi, pack), NT) if table is None else mm(marked, table)


def pack_layout(owned, with_counts):
    packs = len(packs_of(owned))
    base, height = packs * LO * SUB, packs * MARKS
    return base, height, base + (-(-height // 16) * 16 if with_counts else 0)


def write_sums(sums, counts, owned, out_ref):
    base, height, total = pack_layout(owned, counts is not None)
    out_ref[:base, :] = sums.astype(BF16)
    if counts is not None:
        above = jnp.floor(counts * (1.0 / 256.0))
        below = counts - above * 256.0
        pieces = []
        for at in range(0, height, MARKS):
            pieces.append(jnp.concatenate([above[at : at + LO], below[at : at + LO]], axis=0))
        if total > base + height:
            pieces.append(jnp.zeros((total - base - height, LANES), F32))
        out_ref[base:, :] = jnp.concatenate(pieces, axis=0).astype(BF16)


def pack_diagonals(totals, owned, with_counts):
    block = LO * SUB
    sums, counts = [], []
    for total, pack in zip(totals, packs_of(owned)):
        size = len(pack)
        sums.append(diagonal(total[: size * block], block))
        if with_counts:
            counts.append(diagonal(total[size * block :], MARKS))
    return jnp.concatenate(sums, axis=0), jnp.concatenate(counts, axis=0) if with_counts else None


def tree(values):
    while len(values) > 1:
        values = [values[i] + values[i + 1] for i in range(0, len(values), 2)]
    return values[0]


def merge_parts(parts, owned, with_counts):
    base, height, unused = pack_layout(owned, with_counts)
    whole = tree([ref[...].astype(F32) for ref in parts])
    if not with_counts:
        return whole, None
    counts = []
    for at in range(base, base + height, MARKS):
        count = whole[at : at + LO] * 256.0 + whole[at + LO : at + MARKS]
        counts.append(jnp.concatenate([count, jnp.zeros((MARKS - LO, LANES), F32)], axis=0))
    return whole[:base], jnp.concatenate(counts, axis=0)


def code_rows(rows):
    return rows // LANES * 16


def write_codes(codes, out_ref, at):
    owned, rows = codes.shape
    filled = jnp.concatenate([codes, jnp.zeros((16 - owned, rows), F32)], axis=0).astype(BF16)
    for c in range(rows // LANES):
        out_ref[at + 16 * c : at + 16 * c + 16, :] = filled[:, LANES * c : LANES * (c + 1)]


def local_sums_kernel(size, place_ref, rotation_ref, codes_ref, residual_ref, *refs):
    outs, turned, staged = refs[:2], refs[2], refs[3]
    subspaces = codes_ref.shape[0]
    owned = subspaces // size
    base = pack_layout(owned, True)[2]
    rotated = mm(residual_ref[...], rotation_ref[...].astype(BF16)).astype(BF16).astype(F32)
    turned[...] = rotated.T
    for j in range(size):
        staged[j, :owned, :] = codes_ref[j * owned : (j + 1) * owned, :]
    for k in range(size):
        other = place_ref[0] ^ k
        codes = staged[other][:owned]
        value = turned[pl.ds(pl.multiple_of(other * (owned * SUB), 8), owned * SUB), :]
        totals = [pack_sums(value, codes, pack, True) for pack in packs_of(owned)]
        sums, counts = pack_diagonals(totals, owned, True)
        slot = outs[k % 2].at[k // 2]
        write_sums(sums, counts, owned, slot.at[:base])
        write_codes(codes.astype(F32), slot, base)


def local_sums_call(place, rotation, codes, residual, size):
    subspaces, rows = codes.shape
    owned = subspaces // size
    height = -(-owned // 8) * 8
    shape = jax.ShapeDtypeStruct((size // 2, pack_layout(owned, True)[2] + code_rows(rows), LANES), BF16)
    return pl.pallas_call(
        functools.partial(local_sums_kernel, size),
        out_shape=(shape,) * 2,
        in_specs=[smem_spec()] + [vmem_spec()] * 3,
        out_specs=(vmem_spec(),) * 2,
        scratch_shapes=[pltpu.VMEM((rotation.shape[1], rows), F32), pltpu.VMEM((size, height, rows), jnp.int32)],
        compiler_params=params(rotation),
        cost_estimate=cost(0),
        name="local_sums",
    )(place, rotation, codes, residual)


def merge_cores_kernel(owned, even_ref, came_ref, *outs):
    base = pack_layout(owned, True)[2]
    length = even_ref.shape[1] - base
    for i, out_ref in enumerate(outs):
        sums, counts = merge_parts([even_ref.at[i], came_ref.at[i]], owned, True)
        write_sums(sums, counts, owned, out_ref.at[:base])
        out_ref[base : base + length, :] = even_ref[i, base:, :]
        out_ref[base + length :, :] = came_ref[i, base:, :]


def merge_cores_call(even, came, owned):
    slots, height, lanes = even.shape
    shape = jax.ShapeDtypeStruct((2 * height - pack_layout(owned, True)[2], lanes), BF16)
    return pl.pallas_call(
        functools.partial(merge_cores_kernel, owned),
        out_shape=(shape,) * slots,
        in_specs=[vmem_spec()] * 2,
        out_specs=(vmem_spec(),) * slots,
        compiler_params=params(),
        cost_estimate=cost(0),
        name="merge_cores",
    )(even, came)


def merge_chips_kernel(owned, *refs):
    parts, (out_ref, codes_ref) = refs[:-2], refs[-2:]
    base = pack_layout(owned, True)[2]
    sums, counts = merge_parts(parts, owned, True)
    write_sums(sums, counts, owned, out_ref)
    length = (parts[0].shape[0] - base) // 2
    for i, part in enumerate(parts):
        for core in range(2):
            for c in range(length // 16):
                at = base + core * length + 16 * c
                piece = part[at : at + 16, :].astype(F32)
                codes_ref[2 * i + core, :, LANES * c : LANES * (c + 1)] = piece[:owned].astype(jnp.int32)


def merge_chips_call(parts, owned, rows):
    size = 2 * len(parts)
    return pl.pallas_call(
        functools.partial(merge_chips_kernel, owned),
        out_shape=(
            jax.ShapeDtypeStruct((pack_layout(owned, True)[2], LANES), BF16),
            jax.ShapeDtypeStruct((size, owned, rows), jnp.int32),
        ),
        in_specs=[vmem_spec()] * len(parts),
        out_specs=(vmem_spec(),) * 2,
        compiler_params=params(),
        cost_estimate=cost(0),
        name="merge_chips",
    )(*parts)


def merge_kernel(owned, first_ref, second_ref, out_ref):
    sums, counts = merge_parts([first_ref, second_ref], owned, True)
    write_sums(sums, counts, owned, out_ref)


def merge_call(first, second, owned):
    return pl.pallas_call(
        functools.partial(merge_kernel, owned),
        out_shape=jax.ShapeDtypeStruct(first.shape, BF16),
        in_specs=[vmem_spec()] * 2,
        out_specs=vmem_spec(),
        compiler_params=params(),
        cost_estimate=cost(0),
        name="merge_groups",
    )(first, second)


def spans_of(held):
    return [(k, k ^ 1) for k in held if k % 2 == 0]


def span_codes(codes_ref, span):
    return jnp.concatenate([codes_ref[k] for k in span], axis=1)


def span_rows(pieces, span):
    return jnp.concatenate([ref[...] for k in span for ref in pieces[k]], axis=0)


def pieces_of(held, refs):
    at = 0
    pieces = {}
    for k, count in held.items():
        pieces[k] = refs[at : at + count]
        at += count
    return pieces


def read_books(sums, counts_in, owned):
    everything, counts = merge_parts(sums, owned, counts_in is None)
    if counts is None:
        counts = counts_in[...]
    block = LO * SUB
    books = []
    for g in range(len(packs_of(owned))):
        rows = []
        for level in range(LO):
            at = g * block + level * SUB
            rows.append(everything[at : at + SUB] / (counts[g * MARKS + level : g * MARKS + level + 1] + 1.0))
        books.append(jnp.concatenate(rows, axis=0))
    return books, counts


def widen(books, owned):
    owner = lane_owner(LO * SUB)
    return [
        jnp.concatenate([jnp.where(owner == i, book, 0.0) for i in range(len(pack))], axis=0).astype(BF16)
        for book, pack in zip(books, packs_of(owned))
    ]


def add_spans(total, wide, codes_ref, pieces, spans, tables=None):
    owned = codes_ref.shape[1]
    for i, span in enumerate(spans):
        codes = span_codes(codes_ref, span)
        hi, lo = split(codes)
        rows = codes.shape[1]
        rebuilt = []
        for g, pack in enumerate(packs_of(owned)):
            table = hi_table(hi, pack) if tables is None else tables[i, g * LANES : (g + 1) * LANES, :]
            spread = mm(wide[g], table)
            for j, m in enumerate(pack):
                low = jnp.broadcast_to(lo[m : m + 1, :], (SUB, rows))
                at = j * LO * SUB
                value = spread[at : at + SUB]
                for level in range(1, LO):
                    value = jnp.where(low == level, spread[at + level * SUB : at + (level + 1) * SUB], value)
                rebuilt.append(value)
        part = mm(jnp.concatenate(rebuilt, axis=0).astype(BF16), span_rows(pieces, span))
        total = part if total is None else total + part
    return total


def flat(chunks):
    return {k: len(c) for k, c in chunks.items()}, [piece for c in chunks.values() for piece in c]


def cross_near_kernel(held, groups, codes_ref, *refs):
    sums, pieces, outs = refs[:groups], pieces_of(held, refs[groups:]), refs[groups + sum(held.values()) :]
    total_ref, wide_ref, counts_ref = outs
    owned = codes_ref.shape[1]
    books, counts = read_books(sums, None, owned)
    counts_ref[...] = counts
    wide = widen(books, owned)
    for g, one in enumerate(wide):
        wide_ref[g, : one.shape[0], :] = one
    total_ref[...] = add_spans(None, wide, codes_ref, pieces, spans_of(held))


def cross_near_call(codes, sums, chunks):
    owned = codes.shape[1]
    packs = len(packs_of(owned))
    held, rows = flat(chunks)
    return pl.pallas_call(
        functools.partial(cross_near_kernel, held, len(sums)),
        out_shape=(
            jax.ShapeDtypeStruct((owned * SUB, rows[0].shape[1]), F32),
            jax.ShapeDtypeStruct((packs, PACK * LO * SUB, LANES), BF16),
            jax.ShapeDtypeStruct((packs * MARKS, LANES), F32),
        ),
        in_specs=[vmem_spec()] * (1 + len(sums) + len(rows)),
        out_specs=(vmem_spec(),) * 3,
        compiler_params=params(*rows),
        cost_estimate=cost(0),
        name="cross_near",
    )(codes, *sums, *rows)


def cross_far_kernel(held, total_rows, codes_ref, total_ref, wide_ref, *refs):
    pieces, cross_ref = pieces_of(held, refs), refs[-1]
    packs = packs_of(codes_ref.shape[1])
    wide = [wide_ref[g, : len(pack) * LO * SUB, :] for g, pack in enumerate(packs)]
    total = add_spans(total_ref[...], wide, codes_ref, pieces, spans_of(held))
    cross_ref[...] = (total * (1.0 / total_rows)).astype(BF16)


def cross_far_call(codes, total, wide, chunks, total_rows):
    held, rows = flat(chunks)
    return pl.pallas_call(
        functools.partial(cross_far_kernel, held, total_rows),
        out_shape=jax.ShapeDtypeStruct(total.shape, BF16),
        in_specs=[vmem_spec()] * (3 + len(rows)),
        out_specs=vmem_spec(),
        compiler_params=params(*rows),
        cost_estimate=cost(0),
        name="cross_far",
    )(codes, total, wide, *rows)


def cross_kernel(held, groups, total_rows, ready, codes_ref, *refs):
    tables, refs = (refs[0], refs[1:]) if ready else (None, refs)
    sums, counts_in, pieces = refs[:groups], refs[groups], pieces_of(held, refs[groups + 1 :])
    cross_ref, book_ref = refs[-2:]
    owned = codes_ref.shape[1]
    block = LO * SUB
    books, unused = read_books(sums, counts_in, owned)
    for g, book in enumerate(books):
        book_ref[g * block : (g + 1) * block, :] = book
    total = add_spans(None, widen(books, owned), codes_ref, pieces, spans_of(held), tables)
    cross_ref[...] = (total * (1.0 / total_rows)).astype(BF16)


def cross_call(codes, ready, sums, counts, chunks, total_rows):
    owned = codes.shape[1]
    held, rows = flat(chunks)
    tables = [ready[2]] if ready else []
    return pl.pallas_call(
        functools.partial(cross_kernel, held, len(sums), total_rows, bool(ready)),
        out_shape=(
            jax.ShapeDtypeStruct((owned * SUB, rows[0].shape[1]), BF16),
            jax.ShapeDtypeStruct((len(packs_of(owned)) * LO * SUB, LANES), F32),
        ),
        in_specs=[vmem_spec()] * (2 + len(tables) + len(sums) + len(rows)),
        out_specs=(vmem_spec(), vmem_spec()),
        compiler_params=params(*rows, *tables),
        cost_estimate=cost(0),
        name="cross",
    )(codes, *tables, *sums, counts, *rows)


def turn_kernel(held, *refs):
    pieces, turned_ref = pieces_of(held, refs), refs[-1]
    for i, span in enumerate(spans_of(held)):
        turned_ref[i, :, :] = span_rows(pieces, span).T


def tables_kernel(spans, codes_ref, table_ref, across_ref):
    packs = packs_of(codes_ref.shape[1])
    for i, span in enumerate(spans):
        hi = split(span_codes(codes_ref, span))[0]
        for g, pack in enumerate(packs):
            table = hi_table(hi, pack)
            across_ref[i, g * LANES : (g + 1) * LANES, :] = table
            table_ref[i, :, g * LANES : (g + 1) * LANES] = table.T


def prepare_call(codes, chunks, after_codes, after_rows):
    size, owned, rows = codes.shape
    held, pieces = flat(chunks)
    lanes = LANES * len(packs_of(owned))
    width = pieces[0].shape[1]
    spans = spans_of(held)
    each = size // len(spans) * rows
    turned = jax.ShapeDtypeStruct((len(spans), width, each), BF16)
    tables = (
        jax.ShapeDtypeStruct((len(spans), each, lanes), BF16),
        jax.ShapeDtypeStruct((len(spans), lanes, each), BF16),
    )
    if sum(math.prod(a.shape) * 2 for a in (turned, *tables)) > 20 * MIB:
        return None
    rows_turned = pl.pallas_call(
        functools.partial(turn_kernel, held),
        out_shape=turned,
        in_specs=[vmem_spec()] * len(pieces),
        out_specs=vmem_spec(),
        compiler_params=params(turned),
        cost_estimate=cost(0),
        name="turn_rows",
    )(after(pieces[0], *after_rows), *pieces[1:])
    two = pl.pallas_call(
        functools.partial(tables_kernel, spans),
        out_shape=tables,
        in_specs=[vmem_spec()],
        out_specs=(vmem_spec(),) * 2,
        compiler_params=params(*tables),
        cost_estimate=cost(0),
        name="tables",
    )(after(codes, *after_codes))
    return (rows_turned, *two)


def bands(x):
    return [x[i : i + BAND] for i in range(0, x.shape[0], BAND)]


def first_step(xb):
    steps = []
    square = None
    for band in bands(xb):
        gram = mm(band, xb, NT)
        part = jnp.sum(gram * gram, keepdims=True)
        square = part if square is None else square + part
        steps.append(mm(gram.astype(BF16), xb))
    norm_square = jnp.sqrt(square + EPSILON)
    scale = lax.rsqrt(norm_square)
    less = 0.5 * scale / norm_square
    return [(1.5 * scale) * band.astype(F32) - less * step for band, step in zip(bands(xb), steps)]


def join(parts):
    if parts[0].shape[0] % 16 == 0:
        return jnp.concatenate(parts, axis=0)
    return jnp.concatenate([p.astype(F32) for p in parts], axis=0).astype(BF16)


def next_sums_kernel(held, ready, codes_ref, *refs):
    size = len(held)
    parts, out_ref = refs[:size], refs[-1]
    if ready:
        turned_ref, table_ref = refs[size : size + 2]
    else:
        pieces = pieces_of(held, refs[size:])
    owned = codes_ref.shape[1]
    height = parts[0].shape[0]
    x = first_step(join([ref[...] for ref in parts]))
    xb = jnp.concatenate([band.astype(BF16) for band in x], axis=0)
    mine = x[0][:height]
    gram = mm(mine.astype(BF16), xb, NT)
    rotation_rows = (1.5 * mine - 0.5 * mm(gram.astype(BF16), xb)).astype(BF16)
    totals = None
    for i, span in enumerate(spans_of(held)):
        if ready:
            rotated = mm(rotation_rows, turned_ref[i])
        else:
            rotated = mm(rotation_rows, span_rows(pieces, span), NT)
        rotated = rotated.astype(BF16).astype(F32)
        codes = span_codes(codes_ref, span)
        more = []
        for g, pack in enumerate(packs_of(owned)):
            table = table_ref[i, :, g * LANES : (g + 1) * LANES] if ready else None
            more.append(pack_sums(rotated, codes, pack, False, table))
        totals = more if totals is None else [a + b for a, b in zip(totals, more)]
    write_sums(pack_diagonals(totals, owned, False)[0], None, owned, out_ref)


def next_sums_call(codes, ready, blocks, chunks):
    owned = codes.shape[1]
    held, rows = flat(chunks)
    given = list(ready[:2]) if ready else rows
    return pl.pallas_call(
        functools.partial(next_sums_kernel, held, bool(ready)),
        out_shape=jax.ShapeDtypeStruct((pack_layout(owned, False)[2], LANES), BF16),
        in_specs=[vmem_spec()] * (1 + len(blocks) + len(given)),
        out_specs=vmem_spec(),
        compiler_params=params(*given),
        cost_estimate=cost(0),
        name="next_sums",
    )(codes, *blocks, *given)


def final_kernel(size, place_ref, residual_ref, *refs):
    parts, out_ref, whole = refs[:size], refs[size], refs[size + 1]
    height = parts[0].shape[0]
    for k, ref in enumerate(parts):
        at = pl.multiple_of((place_ref[0] ^ k) * height, 16 if whole.dtype == BF16 else 8)
        whole[pl.ds(at, height), :] = ref[...].astype(whole.dtype)
    x = first_step(whole[...].astype(BF16))
    xb = jnp.concatenate([band.astype(BF16) for band in x], axis=0)
    for i in range(0, residual_ref.shape[0], BAND):
        once = mm(residual_ref[i : i + BAND, :], xb, NT)
        less = mm(mm(once.astype(BF16), xb).astype(BF16), xb, NT)
        out_ref[i : i + BAND, :] = (1.5 * once - 0.5 * less).astype(BF16)


def final_call(place, residual, blocks):
    rows, width = residual.shape
    kind = BF16 if blocks[0].shape[0] % 16 == 0 else F32
    return pl.pallas_call(
        functools.partial(final_kernel, len(blocks)),
        out_shape=jax.ShapeDtypeStruct((rows, width), BF16),
        in_specs=[smem_spec()] + [vmem_spec()] * (1 + len(blocks)),
        out_specs=vmem_spec(),
        scratch_shapes=[pltpu.VMEM((width, width), kind)],
        compiler_params=params(),
        cost_estimate=cost(0),
        name="final",
    )(place, residual, *blocks)


def after(x, *first):
    return lax.optimization_barrier((x,) + first)[0]


def near_rows(rows, size):
    return {1 << b: swap(rows, "within", size, 1 << b) for b in range(1, size.bit_length() - 1)}


def far_rows(rows, near, size):
    bits = list(near)
    half = rows.shape[0] // 2
    halves = []
    for order, cut in ((bits, slice(0, half)), (bits[::-1], slice(half, None))):
        here = {0: rows, order[0]: near[order[0]][cut]}
        for bit in order[1:]:
            for k in list(here):
                here[k ^ bit] = swap(here[k], "within", size, bit) if k else near[bit][cut]
        halves.append(here)
    return {k: (halves[0][k], halves[1][k]) for k in halves[0] if k and k not in near}


def both_cores(whole, size):
    return {k ^ 1: tuple(swap(piece, "within", size, 1) for piece in pieces) for k, pieces in whole.items()}


def gather_group(x, size):
    blocks = {k: swap(x, "within", size, k) if k else x for k in range(0, size, 2)}
    for k in list(blocks):
        blocks[k ^ 1] = swap(blocks[k], "within", size, 1)
    return [blocks[k] for k in range(size)]


def scatter_sums(merged, owned, rows, size):
    parts = [merged[0]] + [swap(merged[k // 2], "within", size, k) for k in range(2, size, 2)]
    return merge_chips_call(parts, owned, rows)


def direct(x, size):
    return [x] + [swap(x, "group", size, k) for k in range(1, size)]


def reduce_cross(cross, size, last):
    bits = [1 << b for b in range(size.bit_length() - 1)]
    for bit in bits:
        if bit == bits[-1]:
            cross = after(cross, *last)
        cross = (cross.astype(F32) + swap(cross, "group", size, bit).astype(F32)).astype(BF16)
    return cross


def per_device(vectors, centroids, list_ids, codes, rotation):
    groups = lax.axis_size("group")
    size = lax.axis_size("within")
    rows, width = vectors.shape
    owned = codes.shape[1] // size
    total_rows = rows * size * groups
    place = lax.axis_index("within").astype(jnp.int32).reshape(1)
    residual = residual_call(vectors, centroids, list_ids)
    near = near_rows(residual, size)
    twin = swap(residual, "within", size, 1)
    even, odd = local_sums_call(place, rotation, codes.T, after(residual, twin), size)
    merged = merge_cores_call(even, swap(odd, "within", size, 1), owned)
    sums, own_codes = scatter_sums(merged, owned, rows, size)
    far = far_rows(residual, near, size)
    near = {k: after(rows_near, sums) for k, rows_near in near.items()}
    for bit in [1 << b for b in range(groups.bit_length() - 2)]:
        sums = merge_call(sums, swap(sums, "group", groups, bit), owned)
    parts = [sums, swap(sums, "group", groups, groups // 2)]
    chunks = {0: (residual,), 1: (twin,)}
    for k, rows_near in near.items():
        chunks[k] = (rows_near,)
        chunks[k ^ 1] = (swap(rows_near, "within", size, 1),)
    total, wide, counts = cross_near_call(own_codes, parts, chunks)
    far = {k: tuple(after(piece, parts[1]) for piece in pieces) for k, pieces in far.items()}
    far = {**far, **both_cores(far, size)}
    cross = cross_far_call(own_codes, total, wide, far, total_rows)
    chunks.update(far)
    ready = prepare_call(own_codes, chunks, (cross,), (cross,))
    for alternation in range(1, ALTS):
        block = reduce_cross(cross, groups, ready[:1] if ready else ())
        if ready:
            block = after(block, *ready)
        parts = direct(next_sums_call(own_codes, ready, gather_group(block, size), chunks), groups)
        cross, book = cross_call(own_codes, ready, parts, counts, chunks, total_rows)
    packs = len(packs_of(owned))
    book = book.reshape(packs, LO * SUB, PACK, HI).transpose(0, 2, 3, 1).reshape(packs * PACK, K * SUB)[:owned]
    blocks = gather_group(reduce_cross(cross, groups, (book,)), size)
    rotated_out = final_call(place, residual, blocks)
    return (rotated_out, book)


def solution(mesh):
    in_specs = (
        P(("group", "within"), None),
        P(("group", "within"), None),
        P(("group", "within")),
        P(("group", "within"), None),
        P(),
    )
    out_specs = (P(("group", "within"), None), P("within", None))
    return jax.shard_map(per_device, mesh=mesh, in_specs=in_specs, out_specs=out_specs, check_vma=False)
```

```python
import functools
import math

import jax
import jax.numpy as jnp
from jax import lax
from jax.experimental import pallas as pl
from jax.experimental.pallas import tpu as pltpu
from jax.sharding import PartitionSpec as P

K = 256
ALTS = 2
LO = 4
HI = K // LO
SUB = 8
LANES = 256
PACK = LANES // HI
MARKS = 8
SPAN = 2
EPSILON = 1e-06
MIB = 1024 * 1024
BAND = 256

F32 = jnp.float32
BF16 = jnp.bfloat16
NT = (((1,), (1,)), ((), ()))
NN = (((1,), (0,)), ((), ()))
TN = (((0,), (0,)), ((), ()))


def mm(a, b, dims=NN):
    return lax.dot_general(a, b, dims, preferred_element_type=F32)


def vmem_spec():
    return pl.BlockSpec(memory_space=pltpu.VMEM)


def smem_spec():
    return pl.BlockSpec(memory_space=pltpu.SMEM)


def cost(us):
    return pl.CostEstimate(flops=int(us * 1e9), bytes_accessed=0, transcendentals=0)


def params(*arrays):
    held = sum(math.prod(a.shape) * a.dtype.itemsize for a in arrays)
    return pltpu.CompilerParams(vmem_limit_bytes=held + 12 * MIB)


def swap(x, axis, size, bits):
    return lax.ppermute(x, axis, [(i, i ^ bits) for i in range(size)])


def levels_kernel(out_ref):
    out_ref[...] = lax.broadcasted_iota(jnp.int32, out_ref.shape, 0)


def pick_kernel(lists, ids_ref, levels_ref, table_ref):
    local = lax.rem(ids_ref[...], lists)
    table_ref[...] = jnp.where(levels_ref[...] == local, 1.0, 0.0).astype(BF16)


def pick_call(ids, lists):
    rows = ids.shape[0]
    levels = pl.pallas_call(
        levels_kernel,
        out_shape=jax.ShapeDtypeStruct((lists, rows), jnp.int32),
        out_specs=vmem_spec(),
        compiler_params=params(),
        cost_estimate=cost(10),
        name="levels",
    )()
    return pl.pallas_call(
        functools.partial(pick_kernel, lists),
        out_shape=jax.ShapeDtypeStruct((lists, rows), BF16),
        in_specs=[vmem_spec()] * 2,
        out_specs=vmem_spec(),
        compiler_params=params(),
        cost_estimate=cost(0),
        name="pick",
    )(ids.reshape(1, rows), levels)


def residual_kernel(vectors_ref, centroids_ref, table_ref, out_ref):
    table = table_ref[...]
    center = centroids_ref[...]
    first = center.astype(BF16)
    rest = center - first.astype(F32)
    second = rest.astype(BF16)
    third = (rest - second.astype(F32)).astype(BF16)
    picked = mm(table, first, TN) + mm(table, second, TN) + mm(table, third, TN)
    out_ref[...] = (vectors_ref[...].astype(F32) - picked).astype(BF16)


def residual_call(vectors, centroids, ids):
    return pl.pallas_call(
        residual_kernel,
        out_shape=jax.ShapeDtypeStruct(vectors.shape, BF16),
        in_specs=[vmem_spec()] * 3,
        out_specs=vmem_spec(),
        compiler_params=params(),
        cost_estimate=cost(10),
        name="residual",
    )(vectors, centroids, pick_call(ids, centroids.shape[0]))


def split(codes):
    return codes >> 2, codes & 3


def packs_of(owned):
    return [range(first, min(first + PACK, owned)) for first in range(0, owned, PACK)]


def hi_table(hi, pack):
    rows = hi.shape[1]
    level = lax.broadcasted_iota(jnp.int32, (HI, rows), 0)
    parts = [jnp.where(level == hi[m : m + 1, :], 1.0, 0.0) for m in pack]
    parts += [jnp.zeros((HI, rows), F32)] * (PACK - len(pack))
    return jnp.concatenate(parts, axis=0).astype(BF16)


def lane_owner(rows):
    return lax.broadcasted_iota(jnp.int32, (rows, LANES), 1) // HI


def diagonal(wide, block):
    owner = lane_owner(block)
    total = jnp.zeros((block, LANES), F32)
    for i in range(wide.shape[0] // block):
        total = jnp.where(owner == i, wide[i * block : (i + 1) * block, :], total)
    return total


def pack_sums(rotated, codes, pack, with_counts, table=None):
    rows = codes.shape[1]
    hi, lo = split(codes)
    parts = []
    for m in pack:
        value = rotated[m * SUB : (m + 1) * SUB, :]
        low = jnp.broadcast_to(lo[m : m + 1, :], (SUB, rows))
        parts += [jnp.where(low == level, value, 0.0) for level in range(LO)]
    if with_counts:
        low_level = lax.broadcasted_iota(jnp.int32, (MARKS, rows), 0)
        parts += [jnp.where(low_level == lo[m : m + 1, :], 1.0, 0.0) for m in pack]
    marked = jnp.concatenate(parts, axis=0).astype(BF16)
    return mm(marked, hi_table(hi, pack), NT) if table is None else mm(marked, table)


def pack_layout(owned, with_counts):
    packs = len(packs_of(owned))
    base, height = packs * LO * SUB, packs * MARKS
    return base, height, base + (-(-height // 16) * 16 if with_counts else 0)


def write_sums(sums, counts, owned, out_ref):
    base, height, total = pack_layout(owned, counts is not None)
    out_ref[:base, :] = sums.astype(BF16)
    if counts is not None:
        above = jnp.floor(counts * (1.0 / 256.0))
        below = counts - above * 256.0
        pieces = []
        for at in range(0, height, MARKS):
            pieces.append(jnp.concatenate([above[at : at + LO], below[at : at + LO]], axis=0))
        if total > base + height:
            pieces.append(jnp.zeros((total - base - height, LANES), F32))
        out_ref[base:, :] = jnp.concatenate(pieces, axis=0).astype(BF16)


def pack_diagonals(totals, owned, with_counts):
    block = LO * SUB
    sums, counts = [], []
    for total, pack in zip(totals, packs_of(owned)):
        size = len(pack)
        sums.append(diagonal(total[: size * block], block))
        if with_counts:
            counts.append(diagonal(total[size * block :], MARKS))
    return jnp.concatenate(sums, axis=0), jnp.concatenate(counts, axis=0) if with_counts else None


def tree(values):
    while len(values) > 1:
        values = [values[i] + values[i + 1] for i in range(0, len(values), 2)]
    return values[0]


def merge_parts(parts, owned, with_counts):
    base, height, unused = pack_layout(owned, with_counts)
    whole = tree([ref[...].astype(F32) for ref in parts])
    if not with_counts:
        return whole, None
    counts = []
    for at in range(base, base + height, MARKS):
        count = whole[at : at + LO] * 256.0 + whole[at + LO : at + MARKS]
        counts.append(jnp.concatenate([count, jnp.zeros((MARKS - LO, LANES), F32)], axis=0))
    return whole[:base], jnp.concatenate(counts, axis=0)


def code_rows(rows):
    return rows // LANES * 16


def write_codes(codes, out_ref, at):
    owned, rows = codes.shape
    filled = jnp.concatenate([codes, jnp.zeros((16 - owned, rows), F32)], axis=0).astype(BF16)
    for c in range(rows // LANES):
        out_ref[at + 16 * c : at + 16 * c + 16, :] = filled[:, LANES * c : LANES * (c + 1)]


def local_sums_kernel(size, place_ref, rotation_ref, codes_ref, residual_ref, *refs):
    outs, turned, staged = refs[:2], refs[2], refs[3]
    subspaces = codes_ref.shape[0]
    owned = subspaces // size
    base = pack_layout(owned, True)[2]
    rotated = mm(residual_ref[...], rotation_ref[...].astype(BF16)).astype(BF16).astype(F32)
    turned[...] = rotated.T
    for j in range(size):
        staged[j, :owned, :] = codes_ref[j * owned : (j + 1) * owned, :]
    for k in range(size):
        other = place_ref[0] ^ k
        codes = staged[other][:owned]
        value = turned[pl.ds(pl.multiple_of(other * (owned * SUB), 8), owned * SUB), :]
        totals = [pack_sums(value, codes, pack, True) for pack in packs_of(owned)]
        sums, counts = pack_diagonals(totals, owned, True)
        slot = outs[k % 2].at[k // 2]
        write_sums(sums, counts, owned, slot.at[:base])
        write_codes(codes.astype(F32), slot, base)


def local_sums_call(place, rotation, codes, residual, size):
    subspaces, rows = codes.shape
    owned = subspaces // size
    height = -(-owned // 8) * 8
    shape = jax.ShapeDtypeStruct((size // 2, pack_layout(owned, True)[2] + code_rows(rows), LANES), BF16)
    return pl.pallas_call(
        functools.partial(local_sums_kernel, size),
        out_shape=(shape,) * 2,
        in_specs=[smem_spec()] + [vmem_spec()] * 3,
        out_specs=(vmem_spec(),) * 2,
        scratch_shapes=[pltpu.VMEM((rotation.shape[1], rows), F32), pltpu.VMEM((size, height, rows), jnp.int32)],
        compiler_params=params(rotation),
        cost_estimate=cost(0),
        name="local_sums",
    )(place, rotation, codes, residual)


def merge_cores_kernel(owned, even_ref, came_ref, *outs):
    base = pack_layout(owned, True)[2]
    length = even_ref.shape[1] - base
    for i, out_ref in enumerate(outs):
        sums, counts = merge_parts([even_ref.at[i], came_ref.at[i]], owned, True)
        write_sums(sums, counts, owned, out_ref.at[:base])
        out_ref[base : base + length, :] = even_ref[i, base:, :]
        out_ref[base + length :, :] = came_ref[i, base:, :]


def merge_cores_call(even, came, owned):
    slots, height, lanes = even.shape
    shape = jax.ShapeDtypeStruct((2 * height - pack_layout(owned, True)[2], lanes), BF16)
    return pl.pallas_call(
        functools.partial(merge_cores_kernel, owned),
        out_shape=(shape,) * slots,
        in_specs=[vmem_spec()] * 2,
        out_specs=(vmem_spec(),) * slots,
        compiler_params=params(),
        cost_estimate=cost(0),
        name="merge_cores",
    )(even, came)


def merge_chips_kernel(owned, *refs):
    parts, (out_ref, codes_ref) = refs[:-2], refs[-2:]
    base = pack_layout(owned, True)[2]
    sums, counts = merge_parts(parts, owned, True)
    write_sums(sums, counts, owned, out_ref)
    length = (parts[0].shape[0] - base) // 2
    for i, part in enumerate(parts):
        for core in range(2):
            for c in range(length // 16):
                at = base + core * length + 16 * c
                piece = part[at : at + 16, :].astype(F32)
                codes_ref[2 * i + core, :, LANES * c : LANES * (c + 1)] = piece[:owned].astype(jnp.int32)


def merge_chips_call(parts, owned, rows):
    size = 2 * len(parts)
    return pl.pallas_call(
        functools.partial(merge_chips_kernel, owned),
        out_shape=(
            jax.ShapeDtypeStruct((pack_layout(owned, True)[2], LANES), BF16),
            jax.ShapeDtypeStruct((size, owned, rows), jnp.int32),
        ),
        in_specs=[vmem_spec()] * len(parts),
        out_specs=(vmem_spec(),) * 2,
        compiler_params=params(),
        cost_estimate=cost(0),
        name="merge_chips",
    )(*parts)


def merge_kernel(owned, first_ref, second_ref, out_ref):
    sums, counts = merge_parts([first_ref, second_ref], owned, True)
    write_sums(sums, counts, owned, out_ref)


def merge_call(first, second, owned):
    return pl.pallas_call(
        functools.partial(merge_kernel, owned),
        out_shape=jax.ShapeDtypeStruct(first.shape, BF16),
        in_specs=[vmem_spec()] * 2,
        out_specs=vmem_spec(),
        compiler_params=params(),
        cost_estimate=cost(0),
        name="merge_groups",
    )(first, second)


def spans_of(held):
    peers = [k for even in held if even % 2 == 0 for k in (even, even ^ 1)]
    return [tuple(peers[i : i + SPAN]) for i in range(0, len(peers), SPAN)]


def span_codes(codes_ref, span):
    return jnp.concatenate([codes_ref[k] for k in span], axis=1)


def span_rows(pieces, span):
    return jnp.concatenate([ref[...] for k in span for ref in pieces[k]], axis=0)


def pieces_of(held, refs):
    at = 0
    pieces = {}
    for k, count in held.items():
        pieces[k] = refs[at : at + count]
        at += count
    return pieces


def read_books(sums, counts_in, owned):
    everything, counts = merge_parts(sums, owned, counts_in is None)
    if counts is None:
        counts = counts_in[...]
    block = LO * SUB
    books = []
    for g in range(len(packs_of(owned))):
        rows = []
        for level in range(LO):
            at = g * block + level * SUB
            rows.append(everything[at : at + SUB] / (counts[g * MARKS + level : g * MARKS + level + 1] + 1.0))
        books.append(jnp.concatenate(rows, axis=0))
    return books, counts


def widen(books, owned):
    owner = lane_owner(LO * SUB)
    return [
        jnp.concatenate([jnp.where(owner == i, book, 0.0) for i in range(len(pack))], axis=0).astype(BF16)
        for book, pack in zip(books, packs_of(owned))
    ]


def add_spans(total, wide, codes_ref, pieces, spans, tables=None):
    owned = codes_ref.shape[1]
    for i, span in enumerate(spans):
        codes = span_codes(codes_ref, span)
        hi, lo = split(codes)
        rows = codes.shape[1]
        rebuilt = []
        for g, pack in enumerate(packs_of(owned)):
            table = hi_table(hi, pack) if tables is None else tables[i, g * LANES : (g + 1) * LANES, :]
            spread = mm(wide[g], table)
            for j, m in enumerate(pack):
                low = jnp.broadcast_to(lo[m : m + 1, :], (SUB, rows))
                at = j * LO * SUB
                value = spread[at : at + SUB]
                for level in range(1, LO):
                    value = jnp.where(low == level, spread[at + level * SUB : at + (level + 1) * SUB], value)
                rebuilt.append(value)
        part = mm(jnp.concatenate(rebuilt, axis=0).astype(BF16), span_rows(pieces, span))
        total = part if total is None else total + part
    return total


def flat(chunks):
    return {k: len(c) for k, c in chunks.items()}, [piece for c in chunks.values() for piece in c]


def cross_near_kernel(held, groups, codes_ref, *refs):
    sums, pieces, outs = refs[:groups], pieces_of(held, refs[groups:]), refs[groups + sum(held.values()) :]
    total_ref, wide_ref, counts_ref = outs
    owned = codes_ref.shape[1]
    books, counts = read_books(sums, None, owned)
    counts_ref[...] = counts
    wide = widen(books, owned)
    for g, one in enumerate(wide):
        wide_ref[g, : one.shape[0], :] = one
    total_ref[...] = add_spans(None, wide, codes_ref, pieces, spans_of(held))


def cross_near_call(codes, sums, chunks):
    owned = codes.shape[1]
    packs = len(packs_of(owned))
    held, rows = flat(chunks)
    return pl.pallas_call(
        functools.partial(cross_near_kernel, held, len(sums)),
        out_shape=(
            jax.ShapeDtypeStruct((owned * SUB, rows[0].shape[1]), F32),
            jax.ShapeDtypeStruct((packs, PACK * LO * SUB, LANES), BF16),
            jax.ShapeDtypeStruct((packs * MARKS, LANES), F32),
        ),
        in_specs=[vmem_spec()] * (1 + len(sums) + len(rows)),
        out_specs=(vmem_spec(),) * 3,
        compiler_params=params(*rows),
        cost_estimate=cost(0),
        name="cross_near",
    )(codes, *sums, *rows)


def cross_far_kernel(held, total_rows, codes_ref, total_ref, wide_ref, *refs):
    pieces, cross_ref = pieces_of(held, refs), refs[-1]
    packs = packs_of(codes_ref.shape[1])
    wide = [wide_ref[g, : len(pack) * LO * SUB, :] for g, pack in enumerate(packs)]
    total = add_spans(total_ref[...], wide, codes_ref, pieces, spans_of(held))
    cross_ref[...] = (total * (1.0 / total_rows)).astype(BF16)


def cross_far_call(codes, total, wide, chunks, total_rows):
    held, rows = flat(chunks)
    return pl.pallas_call(
        functools.partial(cross_far_kernel, held, total_rows),
        out_shape=jax.ShapeDtypeStruct(total.shape, BF16),
        in_specs=[vmem_spec()] * (3 + len(rows)),
        out_specs=vmem_spec(),
        compiler_params=params(*rows),
        cost_estimate=cost(0),
        name="cross_far",
    )(codes, total, wide, *rows)


def cross_kernel(held, groups, total_rows, ready, codes_ref, *refs):
    tables, refs = (refs[0], refs[1:]) if ready else (None, refs)
    sums, counts_in, pieces = refs[:groups], refs[groups], pieces_of(held, refs[groups + 1 :])
    cross_ref, book_ref = refs[-2:]
    owned = codes_ref.shape[1]
    block = LO * SUB
    books, unused = read_books(sums, counts_in, owned)
    for g, book in enumerate(books):
        book_ref[g * block : (g + 1) * block, :] = book
    total = add_spans(None, widen(books, owned), codes_ref, pieces, spans_of(held), tables)
    cross_ref[...] = (total * (1.0 / total_rows)).astype(BF16)


def cross_call(codes, ready, sums, counts, chunks, total_rows):
    owned = codes.shape[1]
    held, rows = flat(chunks)
    tables = [ready[2]] if ready else []
    return pl.pallas_call(
        functools.partial(cross_kernel, held, len(sums), total_rows, bool(ready)),
        out_shape=(
            jax.ShapeDtypeStruct((owned * SUB, rows[0].shape[1]), BF16),
            jax.ShapeDtypeStruct((len(packs_of(owned)) * LO * SUB, LANES), F32),
        ),
        in_specs=[vmem_spec()] * (2 + len(tables) + len(sums) + len(rows)),
        out_specs=(vmem_spec(), vmem_spec()),
        compiler_params=params(*rows, *tables),
        cost_estimate=cost(0),
        name="cross",
    )(codes, *tables, *sums, counts, *rows)


def turn_kernel(held, *refs):
    pieces, turned_ref = pieces_of(held, refs), refs[-1]
    for i, span in enumerate(spans_of(held)):
        turned_ref[i, :, :] = span_rows(pieces, span).T


def tables_kernel(spans, codes_ref, table_ref, across_ref):
    packs = packs_of(codes_ref.shape[1])
    for i, span in enumerate(spans):
        hi = split(span_codes(codes_ref, span))[0]
        for g, pack in enumerate(packs):
            table = hi_table(hi, pack)
            across_ref[i, g * LANES : (g + 1) * LANES, :] = table
            table_ref[i, :, g * LANES : (g + 1) * LANES] = table.T


def prepare_call(codes, chunks, after_codes, after_rows):
    size, owned, rows = codes.shape
    held, pieces = flat(chunks)
    lanes = LANES * len(packs_of(owned))
    width = pieces[0].shape[1]
    spans = spans_of(held)
    each = len(spans[0]) * rows
    turned = jax.ShapeDtypeStruct((len(spans), width, each), BF16)
    tables = (
        jax.ShapeDtypeStruct((len(spans), each, lanes), BF16),
        jax.ShapeDtypeStruct((len(spans), lanes, each), BF16),
    )
    if sum(math.prod(a.shape) * 2 for a in (turned, *tables)) > 20 * MIB:
        return None
    rows_turned = pl.pallas_call(
        functools.partial(turn_kernel, held),
        out_shape=turned,
        in_specs=[vmem_spec()] * len(pieces),
        out_specs=vmem_spec(),
        compiler_params=params(turned),
        cost_estimate=cost(0),
        name="turn_rows",
    )(after(pieces[0], *after_rows), *pieces[1:])
    two = pl.pallas_call(
        functools.partial(tables_kernel, spans),
        out_shape=tables,
        in_specs=[vmem_spec()],
        out_specs=(vmem_spec(),) * 2,
        compiler_params=params(*tables),
        cost_estimate=cost(0),
        name="tables",
    )(after(codes, *after_codes))
    return (rows_turned, *two)


def bands(x):
    return [x[i : i + BAND] for i in range(0, x.shape[0], BAND)]


def first_step(xb):
    steps = []
    square = None
    for band in bands(xb):
        gram = mm(band, xb, NT)
        part = jnp.sum(gram * gram, keepdims=True)
        square = part if square is None else square + part
        steps.append(mm(gram.astype(BF16), xb))
    norm_square = jnp.sqrt(square + EPSILON)
    scale = lax.rsqrt(norm_square)
    less = 0.5 * scale / norm_square
    return [(1.5 * scale) * band.astype(F32) - less * step for band, step in zip(bands(xb), steps)]


def join(parts):
    if parts[0].shape[0] % 16 == 0:
        return jnp.concatenate(parts, axis=0)
    return jnp.concatenate([p.astype(F32) for p in parts], axis=0).astype(BF16)


def next_sums_kernel(held, ready, codes_ref, *refs):
    size = len(held)
    parts, out_ref = refs[:size], refs[-1]
    if ready:
        turned_ref, table_ref = refs[size : size + 2]
    else:
        pieces = pieces_of(held, refs[size:])
    owned = codes_ref.shape[1]
    height = parts[0].shape[0]
    x = first_step(join([ref[...] for ref in parts]))
    xb = jnp.concatenate([band.astype(BF16) for band in x], axis=0)
    mine = x[0][:height]
    gram = mm(mine.astype(BF16), xb, NT)
    rotation_rows = (1.5 * mine - 0.5 * mm(gram.astype(BF16), xb)).astype(BF16)
    totals = None
    for i, span in enumerate(spans_of(held)):
        if ready:
            rotated = mm(rotation_rows, turned_ref[i])
        else:
            rotated = mm(rotation_rows, span_rows(pieces, span), NT)
        rotated = rotated.astype(BF16).astype(F32)
        codes = span_codes(codes_ref, span)
        more = []
        for g, pack in enumerate(packs_of(owned)):
            table = table_ref[i, :, g * LANES : (g + 1) * LANES] if ready else None
            more.append(pack_sums(rotated, codes, pack, False, table))
        totals = more if totals is None else [a + b for a, b in zip(totals, more)]
    write_sums(pack_diagonals(totals, owned, False)[0], None, owned, out_ref)


def next_sums_call(codes, ready, blocks, chunks):
    owned = codes.shape[1]
    held, rows = flat(chunks)
    given = list(ready[:2]) if ready else rows
    return pl.pallas_call(
        functools.partial(next_sums_kernel, held, bool(ready)),
        out_shape=jax.ShapeDtypeStruct((pack_layout(owned, False)[2], LANES), BF16),
        in_specs=[vmem_spec()] * (1 + len(blocks) + len(given)),
        out_specs=vmem_spec(),
        compiler_params=params(*given),
        cost_estimate=cost(0),
        name="next_sums",
    )(codes, *blocks, *given)


def final_kernel(size, place_ref, residual_ref, *refs):
    parts, out_ref, whole = refs[:size], refs[size], refs[size + 1]
    height = parts[0].shape[0]
    for k, ref in enumerate(parts):
        at = pl.multiple_of((place_ref[0] ^ k) * height, 16 if whole.dtype == BF16 else 8)
        whole[pl.ds(at, height), :] = ref[...].astype(whole.dtype)
    x = first_step(whole[...].astype(BF16))
    xb = jnp.concatenate([band.astype(BF16) for band in x], axis=0)
    once = mm(residual_ref[...], xb, NT)
    less = mm(mm(once.astype(BF16), xb).astype(BF16), xb, NT)
    out_ref[...] = (1.5 * once - 0.5 * less).astype(BF16)


def final_call(place, residual, blocks):
    rows, width = residual.shape
    kind = BF16 if blocks[0].shape[0] % 16 == 0 else F32
    return pl.pallas_call(
        functools.partial(final_kernel, len(blocks)),
        out_shape=jax.ShapeDtypeStruct((rows, width), BF16),
        in_specs=[smem_spec()] + [vmem_spec()] * (1 + len(blocks)),
        out_specs=vmem_spec(),
        scratch_shapes=[pltpu.VMEM((width, width), kind)],
        compiler_params=params(),
        cost_estimate=cost(0),
        name="final",
    )(place, residual, *blocks)


def after(x, *first):
    return lax.optimization_barrier((x,) + first)[0]


def near_rows(rows, size):
    return {1 << b: swap(rows, "within", size, 1 << b) for b in range(1, size.bit_length() - 1)}


def far_rows(rows, near, size):
    bits = list(near)
    half = rows.shape[0] // 2
    halves = []
    for order, cut in ((bits, slice(0, half)), (bits[::-1], slice(half, None))):
        here = {0: rows, order[0]: near[order[0]][cut]}
        for bit in order[1:]:
            for k in list(here):
                here[k ^ bit] = swap(here[k], "within", size, bit) if k else near[bit][cut]
        halves.append(here)
    return {k: (halves[0][k], halves[1][k]) for k in halves[0] if k and k not in near}


def both_cores(whole, size):
    return {k ^ 1: tuple(swap(piece, "within", size, 1) for piece in pieces) for k, pieces in whole.items()}


def gather_group(x, size):
    blocks = {k: swap(x, "within", size, k) if k else x for k in range(0, size, 2)}
    for k in list(blocks):
        blocks[k ^ 1] = swap(blocks[k], "within", size, 1)
    return [blocks[k] for k in range(size)]


def scatter_sums(merged, owned, rows, size):
    parts = [merged[0]] + [swap(merged[k // 2], "within", size, k) for k in range(2, size, 2)]
    return merge_chips_call(parts, owned, rows)


def direct(x, size):
    return [x] + [swap(x, "group", size, k) for k in range(1, size)]


def reduce_cross(cross, size, last):
    bits = [1 << b for b in range(size.bit_length() - 1)]
    for bit in bits:
        if bit == bits[-1]:
            cross = after(cross, *last)
        cross = (cross.astype(F32) + swap(cross, "group", size, bit).astype(F32)).astype(BF16)
    return cross


def per_device(vectors, centroids, list_ids, codes, rotation):
    groups = lax.axis_size("group")
    size = lax.axis_size("within")
    rows, width = vectors.shape
    owned = codes.shape[1] // size
    total_rows = rows * size * groups
    place = lax.axis_index("within").astype(jnp.int32).reshape(1)
    residual = residual_call(vectors, centroids, list_ids)
    near = near_rows(residual, size)
    twin = swap(residual, "within", size, 1)
    even, odd = local_sums_call(place, rotation, codes.T, after(residual, twin), size)
    merged = merge_cores_call(even, swap(odd, "within", size, 1), owned)
    sums, own_codes = scatter_sums(merged, owned, rows, size)
    far = far_rows(residual, near, size)
    near = {k: after(rows_near, sums) for k, rows_near in near.items()}
    for bit in [1 << b for b in range(groups.bit_length() - 2)]:
        sums = merge_call(sums, swap(sums, "group", groups, bit), owned)
    parts = [sums, swap(sums, "group", groups, groups // 2)]
    chunks = {0: (residual,), 1: (twin,)}
    for k, rows_near in near.items():
        chunks[k] = (rows_near,)
        chunks[k ^ 1] = (swap(rows_near, "within", size, 1),)
    total, wide, counts = cross_near_call(own_codes, parts, chunks)
    far = {k: tuple(after(piece, parts[1]) for piece in pieces) for k, pieces in far.items()}
    far = {**far, **both_cores(far, size)}
    cross = cross_far_call(own_codes, total, wide, far, total_rows)
    chunks.update(far)
    ready = prepare_call(own_codes, chunks, (cross,), (cross,))
    for alternation in range(1, ALTS):
        block = reduce_cross(cross, groups, ready[:1] if ready else ())
        if ready:
            block = after(block, *ready)
        parts = direct(next_sums_call(own_codes, ready, gather_group(block, size), chunks), groups)
        cross, book = cross_call(own_codes, ready, parts, counts, chunks, total_rows)
    packs = len(packs_of(owned))
    book = book.reshape(packs, LO * SUB, PACK, HI).transpose(0, 2, 3, 1).reshape(packs * PACK, K * SUB)[:owned]
    blocks = gather_group(reduce_cross(cross, groups, (book,)), size)
    rotated_out = final_call(place, residual, blocks)
    return (rotated_out, book)


def solution(mesh):
    in_specs = (
        P(("group", "within"), None),
        P(("group", "within"), None),
        P(("group", "within")),
        P(("group", "within"), None),
        P(),
    )
    out_specs = (P(("group", "within"), None), P("within", None))
    return jax.shard_map(per_device, mesh=mesh, in_specs=in_specs, out_specs=out_specs, check_vma=False)
```

```python
import functools
import math

import jax
import jax.numpy as jnp
from jax import lax
from jax.experimental import pallas as pl
from jax.experimental.pallas import tpu as pltpu
from jax.sharding import PartitionSpec as P

K = 256
ALTS = 2
LO = 4
HI = K // LO
SUB = 8
LANES = 256
PACK = LANES // HI
MARKS = 8
SPAN = 2
EPSILON = 1e-06
MIB = 1024 * 1024

F32 = jnp.float32
BF16 = jnp.bfloat16
NT = (((1,), (1,)), ((), ()))
NN = (((1,), (0,)), ((), ()))
TN = (((0,), (0,)), ((), ()))


def mm(a, b, dims=NN):
    return lax.dot_general(a, b, dims, preferred_element_type=F32)


def vmem_spec():
    return pl.BlockSpec(memory_space=pltpu.VMEM)


def smem_spec():
    return pl.BlockSpec(memory_space=pltpu.SMEM)


def cost(us):
    return pl.CostEstimate(flops=int(us * 1e9), bytes_accessed=0, transcendentals=0)


def params(*arrays):
    held = sum(math.prod(a.shape) * a.dtype.itemsize for a in arrays)
    return pltpu.CompilerParams(vmem_limit_bytes=held + 12 * MIB)


def swap(x, axis, size, bits):
    return lax.ppermute(x, axis, [(i, i ^ bits) for i in range(size)])


def levels_kernel(out_ref):
    out_ref[...] = lax.broadcasted_iota(jnp.int32, out_ref.shape, 0)


def pick_kernel(lists, ids_ref, levels_ref, table_ref):
    local = lax.rem(ids_ref[...], lists)
    table_ref[...] = jnp.where(levels_ref[...] == local, 1.0, 0.0).astype(BF16)


def pick_call(ids, lists):
    rows = ids.shape[0]
    levels = pl.pallas_call(
        levels_kernel,
        out_shape=jax.ShapeDtypeStruct((lists, rows), jnp.int32),
        out_specs=vmem_spec(),
        compiler_params=params(),
        cost_estimate=cost(10),
        name="levels",
    )()
    return pl.pallas_call(
        functools.partial(pick_kernel, lists),
        out_shape=jax.ShapeDtypeStruct((lists, rows), BF16),
        in_specs=[vmem_spec()] * 2,
        out_specs=vmem_spec(),
        compiler_params=params(),
        cost_estimate=cost(0),
        name="pick",
    )(ids.reshape(1, rows), levels)


def residual_kernel(vectors_ref, centroids_ref, table_ref, out_ref):
    table = table_ref[...]
    center = centroids_ref[...]
    first = center.astype(BF16)
    rest = center - first.astype(F32)
    second = rest.astype(BF16)
    third = (rest - second.astype(F32)).astype(BF16)
    picked = mm(table, first, TN) + mm(table, second, TN) + mm(table, third, TN)
    out_ref[...] = (vectors_ref[...].astype(F32) - picked).astype(BF16)


def residual_call(vectors, centroids, ids):
    return pl.pallas_call(
        residual_kernel,
        out_shape=jax.ShapeDtypeStruct(vectors.shape, BF16),
        in_specs=[vmem_spec()] * 3,
        out_specs=vmem_spec(),
        compiler_params=params(),
        cost_estimate=cost(10),
        name="residual",
    )(vectors, centroids, pick_call(ids, centroids.shape[0]))


def split(codes):
    return codes >> 2, codes & 3


def packs_of(owned):
    return [range(first, min(first + PACK, owned)) for first in range(0, owned, PACK)]


def hi_table(hi, pack):
    rows = hi.shape[1]
    level = lax.broadcasted_iota(jnp.int32, (HI, rows), 0)
    parts = [jnp.where(level == hi[m : m + 1, :], 1.0, 0.0) for m in pack]
    parts += [jnp.zeros((HI, rows), F32)] * (PACK - len(pack))
    return jnp.concatenate(parts, axis=0).astype(BF16)


def lane_owner(rows):
    return lax.broadcasted_iota(jnp.int32, (rows, LANES), 1) // HI


def diagonal(wide, block):
    owner = lane_owner(block)
    total = jnp.zeros((block, LANES), F32)
    for i in range(wide.shape[0] // block):
        total = jnp.where(owner == i, wide[i * block : (i + 1) * block, :], total)
    return total


def pack_sums(rotated, codes, pack, with_counts, table=None):
    rows = codes.shape[1]
    hi, lo = split(codes)
    parts = []
    for m in pack:
        value = rotated[m * SUB : (m + 1) * SUB, :]
        low = jnp.broadcast_to(lo[m : m + 1, :], (SUB, rows))
        parts += [jnp.where(low == level, value, 0.0) for level in range(LO)]
    if with_counts:
        low_level = lax.broadcasted_iota(jnp.int32, (MARKS, rows), 0)
        parts += [jnp.where(low_level == lo[m : m + 1, :], 1.0, 0.0) for m in pack]
    marked = jnp.concatenate(parts, axis=0).astype(BF16)
    return mm(marked, hi_table(hi, pack), NT) if table is None else mm(marked, table)


def pack_layout(owned, with_counts):
    packs = len(packs_of(owned))
    base, height = packs * LO * SUB, packs * MARKS
    return base, height, base + (-(-height // 16) * 16 if with_counts else 0)


def write_sums(sums, counts, owned, out_ref):
    base, height, total = pack_layout(owned, counts is not None)
    out_ref[:base, :] = sums.astype(BF16)
    if counts is not None:
        above = jnp.floor(counts * (1.0 / 256.0))
        below = counts - above * 256.0
        pieces = []
        for at in range(0, height, MARKS):
            pieces.append(jnp.concatenate([above[at : at + LO], below[at : at + LO]], axis=0))
        if total > base + height:
            pieces.append(jnp.zeros((total - base - height, LANES), F32))
        out_ref[base:, :] = jnp.concatenate(pieces, axis=0).astype(BF16)


def pack_diagonals(totals, owned, with_counts):
    block = LO * SUB
    sums, counts = [], []
    for total, pack in zip(totals, packs_of(owned)):
        size = len(pack)
        sums.append(diagonal(total[: size * block], block))
        if with_counts:
            counts.append(diagonal(total[size * block :], MARKS))
    return jnp.concatenate(sums, axis=0), jnp.concatenate(counts, axis=0) if with_counts else None


def tree(values):
    while len(values) > 1:
        values = [values[i] + values[i + 1] for i in range(0, len(values), 2)]
    return values[0]


def merge_parts(parts, owned, with_counts):
    base, height, unused = pack_layout(owned, with_counts)
    whole = tree([ref[...].astype(F32) for ref in parts])
    if not with_counts:
        return whole, None
    counts = []
    for at in range(base, base + height, MARKS):
        count = whole[at : at + LO] * 256.0 + whole[at + LO : at + MARKS]
        counts.append(jnp.concatenate([count, jnp.zeros((MARKS - LO, LANES), F32)], axis=0))
    return whole[:base], jnp.concatenate(counts, axis=0)


def code_rows(rows):
    return rows // LANES * 16


def write_codes(codes, out_ref, at):
    owned, rows = codes.shape
    filled = jnp.concatenate([codes, jnp.zeros((16 - owned, rows), F32)], axis=0).astype(BF16)
    for c in range(rows // LANES):
        out_ref[at + 16 * c : at + 16 * c + 16, :] = filled[:, LANES * c : LANES * (c + 1)]


def local_sums_kernel(size, place_ref, rotation_ref, codes_ref, residual_ref, *refs):
    outs, turned, staged = refs[:2], refs[2], refs[3]
    subspaces = codes_ref.shape[0]
    owned = subspaces // size
    base = pack_layout(owned, True)[2]
    rotated = mm(residual_ref[...], rotation_ref[...].astype(BF16)).astype(BF16).astype(F32)
    turned[...] = rotated.T
    for j in range(size):
        staged[j, :owned, :] = codes_ref[j * owned : (j + 1) * owned, :]
    for k in range(size):
        other = place_ref[0] ^ k
        codes = staged[other][:owned]
        value = turned[pl.ds(pl.multiple_of(other * (owned * SUB), 8), owned * SUB), :]
        totals = [pack_sums(value, codes, pack, True) for pack in packs_of(owned)]
        sums, counts = pack_diagonals(totals, owned, True)
        slot = outs[k % 2].at[k // 2]
        write_sums(sums, counts, owned, slot.at[:base])
        write_codes(codes.astype(F32), slot, base)


def local_sums_call(place, rotation, codes, residual, size):
    subspaces, rows = codes.shape
    owned = subspaces // size
    height = -(-owned // 8) * 8
    shape = jax.ShapeDtypeStruct((size // 2, pack_layout(owned, True)[2] + code_rows(rows), LANES), BF16)
    return pl.pallas_call(
        functools.partial(local_sums_kernel, size),
        out_shape=(shape,) * 2,
        in_specs=[smem_spec()] + [vmem_spec()] * 3,
        out_specs=(vmem_spec(),) * 2,
        scratch_shapes=[pltpu.VMEM((rotation.shape[1], rows), F32), pltpu.VMEM((size, height, rows), jnp.int32)],
        compiler_params=params(rotation),
        cost_estimate=cost(0),
        name="local_sums",
    )(place, rotation, codes, residual)


def merge_cores_kernel(owned, even_ref, came_ref, *outs):
    base = pack_layout(owned, True)[2]
    length = even_ref.shape[1] - base
    for i, out_ref in enumerate(outs):
        sums, counts = merge_parts([even_ref.at[i], came_ref.at[i]], owned, True)
        write_sums(sums, counts, owned, out_ref.at[:base])
        out_ref[base : base + length, :] = even_ref[i, base:, :]
        out_ref[base + length :, :] = came_ref[i, base:, :]


def merge_cores_call(even, came, owned):
    slots, height, lanes = even.shape
    shape = jax.ShapeDtypeStruct((2 * height - pack_layout(owned, True)[2], lanes), BF16)
    return pl.pallas_call(
        functools.partial(merge_cores_kernel, owned),
        out_shape=(shape,) * slots,
        in_specs=[vmem_spec()] * 2,
        out_specs=(vmem_spec(),) * slots,
        compiler_params=params(),
        cost_estimate=cost(0),
        name="merge_cores",
    )(even, came)


def merge_chips_kernel(owned, *refs):
    parts, (out_ref, codes_ref) = refs[:-2], refs[-2:]
    base = pack_layout(owned, True)[2]
    sums, counts = merge_parts(parts, owned, True)
    write_sums(sums, counts, owned, out_ref)
    length = (parts[0].shape[0] - base) // 2
    for i, part in enumerate(parts):
        for core in range(2):
            for c in range(length // 16):
                at = base + core * length + 16 * c
                piece = part[at : at + 16, :].astype(F32)
                codes_ref[2 * i + core, :, LANES * c : LANES * (c + 1)] = piece[:owned].astype(jnp.int32)


def merge_chips_call(parts, owned, rows):
    size = 2 * len(parts)
    return pl.pallas_call(
        functools.partial(merge_chips_kernel, owned),
        out_shape=(
            jax.ShapeDtypeStruct((pack_layout(owned, True)[2], LANES), BF16),
            jax.ShapeDtypeStruct((size, owned, rows), jnp.int32),
        ),
        in_specs=[vmem_spec()] * len(parts),
        out_specs=(vmem_spec(),) * 2,
        compiler_params=params(),
        cost_estimate=cost(0),
        name="merge_chips",
    )(*parts)


def merge_kernel(owned, first_ref, second_ref, out_ref):
    sums, counts = merge_parts([first_ref, second_ref], owned, True)
    write_sums(sums, counts, owned, out_ref)


def merge_call(first, second, owned):
    return pl.pallas_call(
        functools.partial(merge_kernel, owned),
        out_shape=jax.ShapeDtypeStruct(first.shape, BF16),
        in_specs=[vmem_spec()] * 2,
        out_specs=vmem_spec(),
        compiler_params=params(),
        cost_estimate=cost(0),
        name="merge_groups",
    )(first, second)


def spans_of(held):
    peers = [k for even in held if even % 2 == 0 for k in (even, even ^ 1)]
    return [tuple(peers[i : i + SPAN]) for i in range(0, len(peers), SPAN)]


def span_codes(codes_ref, span):
    return jnp.concatenate([codes_ref[k] for k in span], axis=1)


def span_rows(pieces, span):
    return jnp.concatenate([ref[...] for k in span for ref in pieces[k]], axis=0)


def pieces_of(held, refs):
    at = 0
    pieces = {}
    for k, count in held.items():
        pieces[k] = refs[at : at + count]
        at += count
    return pieces


def read_books(sums, counts_in, owned):
    everything, counts = merge_parts(sums, owned, counts_in is None)
    if counts is None:
        counts = counts_in[...]
    block = LO * SUB
    books = []
    for g in range(len(packs_of(owned))):
        rows = []
        for level in range(LO):
            at = g * block + level * SUB
            rows.append(everything[at : at + SUB] / (counts[g * MARKS + level : g * MARKS + level + 1] + 1.0))
        books.append(jnp.concatenate(rows, axis=0))
    return books, counts


def widen(books, owned):
    owner = lane_owner(LO * SUB)
    return [
        jnp.concatenate([jnp.where(owner == i, book, 0.0) for i in range(len(pack))], axis=0).astype(BF16)
        for book, pack in zip(books, packs_of(owned))
    ]


def add_spans(total, wide, codes_ref, pieces, spans, tables=None):
    owned = codes_ref.shape[1]
    for i, span in enumerate(spans):
        codes = span_codes(codes_ref, span)
        hi, lo = split(codes)
        rows = codes.shape[1]
        rebuilt = []
        for g, pack in enumerate(packs_of(owned)):
            table = hi_table(hi, pack) if tables is None else tables[i, g * LANES : (g + 1) * LANES, :]
            spread = mm(wide[g], table)
            for j, m in enumerate(pack):
                low = jnp.broadcast_to(lo[m : m + 1, :], (SUB, rows))
                at = j * LO * SUB
                value = spread[at : at + SUB]
                for level in range(1, LO):
                    value = jnp.where(low == level, spread[at + level * SUB : at + (level + 1) * SUB], value)
                rebuilt.append(value)
        part = mm(jnp.concatenate(rebuilt, axis=0).astype(BF16), span_rows(pieces, span))
        total = part if total is None else total + part
    return total


def flat(chunks):
    return {k: len(c) for k, c in chunks.items()}, [piece for c in chunks.values() for piece in c]


def cross_near_kernel(held, groups, codes_ref, *refs):
    sums, pieces, outs = refs[:groups], pieces_of(held, refs[groups:]), refs[groups + sum(held.values()) :]
    total_ref, wide_ref, counts_ref = outs
    owned = codes_ref.shape[1]
    books, counts = read_books(sums, None, owned)
    counts_ref[...] = counts
    wide = widen(books, owned)
    for g, one in enumerate(wide):
        wide_ref[g, : one.shape[0], :] = one
    total_ref[...] = add_spans(None, wide, codes_ref, pieces, spans_of(held))


def cross_near_call(codes, sums, chunks):
    owned = codes.shape[1]
    packs = len(packs_of(owned))
    held, rows = flat(chunks)
    return pl.pallas_call(
        functools.partial(cross_near_kernel, held, len(sums)),
        out_shape=(
            jax.ShapeDtypeStruct((owned * SUB, rows[0].shape[1]), F32),
            jax.ShapeDtypeStruct((packs, PACK * LO * SUB, LANES), BF16),
            jax.ShapeDtypeStruct((packs * MARKS, LANES), F32),
        ),
        in_specs=[vmem_spec()] * (1 + len(sums) + len(rows)),
        out_specs=(vmem_spec(),) * 3,
        compiler_params=params(*rows),
        cost_estimate=cost(0),
        name="cross_near",
    )(codes, *sums, *rows)


def cross_far_kernel(held, total_rows, codes_ref, total_ref, wide_ref, *refs):
    pieces, cross_ref = pieces_of(held, refs), refs[-1]
    packs = packs_of(codes_ref.shape[1])
    wide = [wide_ref[g, : len(pack) * LO * SUB, :] for g, pack in enumerate(packs)]
    total = add_spans(total_ref[...], wide, codes_ref, pieces, spans_of(held))
    cross_ref[...] = (total * (1.0 / total_rows)).astype(BF16)


def cross_far_call(codes, total, wide, chunks, total_rows):
    held, rows = flat(chunks)
    return pl.pallas_call(
        functools.partial(cross_far_kernel, held, total_rows),
        out_shape=jax.ShapeDtypeStruct(total.shape, BF16),
        in_specs=[vmem_spec()] * (3 + len(rows)),
        out_specs=vmem_spec(),
        compiler_params=params(*rows),
        cost_estimate=cost(0),
        name="cross_far",
    )(codes, total, wide, *rows)


def cross_kernel(held, groups, total_rows, ready, codes_ref, *refs):
    tables, refs = (refs[0], refs[1:]) if ready else (None, refs)
    sums, counts_in, pieces = refs[:groups], refs[groups], pieces_of(held, refs[groups + 1 :])
    cross_ref, book_ref = refs[-2:]
    owned = codes_ref.shape[1]
    block = LO * SUB
    books, unused = read_books(sums, counts_in, owned)
    for g, book in enumerate(books):
        book_ref[g * block : (g + 1) * block, :] = book
    total = add_spans(None, widen(books, owned), codes_ref, pieces, spans_of(held), tables)
    cross_ref[...] = (total * (1.0 / total_rows)).astype(BF16)


def cross_call(codes, ready, sums, counts, chunks, total_rows):
    owned = codes.shape[1]
    held, rows = flat(chunks)
    tables = [ready[2]] if ready else []
    return pl.pallas_call(
        functools.partial(cross_kernel, held, len(sums), total_rows, bool(ready)),
        out_shape=(
            jax.ShapeDtypeStruct((owned * SUB, rows[0].shape[1]), BF16),
            jax.ShapeDtypeStruct((len(packs_of(owned)) * LO * SUB, LANES), F32),
        ),
        in_specs=[vmem_spec()] * (2 + len(tables) + len(sums) + len(rows)),
        out_specs=(vmem_spec(), vmem_spec()),
        compiler_params=params(*rows, *tables),
        cost_estimate=cost(0),
        name="cross",
    )(codes, *tables, *sums, counts, *rows)


def turn_kernel(held, *refs):
    pieces, turned_ref = pieces_of(held, refs), refs[-1]
    for i, span in enumerate(spans_of(held)):
        turned_ref[i, :, :] = span_rows(pieces, span).T


def tables_kernel(spans, codes_ref, table_ref, across_ref):
    packs = packs_of(codes_ref.shape[1])
    for i, span in enumerate(spans):
        hi = split(span_codes(codes_ref, span))[0]
        for g, pack in enumerate(packs):
            table = hi_table(hi, pack)
            across_ref[i, g * LANES : (g + 1) * LANES, :] = table
            table_ref[i, :, g * LANES : (g + 1) * LANES] = table.T


def prepare_call(codes, chunks, after_codes, after_rows):
    size, owned, rows = codes.shape
    held, pieces = flat(chunks)
    lanes = LANES * len(packs_of(owned))
    width = pieces[0].shape[1]
    spans = spans_of(held)
    each = len(spans[0]) * rows
    turned = jax.ShapeDtypeStruct((len(spans), width, each), BF16)
    tables = (
        jax.ShapeDtypeStruct((len(spans), each, lanes), BF16),
        jax.ShapeDtypeStruct((len(spans), lanes, each), BF16),
    )
    if sum(math.prod(a.shape) * 2 for a in (turned, *tables)) > 20 * MIB:
        return None
    rows_turned = pl.pallas_call(
        functools.partial(turn_kernel, held),
        out_shape=turned,
        in_specs=[vmem_spec()] * len(pieces),
        out_specs=vmem_spec(),
        compiler_params=params(turned),
        cost_estimate=cost(0),
        name="turn_rows",
    )(after(pieces[0], *after_rows), *pieces[1:])
    two = pl.pallas_call(
        functools.partial(tables_kernel, spans),
        out_shape=tables,
        in_specs=[vmem_spec()],
        out_specs=(vmem_spec(),) * 2,
        compiler_params=params(*tables),
        cost_estimate=cost(0),
        name="tables",
    )(after(codes, *after_codes))
    return (rows_turned, *two)


def first_step(xb):
    gram = mm(xb, xb, NT)
    norm_square = jnp.sqrt(jnp.sum(gram * gram, keepdims=True) + EPSILON)
    scale = lax.rsqrt(norm_square)
    step = mm(gram.astype(BF16), xb)
    return (1.5 * scale) * xb.astype(F32) - (0.5 * scale / norm_square) * step


def join(parts):
    if parts[0].shape[0] % 16 == 0:
        return jnp.concatenate(parts, axis=0)
    return jnp.concatenate([p.astype(F32) for p in parts], axis=0).astype(BF16)


def next_sums_kernel(held, ready, codes_ref, *refs):
    size = len(held)
    parts, out_ref = refs[:size], refs[-1]
    if ready:
        turned_ref, table_ref = refs[size : size + 2]
    else:
        pieces = pieces_of(held, refs[size:])
    owned = codes_ref.shape[1]
    height = parts[0].shape[0]
    x = first_step(join([ref[...] for ref in parts]))
    xb = x.astype(BF16)
    mine = x[:height]
    gram = mm(mine.astype(BF16), xb, NT)
    rotation_rows = (1.5 * mine - 0.5 * mm(gram.astype(BF16), xb)).astype(BF16)
    totals = None
    for i, span in enumerate(spans_of(held)):
        if ready:
            rotated = mm(rotation_rows, turned_ref[i])
        else:
            rotated = mm(rotation_rows, span_rows(pieces, span), NT)
        rotated = rotated.astype(BF16).astype(F32)
        codes = span_codes(codes_ref, span)
        more = []
        for g, pack in enumerate(packs_of(owned)):
            table = table_ref[i, :, g * LANES : (g + 1) * LANES] if ready else None
            more.append(pack_sums(rotated, codes, pack, False, table))
        totals = more if totals is None else [a + b for a, b in zip(totals, more)]
    write_sums(pack_diagonals(totals, owned, False)[0], None, owned, out_ref)


def next_sums_call(codes, ready, blocks, chunks):
    owned = codes.shape[1]
    held, rows = flat(chunks)
    given = list(ready[:2]) if ready else rows
    return pl.pallas_call(
        functools.partial(next_sums_kernel, held, bool(ready)),
        out_shape=jax.ShapeDtypeStruct((pack_layout(owned, False)[2], LANES), BF16),
        in_specs=[vmem_spec()] * (1 + len(blocks) + len(given)),
        out_specs=vmem_spec(),
        compiler_params=params(*given),
        cost_estimate=cost(0),
        name="next_sums",
    )(codes, *blocks, *given)


def final_kernel(size, place_ref, residual_ref, *refs):
    parts, out_ref, whole = refs[:size], refs[size], refs[size + 1]
    height = parts[0].shape[0]
    for k, ref in enumerate(parts):
        at = pl.multiple_of((place_ref[0] ^ k) * height, 16 if whole.dtype == BF16 else 8)
        whole[pl.ds(at, height), :] = ref[...].astype(whole.dtype)
    xb = first_step(whole[...].astype(BF16)).astype(BF16)
    once = mm(residual_ref[...], xb, NT)
    less = mm(mm(once.astype(BF16), xb).astype(BF16), xb, NT)
    out_ref[...] = (1.5 * once - 0.5 * less).astype(BF16)


def final_call(place, residual, blocks):
    rows, width = residual.shape
    kind = BF16 if blocks[0].shape[0] % 16 == 0 else F32
    return pl.pallas_call(
        functools.partial(final_kernel, len(blocks)),
        out_shape=jax.ShapeDtypeStruct((rows, width), BF16),
        in_specs=[smem_spec()] + [vmem_spec()] * (1 + len(blocks)),
        out_specs=vmem_spec(),
        scratch_shapes=[pltpu.VMEM((width, width), kind)],
        compiler_params=params(),
        cost_estimate=cost(0),
        name="final",
    )(place, residual, *blocks)


def after(x, *first):
    return lax.optimization_barrier((x,) + first)[0]


def near_rows(rows, size):
    return {1 << b: swap(rows, "within", size, 1 << b) for b in range(1, size.bit_length() - 1)}


def far_rows(rows, near, size):
    bits = list(near)
    half = rows.shape[0] // 2
    halves = []
    for order, cut in ((bits, slice(0, half)), (bits[::-1], slice(half, None))):
        here = {0: rows, order[0]: near[order[0]][cut]}
        for bit in order[1:]:
            for k in list(here):
                here[k ^ bit] = swap(here[k], "within", size, bit) if k else near[bit][cut]
        halves.append(here)
    return {k: (halves[0][k], halves[1][k]) for k in halves[0] if k and k not in near}


def both_cores(whole, size):
    return {k ^ 1: tuple(swap(piece, "within", size, 1) for piece in pieces) for k, pieces in whole.items()}


def gather_group(x, size):
    blocks = {k: swap(x, "within", size, k) if k else x for k in range(0, size, 2)}
    for k in list(blocks):
        blocks[k ^ 1] = swap(blocks[k], "within", size, 1)
    return [blocks[k] for k in range(size)]


def scatter_sums(merged, owned, rows, size):
    parts = [merged[0]] + [swap(merged[k // 2], "within", size, k) for k in range(2, size, 2)]
    return merge_chips_call(parts, owned, rows)


def direct(x, size):
    return [x] + [swap(x, "group", size, k) for k in range(1, size)]


def reduce_cross(cross, size, last):
    bits = [1 << b for b in range(size.bit_length() - 1)]
    for bit in bits:
        if bit == bits[-1]:
            cross = after(cross, *last)
        cross = (cross.astype(F32) + swap(cross, "group", size, bit).astype(F32)).astype(BF16)
    return cross


def per_device(vectors, centroids, list_ids, codes, rotation):
    groups = lax.axis_size("group")
    size = lax.axis_size("within")
    rows, width = vectors.shape
    owned = codes.shape[1] // size
    total_rows = rows * size * groups
    place = lax.axis_index("within").astype(jnp.int32).reshape(1)
    residual = residual_call(vectors, centroids, list_ids)
    near = near_rows(residual, size)
    twin = swap(residual, "within", size, 1)
    even, odd = local_sums_call(place, rotation, codes.T, after(residual, twin), size)
    merged = merge_cores_call(even, swap(odd, "within", size, 1), owned)
    sums, own_codes = scatter_sums(merged, owned, rows, size)
    far = far_rows(residual, near, size)
    near = {k: after(rows_near, sums) for k, rows_near in near.items()}
    for bit in [1 << b for b in range(groups.bit_length() - 2)]:
        sums = merge_call(sums, swap(sums, "group", groups, bit), owned)
    parts = [sums, swap(sums, "group", groups, groups // 2)]
    chunks = {0: (residual,), 1: (twin,)}
    for k, rows_near in near.items():
        chunks[k] = (rows_near,)
        chunks[k ^ 1] = (swap(rows_near, "within", size, 1),)
    total, wide, counts = cross_near_call(own_codes, parts, chunks)
    far = {k: tuple(after(piece, parts[1]) for piece in pieces) for k, pieces in far.items()}
    far = {**far, **both_cores(far, size)}
    cross = cross_far_call(own_codes, total, wide, far, total_rows)
    chunks.update(far)
    ready = prepare_call(own_codes, chunks, (cross,), (cross,))
    for alternation in range(1, ALTS):
        block = reduce_cross(cross, groups, ready[:1] if ready else ())
        if ready:
            block = after(block, *ready)
        parts = direct(next_sums_call(own_codes, ready, gather_group(block, size), chunks), groups)
        cross, book = cross_call(own_codes, ready, parts, counts, chunks, total_rows)
    packs = len(packs_of(owned))
    book = book.reshape(packs, LO * SUB, PACK, HI).transpose(0, 2, 3, 1).reshape(packs * PACK, K * SUB)[:owned]
    blocks = gather_group(reduce_cross(cross, groups, (book,)), size)
    rotated_out = final_call(place, residual, blocks)
    return (rotated_out, book)


def solution(mesh):
    in_specs = (
        P(("group", "within"), None),
        P(("group", "within"), None),
        P(("group", "within")),
        P(("group", "within"), None),
        P(),
    )
    out_specs = (P(("group", "within"), None), P("within", None))
    return jax.shard_map(per_device, mesh=mesh, in_specs=in_specs, out_specs=out_specs, check_vma=False)
```

```python
import functools
import math

import jax
import jax.numpy as jnp
from jax import lax
from jax.experimental import pallas as pl
from jax.experimental.pallas import tpu as pltpu
from jax.sharding import PartitionSpec as P

K = 256
ALTS = 2
LO = 4
HI = K // LO
SUB = 8
LANES = 256
PACK = LANES // HI
MARKS = 8
SPAN = 2
EPSILON = 1e-06
MIB = 1024 * 1024

F32 = jnp.float32
BF16 = jnp.bfloat16
NT = (((1,), (1,)), ((), ()))
NN = (((1,), (0,)), ((), ()))
TN = (((0,), (0,)), ((), ()))


def mm(a, b, dims=NN):
    return lax.dot_general(a, b, dims, preferred_element_type=F32)


def vmem_spec():
    return pl.BlockSpec(memory_space=pltpu.VMEM)


def smem_spec():
    return pl.BlockSpec(memory_space=pltpu.SMEM)


def cost(us):
    return pl.CostEstimate(flops=int(us * 1e9), bytes_accessed=0, transcendentals=0)


def params(*arrays):
    held = sum(math.prod(a.shape) * a.dtype.itemsize for a in arrays)
    return pltpu.CompilerParams(vmem_limit_bytes=held + 12 * MIB)


def swap(x, axis, size, bits):
    return lax.ppermute(x, axis, [(i, i ^ bits) for i in range(size)])


def levels_kernel(out_ref):
    out_ref[...] = lax.broadcasted_iota(jnp.int32, out_ref.shape, 0)


def pick_kernel(lists, ids_ref, levels_ref, table_ref):
    local = lax.rem(ids_ref[...], lists)
    table_ref[...] = jnp.where(levels_ref[...] == local, 1.0, 0.0).astype(BF16)


def pick_call(ids, lists):
    rows = ids.shape[0]
    levels = pl.pallas_call(
        levels_kernel,
        out_shape=jax.ShapeDtypeStruct((lists, rows), jnp.int32),
        out_specs=vmem_spec(),
        compiler_params=params(),
        cost_estimate=cost(10),
        name="levels",
    )()
    return pl.pallas_call(
        functools.partial(pick_kernel, lists),
        out_shape=jax.ShapeDtypeStruct((lists, rows), BF16),
        in_specs=[vmem_spec()] * 2,
        out_specs=vmem_spec(),
        compiler_params=params(),
        cost_estimate=cost(0),
        name="pick",
    )(ids.reshape(1, rows), levels)


def residual_kernel(vectors_ref, centroids_ref, table_ref, out_ref):
    table = table_ref[...]
    center = centroids_ref[...]
    first = center.astype(BF16)
    rest = center - first.astype(F32)
    second = rest.astype(BF16)
    third = (rest - second.astype(F32)).astype(BF16)
    picked = mm(table, first, TN) + mm(table, second, TN) + mm(table, third, TN)
    out_ref[...] = (vectors_ref[...].astype(F32) - picked).astype(BF16)


def residual_call(vectors, centroids, ids):
    return pl.pallas_call(
        residual_kernel,
        out_shape=jax.ShapeDtypeStruct(vectors.shape, BF16),
        in_specs=[vmem_spec()] * 3,
        out_specs=vmem_spec(),
        compiler_params=params(),
        cost_estimate=cost(10),
        name="residual",
    )(vectors, centroids, pick_call(ids, centroids.shape[0]))


def split(codes):
    return codes >> 2, codes & 3


def packs_of(owned):
    return [range(first, min(first + PACK, owned)) for first in range(0, owned, PACK)]


def hi_table(hi, pack):
    rows = hi.shape[1]
    level = lax.broadcasted_iota(jnp.int32, (HI, rows), 0)
    parts = [jnp.where(level == hi[m : m + 1, :], 1.0, 0.0) for m in pack]
    parts += [jnp.zeros((HI, rows), F32)] * (PACK - len(pack))
    return jnp.concatenate(parts, axis=0).astype(BF16)


def lane_owner(rows):
    return lax.broadcasted_iota(jnp.int32, (rows, LANES), 1) // HI


def diagonal(wide, block):
    owner = lane_owner(block)
    total = jnp.zeros((block, LANES), F32)
    for i in range(wide.shape[0] // block):
        total = jnp.where(owner == i, wide[i * block : (i + 1) * block, :], total)
    return total


def pack_sums(rotated, codes, pack, with_counts, table=None):
    rows = codes.shape[1]
    hi, lo = split(codes)
    parts = []
    for m in pack:
        value = rotated[m * SUB : (m + 1) * SUB, :]
        low = jnp.broadcast_to(lo[m : m + 1, :], (SUB, rows))
        parts += [jnp.where(low == level, value, 0.0) for level in range(LO)]
    if with_counts:
        low_level = lax.broadcasted_iota(jnp.int32, (MARKS, rows), 0)
        parts += [jnp.where(low_level == lo[m : m + 1, :], 1.0, 0.0) for m in pack]
    marked = jnp.concatenate(parts, axis=0).astype(BF16)
    return mm(marked, hi_table(hi, pack), NT) if table is None else mm(marked, table)


def pack_layout(owned, with_counts):
    packs = len(packs_of(owned))
    base, height = packs * LO * SUB, packs * MARKS
    return base, height, base + (-(-height // 16) * 16 if with_counts else 0)


def write_sums(sums, counts, owned, out_ref):
    base, height, total = pack_layout(owned, counts is not None)
    out_ref[:base, :] = sums.astype(BF16)
    if counts is not None:
        above = jnp.floor(counts * (1.0 / 256.0))
        below = counts - above * 256.0
        pieces = []
        for at in range(0, height, MARKS):
            pieces.append(jnp.concatenate([above[at : at + LO], below[at : at + LO]], axis=0))
        if total > base + height:
            pieces.append(jnp.zeros((total - base - height, LANES), F32))
        out_ref[base:, :] = jnp.concatenate(pieces, axis=0).astype(BF16)


def pack_diagonals(totals, owned, with_counts):
    block = LO * SUB
    sums, counts = [], []
    for total, pack in zip(totals, packs_of(owned)):
        size = len(pack)
        sums.append(diagonal(total[: size * block], block))
        if with_counts:
            counts.append(diagonal(total[size * block :], MARKS))
    return jnp.concatenate(sums, axis=0), jnp.concatenate(counts, axis=0) if with_counts else None


def tree(values):
    while len(values) > 1:
        values = [values[i] + values[i + 1] for i in range(0, len(values), 2)]
    return values[0]


def merge_parts(parts, owned, with_counts):
    base, height, unused = pack_layout(owned, with_counts)
    whole = tree([ref[...].astype(F32) for ref in parts])
    if not with_counts:
        return whole, None
    counts = []
    for at in range(base, base + height, MARKS):
        count = whole[at : at + LO] * 256.0 + whole[at + LO : at + MARKS]
        counts.append(jnp.concatenate([count, jnp.zeros((MARKS - LO, LANES), F32)], axis=0))
    return whole[:base], jnp.concatenate(counts, axis=0)


def code_rows(rows):
    return rows // LANES * 16


def write_codes(codes, out_ref, at):
    owned, rows = codes.shape
    filled = jnp.concatenate([codes, jnp.zeros((16 - owned, rows), F32)], axis=0).astype(BF16)
    for c in range(rows // LANES):
        out_ref[at + 16 * c : at + 16 * c + 16, :] = filled[:, LANES * c : LANES * (c + 1)]


def local_sums_kernel(size, place_ref, rotation_ref, codes_ref, residual_ref, *refs):
    outs, turned, staged = refs[:2], refs[2], refs[3]
    subspaces = codes_ref.shape[0]
    owned = subspaces // size
    base = pack_layout(owned, True)[2]
    rotated = mm(residual_ref[...], rotation_ref[...].astype(BF16)).astype(BF16).astype(F32)
    turned[...] = rotated.T
    for j in range(size):
        staged[j, :owned, :] = codes_ref[j * owned : (j + 1) * owned, :]
    for k in range(size):
        other = place_ref[0] ^ k
        codes = staged[other][:owned]
        value = turned[pl.ds(pl.multiple_of(other * (owned * SUB), 8), owned * SUB), :]
        totals = [pack_sums(value, codes, pack, True) for pack in packs_of(owned)]
        sums, counts = pack_diagonals(totals, owned, True)
        slot = outs[k % 2].at[k // 2]
        write_sums(sums, counts, owned, slot.at[:base])
        write_codes(codes.astype(F32), slot, base)


def local_sums_call(place, rotation, codes, residual, size):
    subspaces, rows = codes.shape
    owned = subspaces // size
    height = -(-owned // 8) * 8
    shape = jax.ShapeDtypeStruct((size // 2, pack_layout(owned, True)[2] + code_rows(rows), LANES), BF16)
    return pl.pallas_call(
        functools.partial(local_sums_kernel, size),
        out_shape=(shape,) * 2,
        in_specs=[smem_spec()] + [vmem_spec()] * 3,
        out_specs=(vmem_spec(),) * 2,
        scratch_shapes=[pltpu.VMEM((rotation.shape[1], rows), F32), pltpu.VMEM((size, height, rows), jnp.int32)],
        compiler_params=params(rotation),
        cost_estimate=cost(0),
        name="local_sums",
    )(place, rotation, codes, residual)


def merge_cores_kernel(owned, even_ref, came_ref, *outs):
    base = pack_layout(owned, True)[2]
    length = even_ref.shape[1] - base
    for i, out_ref in enumerate(outs):
        sums, counts = merge_parts([even_ref.at[i], came_ref.at[i]], owned, True)
        write_sums(sums, counts, owned, out_ref.at[:base])
        out_ref[base : base + length, :] = even_ref[i, base:, :]
        out_ref[base + length :, :] = came_ref[i, base:, :]


def merge_cores_call(even, came, owned):
    slots, height, lanes = even.shape
    shape = jax.ShapeDtypeStruct((2 * height - pack_layout(owned, True)[2], lanes), BF16)
    return pl.pallas_call(
        functools.partial(merge_cores_kernel, owned),
        out_shape=(shape,) * slots,
        in_specs=[vmem_spec()] * 2,
        out_specs=(vmem_spec(),) * slots,
        compiler_params=params(),
        cost_estimate=cost(0),
        name="merge_cores",
    )(even, came)


def merge_chips_kernel(owned, *refs):
    parts, (out_ref, codes_ref) = refs[:-2], refs[-2:]
    base = pack_layout(owned, True)[2]
    sums, counts = merge_parts(parts, owned, True)
    write_sums(sums, counts, owned, out_ref)
    length = (parts[0].shape[0] - base) // 2
    for i, part in enumerate(parts):
        for core in range(2):
            for c in range(length // 16):
                at = base + core * length + 16 * c
                piece = part[at : at + 16, :].astype(F32)
                codes_ref[2 * i + core, :, LANES * c : LANES * (c + 1)] = piece[:owned].astype(jnp.int32)


def merge_chips_call(parts, owned, rows):
    size = 2 * len(parts)
    return pl.pallas_call(
        functools.partial(merge_chips_kernel, owned),
        out_shape=(
            jax.ShapeDtypeStruct((pack_layout(owned, True)[2], LANES), BF16),
            jax.ShapeDtypeStruct((size, owned, rows), jnp.int32),
        ),
        in_specs=[vmem_spec()] * len(parts),
        out_specs=(vmem_spec(),) * 2,
        compiler_params=params(),
        cost_estimate=cost(0),
        name="merge_chips",
    )(*parts)


def merge_kernel(owned, first_ref, second_ref, out_ref):
    sums, counts = merge_parts([first_ref, second_ref], owned, True)
    write_sums(sums, counts, owned, out_ref)


def merge_call(first, second, owned):
    return pl.pallas_call(
        functools.partial(merge_kernel, owned),
        out_shape=jax.ShapeDtypeStruct(first.shape, BF16),
        in_specs=[vmem_spec()] * 2,
        out_specs=vmem_spec(),
        compiler_params=params(),
        cost_estimate=cost(0),
        name="merge_groups",
    )(first, second)


def spans_of(held):
    peers = [k for even in held if even % 2 == 0 for k in (even, even ^ 1)]
    return [tuple(peers[i : i + SPAN]) for i in range(0, len(peers), SPAN)]


def span_codes(codes_ref, span):
    return jnp.concatenate([codes_ref[k] for k in span], axis=1)


def span_rows(pieces, span):
    return jnp.concatenate([ref[...] for k in span for ref in pieces[k]], axis=0)


def pieces_of(held, refs):
    at = 0
    pieces = {}
    for k, count in held.items():
        pieces[k] = refs[at : at + count]
        at += count
    return pieces


def read_books(sums, counts_in, owned):
    everything, counts = merge_parts(sums, owned, counts_in is None)
    if counts is None:
        counts = counts_in[...]
    block = LO * SUB
    books = []
    for g in range(len(packs_of(owned))):
        rows = []
        for level in range(LO):
            at = g * block + level * SUB
            rows.append(everything[at : at + SUB] / (counts[g * MARKS + level : g * MARKS + level + 1] + 1.0))
        books.append(jnp.concatenate(rows, axis=0))
    return books, counts


def widen(books, owned):
    owner = lane_owner(LO * SUB)
    return [
        jnp.concatenate([jnp.where(owner == i, book, 0.0) for i in range(len(pack))], axis=0).astype(BF16)
        for book, pack in zip(books, packs_of(owned))
    ]


def add_spans(total, wide, codes_ref, pieces, spans, tables=None, first=0):
    owned = codes_ref.shape[1]
    for i, span in enumerate(spans):
        codes = span_codes(codes_ref, span)
        hi, lo = split(codes)
        rows = codes.shape[1]
        rebuilt = []
        for g, pack in enumerate(packs_of(owned)):
            table = hi_table(hi, pack) if tables is None else tables[first + i, g * LANES : (g + 1) * LANES, :]
            spread = mm(wide[g], table)
            for j, m in enumerate(pack):
                low = jnp.broadcast_to(lo[m : m + 1, :], (SUB, rows))
                at = j * LO * SUB
                value = spread[at : at + SUB]
                for level in range(1, LO):
                    value = jnp.where(low == level, spread[at + level * SUB : at + (level + 1) * SUB], value)
                rebuilt.append(value)
        part = mm(jnp.concatenate(rebuilt, axis=0).astype(BF16), span_rows(pieces, span))
        total = part if total is None else total + part
    return total


def flat(chunks):
    return {k: len(c) for k, c in chunks.items()}, [piece for c in chunks.values() for piece in c]


def cross_near_kernel(held, groups, ready, codes_ref, *refs):
    tables, refs = (refs[0], refs[1:]) if ready else (None, refs)
    sums, pieces, outs = refs[:groups], pieces_of(held, refs[groups:]), refs[groups + sum(held.values()) :]
    total_ref, wide_ref, counts_ref = outs
    owned = codes_ref.shape[1]
    books, counts = read_books(sums, None, owned)
    counts_ref[...] = counts
    wide = widen(books, owned)
    for g, one in enumerate(wide):
        wide_ref[g, : one.shape[0], :] = one
    total_ref[...] = add_spans(None, wide, codes_ref, pieces, spans_of(held), tables)


def cross_near_call(codes, tables, sums, chunks):
    owned = codes.shape[1]
    packs = len(packs_of(owned))
    held, rows = flat(chunks)
    return pl.pallas_call(
        functools.partial(cross_near_kernel, held, len(sums), bool(tables)),
        out_shape=(
            jax.ShapeDtypeStruct((owned * SUB, rows[0].shape[1]), F32),
            jax.ShapeDtypeStruct((packs, PACK * LO * SUB, LANES), BF16),
            jax.ShapeDtypeStruct((packs * MARKS, LANES), F32),
        ),
        in_specs=[vmem_spec()] * (1 + len(tables) + len(sums) + len(rows)),
        out_specs=(vmem_spec(),) * 3,
        compiler_params=params(*rows),
        cost_estimate=cost(0),
        name="cross_near",
    )(codes, *tables, *sums, *rows)


def cross_far_kernel(held, total_rows, first, codes_ref, total_ref, wide_ref, *refs):
    tables, refs = (refs[0], refs[1:]) if first else (None, refs)
    pieces, cross_ref = pieces_of(held, refs), refs[-1]
    packs = packs_of(codes_ref.shape[1])
    wide = [wide_ref[g, : len(pack) * LO * SUB, :] for g, pack in enumerate(packs)]
    total = add_spans(total_ref[...], wide, codes_ref, pieces, spans_of(held), tables, first)
    cross_ref[...] = (total * (1.0 / total_rows)).astype(BF16)


def cross_far_call(codes, tables, first, total, wide, chunks, total_rows):
    held, rows = flat(chunks)
    return pl.pallas_call(
        functools.partial(cross_far_kernel, held, total_rows, first if tables else 0),
        out_shape=jax.ShapeDtypeStruct(total.shape, BF16),
        in_specs=[vmem_spec()] * (3 + len(tables) + len(rows)),
        out_specs=vmem_spec(),
        compiler_params=params(*rows),
        cost_estimate=cost(0),
        name="cross_far",
    )(codes, total, wide, *tables, *rows)


def cross_kernel(held, groups, total_rows, ready, codes_ref, *refs):
    tables, refs = (refs[0], refs[1:]) if ready else (None, refs)
    sums, counts_in, pieces = refs[:groups], refs[groups], pieces_of(held, refs[groups + 1 :])
    cross_ref, book_ref = refs[-2:]
    owned = codes_ref.shape[1]
    block = LO * SUB
    books, unused = read_books(sums, counts_in, owned)
    for g, book in enumerate(books):
        book_ref[g * block : (g + 1) * block, :] = book
    total = add_spans(None, widen(books, owned), codes_ref, pieces, spans_of(held), tables)
    cross_ref[...] = (total * (1.0 / total_rows)).astype(BF16)


def cross_call(codes, ready, sums, counts, chunks, total_rows):
    owned = codes.shape[1]
    held, rows = flat(chunks)
    tables = [ready[2]] if ready else []
    return pl.pallas_call(
        functools.partial(cross_kernel, held, len(sums), total_rows, bool(ready)),
        out_shape=(
            jax.ShapeDtypeStruct((owned * SUB, rows[0].shape[1]), BF16),
            jax.ShapeDtypeStruct((len(packs_of(owned)) * LO * SUB, LANES), F32),
        ),
        in_specs=[vmem_spec()] * (2 + len(tables) + len(sums) + len(rows)),
        out_specs=(vmem_spec(), vmem_spec()),
        compiler_params=params(*rows, *tables),
        cost_estimate=cost(0),
        name="cross",
    )(codes, *tables, *sums, counts, *rows)


def turn_kernel(held, *refs):
    pieces, turned_ref = pieces_of(held, refs), refs[-1]
    for i, span in enumerate(spans_of(held)):
        turned_ref[i, :, :] = span_rows(pieces, span).T


def tables_kernel(spans, codes_ref, table_ref, across_ref):
    packs = packs_of(codes_ref.shape[1])
    for i, span in enumerate(spans):
        hi = split(span_codes(codes_ref, span))[0]
        for g, pack in enumerate(packs):
            table = hi_table(hi, pack)
            across_ref[i, g * LANES : (g + 1) * LANES, :] = table
            table_ref[i, :, g * LANES : (g + 1) * LANES] = table.T


def tables_call(codes, peers):
    owned, rows = codes.shape[1:]
    lanes = LANES * len(packs_of(owned))
    spans = spans_of(dict.fromkeys(peers))
    each = len(spans[0]) * rows
    shapes = (
        jax.ShapeDtypeStruct((len(spans), each, lanes), BF16),
        jax.ShapeDtypeStruct((len(spans), lanes, each), BF16),
    )
    if sum(math.prod(a.shape) * 2 for a in shapes) > 14 * MIB:
        return ()
    return pl.pallas_call(
        functools.partial(tables_kernel, spans),
        out_shape=shapes,
        in_specs=[vmem_spec()],
        out_specs=(vmem_spec(),) * 2,
        compiler_params=params(*shapes),
        cost_estimate=cost(0),
        name="tables",
    )(codes)


def turn_call(chunks):
    held, pieces = flat(chunks)
    spans = spans_of(held)
    each = len(spans[0]) * chunks[0][0].shape[0]
    turned = jax.ShapeDtypeStruct((len(spans), pieces[0].shape[1], each), BF16)
    return pl.pallas_call(
        functools.partial(turn_kernel, held),
        out_shape=turned,
        in_specs=[vmem_spec()] * len(pieces),
        out_specs=vmem_spec(),
        compiler_params=params(turned),
        cost_estimate=cost(0),
        name="turn_rows",
    )(*pieces)


def first_step(xb):
    gram = mm(xb, xb, NT)
    norm_square = jnp.sqrt(jnp.sum(gram * gram, keepdims=True) + EPSILON)
    scale = lax.rsqrt(norm_square)
    step = mm(gram.astype(BF16), xb)
    return (1.5 * scale) * xb.astype(F32) - (0.5 * scale / norm_square) * step


def join(parts):
    if parts[0].shape[0] % 16 == 0:
        return jnp.concatenate(parts, axis=0)
    return jnp.concatenate([p.astype(F32) for p in parts], axis=0).astype(BF16)


def next_sums_kernel(held, ready, codes_ref, *refs):
    size = len(held)
    parts, out_ref = refs[:size], refs[-1]
    if ready:
        turned_ref, table_ref = refs[size : size + 2]
    else:
        pieces = pieces_of(held, refs[size:])
    owned = codes_ref.shape[1]
    height = parts[0].shape[0]
    x = first_step(join([ref[...] for ref in parts]))
    xb = x.astype(BF16)
    mine = x[:height]
    gram = mm(mine.astype(BF16), xb, NT)
    rotation_rows = (1.5 * mine - 0.5 * mm(gram.astype(BF16), xb)).astype(BF16)
    totals = None
    for i, span in enumerate(spans_of(held)):
        if ready:
            rotated = mm(rotation_rows, turned_ref[i])
        else:
            rotated = mm(rotation_rows, span_rows(pieces, span), NT)
        rotated = rotated.astype(BF16).astype(F32)
        codes = span_codes(codes_ref, span)
        more = []
        for g, pack in enumerate(packs_of(owned)):
            table = table_ref[i, :, g * LANES : (g + 1) * LANES] if ready else None
            more.append(pack_sums(rotated, codes, pack, False, table))
        totals = more if totals is None else [a + b for a, b in zip(totals, more)]
    write_sums(pack_diagonals(totals, owned, False)[0], None, owned, out_ref)


def next_sums_call(codes, ready, blocks, chunks):
    owned = codes.shape[1]
    held, rows = flat(chunks)
    given = list(ready[:2]) if ready else rows
    return pl.pallas_call(
        functools.partial(next_sums_kernel, held, bool(ready)),
        out_shape=jax.ShapeDtypeStruct((pack_layout(owned, False)[2], LANES), BF16),
        in_specs=[vmem_spec()] * (1 + len(blocks) + len(given)),
        out_specs=vmem_spec(),
        compiler_params=params(*given),
        cost_estimate=cost(0),
        name="next_sums",
    )(codes, *blocks, *given)


def final_kernel(size, place_ref, residual_ref, *refs):
    parts, out_ref, whole = refs[:size], refs[size], refs[size + 1]
    height = parts[0].shape[0]
    for k, ref in enumerate(parts):
        at = pl.multiple_of((place_ref[0] ^ k) * height, 16 if whole.dtype == BF16 else 8)
        whole[pl.ds(at, height), :] = ref[...].astype(whole.dtype)
    xb = first_step(whole[...].astype(BF16)).astype(BF16)
    once = mm(residual_ref[...], xb, NT)
    less = mm(mm(once.astype(BF16), xb).astype(BF16), xb, NT)
    out_ref[...] = (1.5 * once - 0.5 * less).astype(BF16)


def final_call(place, residual, blocks):
    rows, width = residual.shape
    kind = BF16 if blocks[0].shape[0] % 16 == 0 else F32
    return pl.pallas_call(
        functools.partial(final_kernel, len(blocks)),
        out_shape=jax.ShapeDtypeStruct((rows, width), BF16),
        in_specs=[smem_spec()] + [vmem_spec()] * (1 + len(blocks)),
        out_specs=vmem_spec(),
        scratch_shapes=[pltpu.VMEM((width, width), kind)],
        compiler_params=params(),
        cost_estimate=cost(0),
        name="final",
    )(place, residual, *blocks)


def after(x, *first):
    return lax.optimization_barrier((x,) + first)[0]


def near_rows(rows, size):
    return {1 << b: swap(rows, "within", size, 1 << b) for b in range(1, size.bit_length() - 1)}


def far_rows(rows, near, size):
    bits = list(near)
    half = rows.shape[0] // 2
    halves = []
    for order, cut in ((bits, slice(0, half)), (bits[::-1], slice(half, None))):
        here = {0: rows, order[0]: near[order[0]][cut]}
        for bit in order[1:]:
            for k in list(here):
                here[k ^ bit] = swap(here[k], "within", size, bit) if k else near[bit][cut]
        halves.append(here)
    return {k: (halves[0][k], halves[1][k]) for k in halves[0] if k and k not in near}


def both_cores(whole, size):
    return {k ^ 1: tuple(swap(piece, "within", size, 1) for piece in pieces) for k, pieces in whole.items()}


def gather_group(x, size):
    blocks = {k: swap(x, "within", size, k) if k else x for k in range(0, size, 2)}
    for k in list(blocks):
        blocks[k ^ 1] = swap(blocks[k], "within", size, 1)
    return [blocks[k] for k in range(size)]


def scatter_sums(merged, owned, rows, size):
    parts = [merged[0]] + [swap(merged[k // 2], "within", size, k) for k in range(2, size, 2)]
    return merge_chips_call(parts, owned, rows)


def direct(x, size):
    return [x] + [swap(x, "group", size, k) for k in range(1, size)]


def reduce_cross(cross, size, last):
    bits = [1 << b for b in range(size.bit_length() - 1)]
    for bit in bits:
        if bit == bits[-1]:
            cross = after(cross, *last)
        cross = (cross.astype(F32) + swap(cross, "group", size, bit).astype(F32)).astype(BF16)
    return cross


def per_device(vectors, centroids, list_ids, codes, rotation):
    groups = lax.axis_size("group")
    size = lax.axis_size("within")
    rows, width = vectors.shape
    owned = codes.shape[1] // size
    total_rows = rows * size * groups
    place = lax.axis_index("within").astype(jnp.int32).reshape(1)
    residual = residual_call(vectors, centroids, list_ids)
    near = near_rows(residual, size)
    twin = swap(residual, "within", size, 1)
    even, odd = local_sums_call(place, rotation, codes.T, after(residual, twin), size)
    merged = merge_cores_call(even, swap(odd, "within", size, 1), owned)
    sums, own_codes = scatter_sums(merged, owned, rows, size)
    far = far_rows(residual, near, size)
    near = {k: after(rows_near, sums) for k, rows_near in near.items()}
    for bit in [1 << b for b in range(groups.bit_length() - 2)]:
        sums = merge_call(sums, swap(sums, "group", groups, bit), owned)
    chunks = {0: (residual,), 1: (twin,)}
    for k, rows_near in near.items():
        chunks[k] = (rows_near,)
        chunks[k ^ 1] = (swap(rows_near, "within", size, 1),)
    tables = tables_call(after(own_codes, sums), list(chunks) + [peer for k in far for peer in (k, k ^ 1)])
    parts = [sums, after(swap(sums, "group", groups, groups // 2), *tables)]
    total, wide, counts = cross_near_call(own_codes, tables[1:], parts, chunks)
    far = {k: tuple(after(piece, parts[1]) for piece in pieces) for k, pieces in far.items()}
    far = {**far, **both_cores(far, size)}
    cross = cross_far_call(own_codes, tables[1:], len(spans_of(chunks)), total, wide, far, total_rows)
    chunks.update({k: far[k] for even in far if even % 2 == 0 for k in (even, even ^ 1)})
    ready = ()
    if tables:
        ready = (turn_call({**chunks, 0: (after(residual, cross),)}), *tables)
    for alternation in range(1, ALTS):
        block = reduce_cross(cross, groups, ready[:1])
        parts = direct(next_sums_call(own_codes, ready, gather_group(block, size), chunks), groups)
        cross, book = cross_call(own_codes, ready, parts, counts, chunks, total_rows)
    packs = len(packs_of(owned))
    book = book.reshape(packs, LO * SUB, PACK, HI).transpose(0, 2, 3, 1).reshape(packs * PACK, K * SUB)[:owned]
    blocks = gather_group(reduce_cross(cross, groups, (book,)), size)
    rotated_out = final_call(place, residual, blocks)
    return (rotated_out, book)


def solution(mesh):
    in_specs = (
        P(("group", "within"), None),
        P(("group", "within"), None),
        P(("group", "within")),
        P(("group", "within"), None),
        P(),
    )
    out_specs = (P(("group", "within"), None), P("within", None))
    return jax.shard_map(per_device, mesh=mesh, in_specs=in_specs, out_specs=out_specs, check_vma=False)
```

```python
import functools
import math

import jax
import jax.numpy as jnp
from jax import lax
from jax.experimental import pallas as pl
from jax.experimental.pallas import tpu as pltpu
from jax.sharding import PartitionSpec as P

K = 256
ALTS = 2
LO = 4
HI = K // LO
SUB = 8
LANES = 256
PACK = LANES // HI
MARKS = 8
SPAN = 2
EPSILON = 1e-06
MIB = 1024 * 1024

F32 = jnp.float32
BF16 = jnp.bfloat16
NT = (((1,), (1,)), ((), ()))
NN = (((1,), (0,)), ((), ()))
TN = (((0,), (0,)), ((), ()))


def mm(a, b, dims=NN):
    return lax.dot_general(a, b, dims, preferred_element_type=F32)


def vmem_spec():
    return pl.BlockSpec(memory_space=pltpu.VMEM)


def smem_spec():
    return pl.BlockSpec(memory_space=pltpu.SMEM)


def cost(us):
    return pl.CostEstimate(flops=int(us * 1e9), bytes_accessed=0, transcendentals=0)


def params(*arrays):
    held = sum(math.prod(a.shape) * a.dtype.itemsize for a in arrays)
    return pltpu.CompilerParams(vmem_limit_bytes=held + 12 * MIB)


def swap(x, axis, size, bits):
    return lax.ppermute(x, axis, [(i, i ^ bits) for i in range(size)])


def levels_kernel(out_ref):
    out_ref[...] = lax.broadcasted_iota(jnp.int32, out_ref.shape, 0)


def pick_kernel(lists, ids_ref, levels_ref, table_ref):
    local = lax.rem(ids_ref[...], lists)
    table_ref[...] = jnp.where(levels_ref[...] == local, 1.0, 0.0).astype(BF16)


def pick_call(ids, lists):
    rows = ids.shape[0]
    levels = pl.pallas_call(
        levels_kernel,
        out_shape=jax.ShapeDtypeStruct((lists, rows), jnp.int32),
        out_specs=vmem_spec(),
        compiler_params=params(),
        cost_estimate=cost(10),
        name="levels",
    )()
    return pl.pallas_call(
        functools.partial(pick_kernel, lists),
        out_shape=jax.ShapeDtypeStruct((lists, rows), BF16),
        in_specs=[vmem_spec()] * 2,
        out_specs=vmem_spec(),
        compiler_params=params(),
        cost_estimate=cost(0),
        name="pick",
    )(ids.reshape(1, rows), levels)


def residual_kernel(vectors_ref, centroids_ref, table_ref, out_ref):
    table = table_ref[...]
    center = centroids_ref[...]
    first = center.astype(BF16)
    rest = center - first.astype(F32)
    second = rest.astype(BF16)
    third = (rest - second.astype(F32)).astype(BF16)
    picked = mm(table, first, TN) + mm(table, second, TN) + mm(table, third, TN)
    out_ref[...] = (vectors_ref[...].astype(F32) - picked).astype(BF16)


def residual_call(vectors, centroids, ids):
    return pl.pallas_call(
        residual_kernel,
        out_shape=jax.ShapeDtypeStruct(vectors.shape, BF16),
        in_specs=[vmem_spec()] * 3,
        out_specs=vmem_spec(),
        compiler_params=params(),
        cost_estimate=cost(10),
        name="residual",
    )(vectors, centroids, pick_call(ids, centroids.shape[0]))


def split(codes):
    return codes >> 2, codes & 3


def packs_of(owned):
    return [range(first, min(first + PACK, owned)) for first in range(0, owned, PACK)]


def hi_table(hi, pack):
    rows = hi.shape[1]
    level = lax.broadcasted_iota(jnp.int32, (HI, rows), 0)
    parts = [jnp.where(level == hi[m : m + 1, :], 1.0, 0.0) for m in pack]
    parts += [jnp.zeros((HI, rows), F32)] * (PACK - len(pack))
    return jnp.concatenate(parts, axis=0).astype(BF16)


def lane_owner(rows):
    return lax.broadcasted_iota(jnp.int32, (rows, LANES), 1) // HI


def diagonal(wide, block):
    owner = lane_owner(block)
    total = jnp.zeros((block, LANES), F32)
    for i in range(wide.shape[0] // block):
        total = jnp.where(owner == i, wide[i * block : (i + 1) * block, :], total)
    return total


def pack_sums(rotated, codes, pack, with_counts, table=None):
    rows = codes.shape[1]
    hi, lo = split(codes)
    parts = []
    for m in pack:
        value = rotated[m * SUB : (m + 1) * SUB, :]
        low = jnp.broadcast_to(lo[m : m + 1, :], (SUB, rows))
        parts += [jnp.where(low == level, value, 0.0) for level in range(LO)]
    if with_counts:
        low_level = lax.broadcasted_iota(jnp.int32, (MARKS, rows), 0)
        parts += [jnp.where(low_level == lo[m : m + 1, :], 1.0, 0.0) for m in pack]
    marked = jnp.concatenate(parts, axis=0).astype(BF16)
    return mm(marked, hi_table(hi, pack), NT) if table is None else mm(marked, table)


def pack_layout(owned, with_counts):
    packs = len(packs_of(owned))
    base, height = packs * LO * SUB, packs * MARKS
    return base, height, base + (-(-height // 16) * 16 if with_counts else 0)


def write_sums(sums, counts, owned, out_ref):
    base, height, total = pack_layout(owned, counts is not None)
    out_ref[:base, :] = sums.astype(BF16)
    if counts is not None:
        above = jnp.floor(counts * (1.0 / 256.0))
        below = counts - above * 256.0
        pieces = []
        for at in range(0, height, MARKS):
            pieces.append(jnp.concatenate([above[at : at + LO], below[at : at + LO]], axis=0))
        if total > base + height:
            pieces.append(jnp.zeros((total - base - height, LANES), F32))
        out_ref[base:, :] = jnp.concatenate(pieces, axis=0).astype(BF16)


def pack_diagonals(totals, owned, with_counts):
    block = LO * SUB
    sums, counts = [], []
    for total, pack in zip(totals, packs_of(owned)):
        size = len(pack)
        sums.append(diagonal(total[: size * block], block))
        if with_counts:
            counts.append(diagonal(total[size * block :], MARKS))
    return jnp.concatenate(sums, axis=0), jnp.concatenate(counts, axis=0) if with_counts else None


def tree(values):
    while len(values) > 1:
        values = [values[i] + values[i + 1] for i in range(0, len(values), 2)]
    return values[0]


def merge_parts(parts, owned, with_counts):
    base, height, unused = pack_layout(owned, with_counts)
    whole = tree([ref[...].astype(F32) for ref in parts])
    if not with_counts:
        return whole, None
    counts = []
    for at in range(base, base + height, MARKS):
        count = whole[at : at + LO] * 256.0 + whole[at + LO : at + MARKS]
        counts.append(jnp.concatenate([count, jnp.zeros((MARKS - LO, LANES), F32)], axis=0))
    return whole[:base], jnp.concatenate(counts, axis=0)


def code_rows(rows):
    return rows // LANES * 16


def write_codes(codes, out_ref, at):
    owned, rows = codes.shape
    filled = jnp.concatenate([codes, jnp.zeros((16 - owned, rows), F32)], axis=0).astype(BF16)
    for c in range(rows // LANES):
        out_ref[at + 16 * c : at + 16 * c + 16, :] = filled[:, LANES * c : LANES * (c + 1)]


def local_sums_kernel(size, place_ref, rotation_ref, codes_ref, residual_ref, *refs):
    outs, turned, staged = refs[:2], refs[2], refs[3]
    subspaces = codes_ref.shape[0]
    owned = subspaces // size
    base = pack_layout(owned, True)[2]
    rotated = mm(residual_ref[...], rotation_ref[...].astype(BF16)).astype(BF16).astype(F32)
    turned[...] = rotated.T
    for j in range(size):
        staged[j, :owned, :] = codes_ref[j * owned : (j + 1) * owned, :]
    for k in range(size):
        other = place_ref[0] ^ k
        codes = staged[other][:owned]
        value = turned[pl.ds(pl.multiple_of(other * (owned * SUB), 8), owned * SUB), :]
        totals = [pack_sums(value, codes, pack, True) for pack in packs_of(owned)]
        sums, counts = pack_diagonals(totals, owned, True)
        slot = outs[k % 2].at[k // 2]
        write_sums(sums, counts, owned, slot.at[:base])
        write_codes(codes.astype(F32), slot, base)


def local_sums_call(place, rotation, codes, residual, size):
    subspaces, rows = codes.shape
    owned = subspaces // size
    height = -(-owned // 8) * 8
    shape = jax.ShapeDtypeStruct((size // 2, pack_layout(owned, True)[2] + code_rows(rows), LANES), BF16)
    return pl.pallas_call(
        functools.partial(local_sums_kernel, size),
        out_shape=(shape,) * 2,
        in_specs=[smem_spec()] + [vmem_spec()] * 3,
        out_specs=(vmem_spec(),) * 2,
        scratch_shapes=[pltpu.VMEM((rotation.shape[1], rows), F32), pltpu.VMEM((size, height, rows), jnp.int32)],
        compiler_params=params(rotation),
        cost_estimate=cost(0),
        name="local_sums",
    )(place, rotation, codes, residual)


def merge_cores_kernel(owned, even_ref, came_ref, *outs):
    base = pack_layout(owned, True)[2]
    length = even_ref.shape[1] - base
    for i, out_ref in enumerate(outs):
        sums, counts = merge_parts([even_ref.at[i], came_ref.at[i]], owned, True)
        write_sums(sums, counts, owned, out_ref.at[:base])
        out_ref[base : base + length, :] = even_ref[i, base:, :]
        out_ref[base + length :, :] = came_ref[i, base:, :]


def merge_cores_call(even, came, owned):
    slots, height, lanes = even.shape
    shape = jax.ShapeDtypeStruct((2 * height - pack_layout(owned, True)[2], lanes), BF16)
    return pl.pallas_call(
        functools.partial(merge_cores_kernel, owned),
        out_shape=(shape,) * slots,
        in_specs=[vmem_spec()] * 2,
        out_specs=(vmem_spec(),) * slots,
        compiler_params=params(),
        cost_estimate=cost(0),
        name="merge_cores",
    )(even, came)


def merge_chips_kernel(owned, *refs):
    parts, (out_ref, codes_ref) = refs[:-2], refs[-2:]
    base = pack_layout(owned, True)[2]
    sums, counts = merge_parts(parts, owned, True)
    write_sums(sums, counts, owned, out_ref)
    length = (parts[0].shape[0] - base) // 2
    for i, part in enumerate(parts):
        for core in range(2):
            for c in range(length // 16):
                at = base + core * length + 16 * c
                piece = part[at : at + 16, :].astype(F32)
                codes_ref[2 * i + core, :, LANES * c : LANES * (c + 1)] = piece[:owned].astype(jnp.int32)


def merge_chips_call(parts, owned, rows):
    size = 2 * len(parts)
    return pl.pallas_call(
        functools.partial(merge_chips_kernel, owned),
        out_shape=(
            jax.ShapeDtypeStruct((pack_layout(owned, True)[2], LANES), BF16),
            jax.ShapeDtypeStruct((size, owned, rows), jnp.int32),
        ),
        in_specs=[vmem_spec()] * len(parts),
        out_specs=(vmem_spec(),) * 2,
        compiler_params=params(),
        cost_estimate=cost(0),
        name="merge_chips",
    )(*parts)


def merge_kernel(owned, first_ref, second_ref, out_ref):
    sums, counts = merge_parts([first_ref, second_ref], owned, True)
    write_sums(sums, counts, owned, out_ref)


def merge_call(first, second, owned):
    return pl.pallas_call(
        functools.partial(merge_kernel, owned),
        out_shape=jax.ShapeDtypeStruct(first.shape, BF16),
        in_specs=[vmem_spec()] * 2,
        out_specs=vmem_spec(),
        compiler_params=params(),
        cost_estimate=cost(0),
        name="merge_groups",
    )(first, second)


def spans_of(held):
    peers = [k for even in held if even % 2 == 0 for k in (even, even ^ 1)]
    return [tuple(peers[i : i + SPAN]) for i in range(0, len(peers), SPAN)]


def span_codes(codes_ref, span):
    return jnp.concatenate([codes_ref[k] for k in span], axis=1)


def span_rows(pieces, span):
    return jnp.concatenate([ref[...] for k in span for ref in pieces[k]], axis=0)


def pieces_of(held, refs):
    at = 0
    pieces = {}
    for k, count in held.items():
        pieces[k] = refs[at : at + count]
        at += count
    return pieces


def read_books(sums, counts_in, owned):
    everything, counts = merge_parts(sums, owned, counts_in is None)
    if counts is None:
        counts = counts_in[...]
    block = LO * SUB
    books = []
    for g in range(len(packs_of(owned))):
        rows = []
        for level in range(LO):
            at = g * block + level * SUB
            rows.append(everything[at : at + SUB] / (counts[g * MARKS + level : g * MARKS + level + 1] + 1.0))
        books.append(jnp.concatenate(rows, axis=0))
    return books, counts


def widen(books, owned):
    owner = lane_owner(LO * SUB)
    return [
        jnp.concatenate([jnp.where(owner == i, book, 0.0) for i in range(len(pack))], axis=0).astype(BF16)
        for book, pack in zip(books, packs_of(owned))
    ]


def add_spans(total, wide, codes_ref, pieces, spans, tables=None, first=0):
    owned = codes_ref.shape[1]
    for i, span in enumerate(spans):
        codes = span_codes(codes_ref, span)
        hi, lo = split(codes)
        rows = codes.shape[1]
        rebuilt = []
        for g, pack in enumerate(packs_of(owned)):
            table = hi_table(hi, pack) if tables is None else tables[first + i, g * LANES : (g + 1) * LANES, :]
            spread = mm(wide[g], table)
            for j, m in enumerate(pack):
                low = jnp.broadcast_to(lo[m : m + 1, :], (SUB, rows))
                at = j * LO * SUB
                value = spread[at : at + SUB]
                for level in range(1, LO):
                    value = jnp.where(low == level, spread[at + level * SUB : at + (level + 1) * SUB], value)
                rebuilt.append(value)
        part = mm(jnp.concatenate(rebuilt, axis=0).astype(BF16), span_rows(pieces, span))
        total = part if total is None else total + part
    return total


def flat(chunks):
    return {k: len(c) for k, c in chunks.items()}, [piece for c in chunks.values() for piece in c]


def cross_near_kernel(held, groups, ready, codes_ref, *refs):
    tables, refs = (refs[0], refs[1:]) if ready else (None, refs)
    sums, pieces, outs = refs[:groups], pieces_of(held, refs[groups:]), refs[groups + sum(held.values()) :]
    total_ref, wide_ref, counts_ref = outs
    owned = codes_ref.shape[1]
    books, counts = read_books(sums, None, owned)
    counts_ref[...] = counts
    wide = widen(books, owned)
    for g, one in enumerate(wide):
        wide_ref[g, : one.shape[0], :] = one
    total_ref[...] = add_spans(None, wide, codes_ref, pieces, spans_of(held), tables)


def cross_near_call(codes, tables, sums, chunks):
    owned = codes.shape[1]
    packs = len(packs_of(owned))
    held, rows = flat(chunks)
    return pl.pallas_call(
        functools.partial(cross_near_kernel, held, len(sums), bool(tables)),
        out_shape=(
            jax.ShapeDtypeStruct((owned * SUB, rows[0].shape[1]), F32),
            jax.ShapeDtypeStruct((packs, PACK * LO * SUB, LANES), BF16),
            jax.ShapeDtypeStruct((packs * MARKS, LANES), F32),
        ),
        in_specs=[vmem_spec()] * (1 + len(tables) + len(sums) + len(rows)),
        out_specs=(vmem_spec(),) * 3,
        compiler_params=params(*rows),
        cost_estimate=cost(0),
        name="cross_near",
    )(codes, *tables, *sums, *rows)


def cross_far_kernel(held, total_rows, first, codes_ref, total_ref, wide_ref, *refs):
    tables, refs = (refs[0], refs[1:]) if first else (None, refs)
    pieces, cross_ref = pieces_of(held, refs), refs[-1]
    packs = packs_of(codes_ref.shape[1])
    wide = [wide_ref[g, : len(pack) * LO * SUB, :] for g, pack in enumerate(packs)]
    total = add_spans(total_ref[...], wide, codes_ref, pieces, spans_of(held), tables, first)
    cross_ref[...] = (total * (1.0 / total_rows)).astype(BF16)


def cross_far_call(codes, tables, first, total, wide, chunks, total_rows):
    held, rows = flat(chunks)
    return pl.pallas_call(
        functools.partial(cross_far_kernel, held, total_rows, first if tables else 0),
        out_shape=jax.ShapeDtypeStruct(total.shape, BF16),
        in_specs=[vmem_spec()] * (3 + len(tables) + len(rows)),
        out_specs=vmem_spec(),
        compiler_params=params(*rows),
        cost_estimate=cost(0),
        name="cross_far",
    )(codes, total, wide, *tables, *rows)


def cross_kernel(held, groups, total_rows, ready, codes_ref, *refs):
    tables, refs = (refs[0], refs[1:]) if ready else (None, refs)
    sums, counts_in, pieces = refs[:groups], refs[groups], pieces_of(held, refs[groups + 1 :])
    cross_ref, book_ref = refs[-2:]
    owned = codes_ref.shape[1]
    block = LO * SUB
    books, unused = read_books(sums, counts_in, owned)
    for g, book in enumerate(books):
        book_ref[g * block : (g + 1) * block, :] = book
    total = add_spans(None, widen(books, owned), codes_ref, pieces, spans_of(held), tables)
    cross_ref[...] = (total * (1.0 / total_rows)).astype(BF16)


def cross_call(codes, ready, sums, counts, chunks, total_rows):
    owned = codes.shape[1]
    held, rows = flat(chunks)
    tables = [ready[2]] if ready else []
    return pl.pallas_call(
        functools.partial(cross_kernel, held, len(sums), total_rows, bool(ready)),
        out_shape=(
            jax.ShapeDtypeStruct((owned * SUB, rows[0].shape[1]), BF16),
            jax.ShapeDtypeStruct((len(packs_of(owned)) * LO * SUB, LANES), F32),
        ),
        in_specs=[vmem_spec()] * (2 + len(tables) + len(sums) + len(rows)),
        out_specs=(vmem_spec(), vmem_spec()),
        compiler_params=params(*rows, *tables),
        cost_estimate=cost(0),
        name="cross",
    )(codes, *tables, *sums, counts, *rows)


def turn_kernel(held, *refs):
    pieces, turned_ref = pieces_of(held, refs), refs[-1]
    for i, span in enumerate(spans_of(held)):
        turned_ref[i, :, :] = span_rows(pieces, span).T


def tables_kernel(spans, codes_ref, table_ref, across_ref):
    packs = packs_of(codes_ref.shape[1])
    for i, span in enumerate(spans):
        hi = split(span_codes(codes_ref, span))[0]
        for g, pack in enumerate(packs):
            table = hi_table(hi, pack)
            across_ref[i, g * LANES : (g + 1) * LANES, :] = table
            table_ref[i, :, g * LANES : (g + 1) * LANES] = table.T


def tables_call(codes, peers):
    owned, rows = codes.shape[1:]
    lanes = LANES * len(packs_of(owned))
    spans = spans_of(dict.fromkeys(peers))
    each = len(spans[0]) * rows
    shapes = (
        jax.ShapeDtypeStruct((len(spans), each, lanes), BF16),
        jax.ShapeDtypeStruct((len(spans), lanes, each), BF16),
    )
    if sum(math.prod(a.shape) * 2 for a in shapes) > 14 * MIB:
        return ()
    return pl.pallas_call(
        functools.partial(tables_kernel, spans),
        out_shape=shapes,
        in_specs=[vmem_spec()],
        out_specs=(vmem_spec(),) * 2,
        compiler_params=params(*shapes),
        cost_estimate=cost(0),
        name="tables",
    )(codes)


def turn_call(chunks):
    held, pieces = flat(chunks)
    spans = spans_of(held)
    each = len(spans[0]) * chunks[0][0].shape[0]
    turned = jax.ShapeDtypeStruct((len(spans), pieces[0].shape[1], each), BF16)
    return pl.pallas_call(
        functools.partial(turn_kernel, held),
        out_shape=turned,
        in_specs=[vmem_spec()] * len(pieces),
        out_specs=vmem_spec(),
        compiler_params=params(turned),
        cost_estimate=cost(0),
        name="turn_rows",
    )(*pieces)


def first_step(xb):
    gram = mm(xb, xb, NT)
    norm_square = jnp.sqrt(jnp.sum(gram * gram, keepdims=True) + EPSILON)
    scale = lax.rsqrt(norm_square)
    step = mm(gram.astype(BF16), xb)
    return (1.5 * scale) * xb.astype(F32) - (0.5 * scale / norm_square) * step


def join(parts):
    if parts[0].shape[0] % 16 == 0:
        return jnp.concatenate(parts, axis=0)
    return jnp.concatenate([p.astype(F32) for p in parts], axis=0).astype(BF16)


def next_sums_kernel(held, ready, codes_ref, *refs):
    size = len(held)
    parts, out_ref = refs[:size], refs[-1]
    if ready:
        turned_ref, table_ref = refs[size : size + 2]
    else:
        pieces = pieces_of(held, refs[size:])
    owned = codes_ref.shape[1]
    height = parts[0].shape[0]
    x = first_step(join([ref[...] for ref in parts]))
    xb = x.astype(BF16)
    mine = x[:height]
    gram = mm(mine.astype(BF16), xb, NT)
    rotation_rows = (1.5 * mine - 0.5 * mm(gram.astype(BF16), xb)).astype(BF16)
    totals = None
    for i, span in enumerate(spans_of(held)):
        if ready:
            rotated = mm(rotation_rows, turned_ref[i])
        else:
            rotated = mm(rotation_rows, span_rows(pieces, span), NT)
        rotated = rotated.astype(BF16).astype(F32)
        codes = span_codes(codes_ref, span)
        more = []
        for g, pack in enumerate(packs_of(owned)):
            table = table_ref[i, :, g * LANES : (g + 1) * LANES] if ready else None
            more.append(pack_sums(rotated, codes, pack, False, table))
        totals = more if totals is None else [a + b for a, b in zip(totals, more)]
    write_sums(pack_diagonals(totals, owned, False)[0], None, owned, out_ref)


def next_sums_call(codes, ready, blocks, chunks):
    owned = codes.shape[1]
    held, rows = flat(chunks)
    given = list(ready[:2]) if ready else rows
    return pl.pallas_call(
        functools.partial(next_sums_kernel, held, bool(ready)),
        out_shape=jax.ShapeDtypeStruct((pack_layout(owned, False)[2], LANES), BF16),
        in_specs=[vmem_spec()] * (1 + len(blocks) + len(given)),
        out_specs=vmem_spec(),
        compiler_params=params(*given),
        cost_estimate=cost(0),
        name="next_sums",
    )(codes, *blocks, *given)


def final_kernel(size, place_ref, residual_ref, *refs):
    parts, (out_hbm, whole, out_ref, sems) = refs[:size], refs[size:]
    height = parts[0].shape[0]
    for k, ref in enumerate(parts):
        at = pl.multiple_of((place_ref[0] ^ k) * height, 16 if whole.dtype == BF16 else 8)
        whole[pl.ds(at, height), :] = ref[...].astype(whole.dtype)
    xb = first_step(whole[...].astype(BF16)).astype(BF16)
    once = mm(residual_ref[...], xb, NT)
    less = mm(mm(once.astype(BF16), xb).astype(BF16), xb, NT)
    half = out_ref.shape[0] // 2
    copies = []
    for h in range(2):
        rows = slice(h * half, (h + 1) * half)
        out_ref[rows, :] = (1.5 * once[rows] - 0.5 * less[rows]).astype(BF16)
        copies.append(pltpu.make_async_copy(out_ref.at[pl.ds(h * half, half)], out_hbm.at[pl.ds(h * half, half)], sems.at[h]))
        copies[-1].start()
    for copy in copies:
        copy.wait()


def final_call(place, residual, blocks):
    rows, width = residual.shape
    kind = BF16 if blocks[0].shape[0] % 16 == 0 else F32
    return pl.pallas_call(
        functools.partial(final_kernel, len(blocks)),
        out_shape=jax.ShapeDtypeStruct((rows, width), BF16),
        in_specs=[smem_spec()] + [vmem_spec()] * (1 + len(blocks)),
        out_specs=pl.BlockSpec(memory_space=pl.ANY),
        scratch_shapes=[pltpu.VMEM((width, width), kind), pltpu.VMEM((rows, width), BF16), pltpu.SemaphoreType.DMA((2,))],
        compiler_params=params(),
        cost_estimate=cost(0),
        name="final",
    )(place, residual, *blocks)


def after(x, *first):
    return lax.optimization_barrier((x,) + first)[0]


def near_rows(rows, size):
    return {1 << b: swap(rows, "within", size, 1 << b) for b in range(1, size.bit_length() - 1)}


def far_rows(rows, near, size):
    bits = list(near)
    half = rows.shape[0] // 2
    halves = []
    for order, cut in ((bits, slice(0, half)), (bits[::-1], slice(half, None))):
        here = {0: rows, order[0]: near[order[0]][cut]}
        for bit in order[1:]:
            for k in list(here):
                here[k ^ bit] = swap(here[k], "within", size, bit) if k else near[bit][cut]
        halves.append(here)
    return {k: (halves[0][k], halves[1][k]) for k in halves[0] if k and k not in near}


def both_cores(whole, size):
    return {k ^ 1: tuple(swap(piece, "within", size, 1) for piece in pieces) for k, pieces in whole.items()}


def gather_group(x, size):
    blocks = {k: swap(x, "within", size, k) if k else x for k in range(0, size, 2)}
    for k in list(blocks):
        blocks[k ^ 1] = swap(blocks[k], "within", size, 1)
    return [blocks[k] for k in range(size)]


def scatter_sums(merged, owned, rows, size):
    parts = [merged[0]] + [swap(merged[k // 2], "within", size, k) for k in range(2, size, 2)]
    return merge_chips_call(parts, owned, rows)


def direct(x, size):
    return [x] + [swap(x, "group", size, k) for k in range(1, size)]


def reduce_cross(cross, size, last):
    bits = [1 << b for b in range(size.bit_length() - 1)]
    for bit in bits:
        if bit == bits[-1]:
            cross = after(cross, *last)
        cross = (cross.astype(F32) + swap(cross, "group", size, bit).astype(F32)).astype(BF16)
    return cross


def per_device(vectors, centroids, list_ids, codes, rotation):
    groups = lax.axis_size("group")
    size = lax.axis_size("within")
    rows, width = vectors.shape
    owned = codes.shape[1] // size
    total_rows = rows * size * groups
    place = lax.axis_index("within").astype(jnp.int32).reshape(1)
    residual = residual_call(vectors, centroids, list_ids)
    near = near_rows(residual, size)
    twin = swap(residual, "within", size, 1)
    even, odd = local_sums_call(place, rotation, codes.T, after(residual, twin), size)
    merged = merge_cores_call(even, swap(odd, "within", size, 1), owned)
    sums, own_codes = scatter_sums(merged, owned, rows, size)
    far = far_rows(residual, near, size)
    near = {k: after(rows_near, sums) for k, rows_near in near.items()}
    for bit in [1 << b for b in range(groups.bit_length() - 2)]:
        sums = merge_call(sums, swap(sums, "group", groups, bit), owned)
    chunks = {0: (residual,), 1: (twin,)}
    for k, rows_near in near.items():
        chunks[k] = (rows_near,)
        chunks[k ^ 1] = (swap(rows_near, "within", size, 1),)
    tables = tables_call(after(own_codes, sums), list(chunks) + [peer for k in far for peer in (k, k ^ 1)])
    parts = [sums, after(swap(sums, "group", groups, groups // 2), *tables)]
    total, wide, counts = cross_near_call(own_codes, tables[1:], parts, chunks)
    far = {k: tuple(after(piece, parts[1]) for piece in pieces) for k, pieces in far.items()}
    far = {**far, **both_cores(far, size)}
    cross = cross_far_call(own_codes, tables[1:], len(spans_of(chunks)), total, wide, far, total_rows)
    chunks.update({k: far[k] for even in far if even % 2 == 0 for k in (even, even ^ 1)})
    ready = ()
    if tables:
        ready = (turn_call({**chunks, 0: (after(residual, cross),)}), *tables)
    for alternation in range(1, ALTS):
        block = reduce_cross(cross, groups, ready[:1])
        parts = direct(next_sums_call(own_codes, ready, gather_group(block, size), chunks), groups)
        cross, book = cross_call(own_codes, ready, parts, counts, chunks, total_rows)
    packs = len(packs_of(owned))
    book = book.reshape(packs, LO * SUB, PACK, HI).transpose(0, 2, 3, 1).reshape(packs * PACK, K * SUB)[:owned]
    blocks = gather_group(reduce_cross(cross, groups, (book,)), size)
    rotated_out = final_call(place, residual, blocks)
    return (rotated_out, book)


def solution(mesh):
    in_specs = (
        P(("group", "within"), None),
        P(("group", "within"), None),
        P(("group", "within")),
        P(("group", "within"), None),
        P(),
    )
    out_specs = (P(("group", "within"), None), P("within", None))
    return jax.shard_map(per_device, mesh=mesh, in_specs=in_specs, out_specs=out_specs, check_vma=False)
```
